32 devices in a mesh: dp: 8 (over z, y), fsdp: 4 (over x, core).
Axes of the slice: x: 2, y: 2, z: 4, core: 2. Of those that a mesh axis runs over, the one named last changes fastest.
Arguments:
- frames: bfloat16 [16, 3072, 1024], P('dp', 'fsdp'), may hold values from -6 to 6
- lengths: int32 [16], P('dp'), may hold values from 1536 to 3072, as said below
- t_index: int32 [16], P('dp'), may hold values from 0 to 999
- w_ada: bfloat16 [1024, 6144], P(('dp', 'fsdp')), may hold values from -0.375 to 0.375
- b_ada: bfloat16 [6144], P(('dp', 'fsdp')), may hold values from -3 to 3
- w_query: bfloat16 [1024, 1024], P(('dp', 'fsdp')), may hold values from -0.1875 to 0.1875
- b_query: bfloat16 [1024], P(('dp', 'fsdp')), may hold values from -2 to 2
- w_key: bfloat16 [1024, 1024], P(('dp', 'fsdp')), may hold values from -0.1875 to 0.1875
- b_key: bfloat16 [1024], P(('dp', 'fsdp')), may hold values from -2 to 2
- w_value: bfloat16 [1024, 1024], P(('dp', 'fsdp')), may hold values from -0.1875 to 0.1875
- b_value: bfloat16 [1024], P(('dp', 'fsdp')), may hold values from -2 to 2
- w_out: bfloat16 [1024, 1024], P(('dp', 'fsdp')), may hold values from -0.75 to 0.75
- b_out: bfloat16 [1024], P(('dp', 'fsdp')), may hold values from -2 to 2
- w_up: bfloat16 [1024, 2048], P(('dp', 'fsdp')), may hold values from -0.1875 to 0.1875
- b_up: bfloat16 [2048], P(('dp', 'fsdp')), may hold values from -2 to 2
- w_down: bfloat16 [2048, 1024], P(('dp', 'fsdp')), may hold values from -0.125 to 0.125
- b_down: bfloat16 [1024], P(('dp', 'fsdp')), may hold values from -2 to 2
- grad_out: bfloat16 [16, 3072, 1024], P('dp', 'fsdp'), may hold values from -6 to 6
Outputs:
- mixed: bfloat16 [16, 3072, 1024], P('dp', 'fsdp')
- grad_frames: bfloat16 [16, 3072, 1024], P('dp', 'fsdp')
- grad_w_ada: float32 [1024, 6144], P(('dp', 'fsdp'))
- grad_b_ada: float32 [6144], P(('dp', 'fsdp'))
- grad_w_query: float32 [1024, 1024], P(('dp', 'fsdp'))
- grad_b_query: float32 [1024], P(('dp', 'fsdp'))
- grad_w_key: float32 [1024, 1024], P(('dp', 'fsdp'))
- grad_b_key: float32 [1024], P(('dp', 'fsdp'))
- grad_w_value: float32 [1024, 1024], P(('dp', 'fsdp'))
- grad_b_value: float32 [1024], P(('dp', 'fsdp'))
- grad_w_out: float32 [1024, 1024], P(('dp', 'fsdp'))
- grad_b_out: float32 [1024], P(('dp', 'fsdp'))
- grad_w_up: float32 [1024, 2048], P(('dp', 'fsdp'))
- grad_b_up: float32 [2048], P(('dp', 'fsdp'))
- grad_w_down: float32 [2048, 1024], P(('dp', 'fsdp'))
- grad_b_down: float32 [1024], P(('dp', 'fsdp'))
The draws below stay inside these ranges and needn't reach their ends.
Inputs may be any that keep to these rules, and one draw needn't show every extreme that they name: `lengths`: in each aligned block of 2 slots (those of one index of dp) exactly one slot, drawn from the seed, has 3072 frames and the others have fewer; one slot of all has exactly half of 3072.
All inputs are finite; a program needn't handle non-finite values.
Results may differ from the reference program's by a relative error of at most 0.017.
The reference program's roundings to bfloat16 on the way count: a program that leaves them out, or rounds other values in their place, can miss the bound.
Values may be sent and summed in bfloat16 or wider, within the bound.
No kernel may reach another device: no remote copies, remote signals or barrier semaphores. Data moves between devices by JAX's collectives and lax.ppermute only.
A program may use at most 320 MiB of HBM per device.

```python
import math
import jax
import jax.numpy as jnp
from jax import lax

D = 1024
HEADS = 16
HDIM = 64
FF = 2048
ROWS_DEV = 2
TSTEPS = 1000
PACK = 3072
ROWS = 16


def draw_lengths(key, part):
    key = jax.random.fold_in(key, 11)
    first_key, second_key, third_key, fourth_key = jax.random.split(key, 4)
    blocks = ROWS // ROWS_DEV
    random_lengths = jax.random.randint(first_key, (ROWS,), PACK // 2, PACK)
    chosen = jax.random.randint(second_key, (blocks,), 0, ROWS_DEV)
    slot_ids = jnp.arange(ROWS_DEV)
    longest = (slot_ids[None, :] == chosen[:, None]).reshape(ROWS)
    short_block = jax.random.randint(third_key, (), 0, blocks)
    offset = jax.random.randint(fourth_key, (), 0, ROWS_DEV - 1)
    short_slot = (chosen[short_block] + 1 + offset) % ROWS_DEV
    shortest = jnp.arange(ROWS) == short_block * ROWS_DEV + short_slot
    lengths = jnp.where(shortest, PACK // 2, random_lengths)
    return jnp.where(longest, PACK, lengths).astype(jnp.int32)


def touch_ends(values, stream_key, smallest, top_value):
    longest = values.shape.index(max(values.shape))
    spots = []
    for shift in (0, 1):
        where = [jax.random.randint(jax.random.fold_in(stream_key, axis), (), 0, length) for axis, length in enumerate(values.shape)]
        where[longest] = (where[longest] + shift) % values.shape[longest]
        spots.append(tuple(where))
    return values.at[spots[0]].set(smallest).at[spots[1]].set(top_value)


def shard_levels(rng, dims, cuts, smallest, top_value):
    gain = 1.0
    for axis_at, shards_of in cuts:
        steps = jax.random.uniform(jax.random.fold_in(jax.random.fold_in(rng, 6), axis_at), (shards_of,), jnp.float32, smallest / len(cuts), top_value / len(cuts))
        gain = gain * jnp.repeat(jnp.exp(steps), dims[axis_at] // shards_of).reshape((-1,) + (1,) * (len(dims) - 1 - axis_at))
    return gain


def centred(key, shape, scale, bound, shards=(), kind=jnp.bfloat16):
    array = scale * jax.random.normal(key, shape, jnp.float32)
    if shards:
        array = array * shard_levels(key, shape, shards, -0.22, 0.18)
    return jnp.clip(array, -bound, bound).astype(kind)


def setup_inputs(seed: int = 0) -> dict:
    key_list = jax.random.split(jax.random.key(seed), 19)
    frames = centred(key_list[0], (ROWS, PACK, D), 1.0, 6.0, ((0, 8), (1, 4)))
    lengths = draw_lengths(jax.random.fold_in(key_list[18], 71), 0)
    t_index = touch_ends(jax.random.randint(key_list[2], (ROWS,), 0, TSTEPS), jax.random.fold_in(key_list[2], 1), 0, TSTEPS - 1).astype(jnp.int32)
    w_ada = centred(key_list[3], (D, 6 * D), (D // 4) ** -0.5, 0.375, ((0, 32),))
    b_ada = centred(key_list[4], (6 * D,), 0.5, 3.0, ((0, 32),))
    w_query = centred(key_list[5], (D, D), D ** -0.5, 0.1875, ((0, 32),))
    b_query = centred(key_list[6], (D,), 0.3, 2.0, ((0, 32),))
    w_key = centred(key_list[7], (D, D), D ** -0.5, 0.1875, ((0, 32),))
    b_key = centred(key_list[8], (D,), 0.3, 2.0, ((0, 32),))
    w_value = centred(key_list[9], (D, D), D ** -0.5, 0.1875, ((0, 32),))
    b_value = centred(key_list[10], (D,), 0.3, 2.0, ((0, 32),))
    w_out = centred(key_list[11], (D, D), (D // 16) ** -0.5, 0.75, ((0, 32),))
    b_out = centred(key_list[12], (D,), 0.3, 2.0, ((0, 32),))
    w_up = centred(key_list[13], (D, FF), D ** -0.5, 0.1875, ((0, 32),))
    b_up = centred(key_list[14], (FF,), 0.3, 2.0, ((0, 32),))
    w_down = centred(key_list[15], (FF, D), FF ** -0.5, 0.125, ((0, 32),))
    b_down = centred(key_list[16], (D,), 0.3, 2.0, ((0, 32),))
    grad_out = centred(key_list[17], (ROWS, PACK, D), 1.0, 6.0, ((0, 8), (1, 4)))
    return dict(frames=frames, lengths=lengths, t_index=t_index, w_ada=w_ada, b_ada=b_ada, w_query=w_query, b_query=b_query, w_key=w_key, b_key=b_key, w_value=w_value, b_value=b_value, w_out=w_out, b_out=b_out, w_up=w_up, b_up=b_up, w_down=w_down, b_down=b_down, grad_out=grad_out)


@jax.custom_vjp
def low(v):
    return lax.optimization_barrier(v.astype(jnp.bfloat16)).astype(jnp.float32)

@jax.custom_vjp
def low_back(v):
    return v

def low_keep(v):
    return (low(v), None)

def low_pass(kept, grad):
    return (grad,)

def back_keep(v):
    return (v, None)

def back_low(kept, grad):
    return (low(grad),)
low.defvjp(low_keep, low_pass)
low_back.defvjp(back_keep, back_low)

def time_features(t_index, model_width):
    half_width = model_width // 2
    indices = jnp.arange(half_width).astype(jnp.float32)
    frequency = jnp.exp(indices * (-math.log(10000.0) / (half_width - 1)))
    angles = t_index.astype(jnp.float32)[:, None] * frequency[None, :]
    return jnp.concatenate([jnp.sin(angles), jnp.cos(angles)], axis=1)

def rotary_tables(first_frame, count_frames, head_size):
    half_size = head_size // 2
    inverse = jnp.exp(jnp.arange(half_size).astype(jnp.float32) * (-2.0 * math.log(10000.0) / head_size))
    places = (first_frame + jnp.arange(count_frames, dtype=jnp.int32)).astype(jnp.float32)
    angles = places[:, None] * inverse[None, :]
    cosine = jnp.cos(angles)
    sine_table = jnp.sin(angles)
    return (jnp.concatenate([cosine, cosine], axis=1), jnp.concatenate([sine_table, sine_table], axis=1))

def layer_norm(values):
    centered = values - lax.optimization_barrier(jnp.mean(values, axis=-1, keepdims=True))
    return centered * lax.rsqrt(lax.optimization_barrier(jnp.mean(centered * centered, axis=-1, keepdims=True)) + 1e-06)

def gelu_tanh(values):
    return 0.5 * values * (1.0 + jnp.tanh(0.7978845608028654 * (values + 0.044715 * values * values * values)))

def rotate(values, cosine, sine_table):
    leading = values.shape[:-1]
    pieces = values.reshape(leading + (HEADS, values.shape[-1] // HEADS))
    half_size = pieces.shape[-1] // 2
    turned = jnp.concatenate([-pieces[..., half_size:], pieces[..., :half_size]], axis=-1)
    rotated = pieces * cosine[:, None, :] + turned * sine_table[:, None, :]
    return rotated.reshape(values.shape)

def attend_block(q_block, key_heads, heads_v, key_mask):
    highest = lax.Precision.HIGHEST
    scores = jnp.einsum('qhd,khd->hqk', q_block, key_heads, precision=highest) * HDIM ** (-0.5)
    scores = jnp.where(key_mask[None, None, :], low_back(scores), -1e+30)
    row_max = lax.optimization_barrier(jnp.max(scores, axis=2, keepdims=True))
    weights = jnp.exp(scores - row_max)
    probabilities = low(weights / lax.optimization_barrier(jnp.sum(weights, axis=2, keepdims=True)))
    return jnp.einsum('hqk,khd->qhd', probabilities, heads_v, precision=highest)

def row_forward(params, frame_row, length, time_feats, cosine, sine_table):
    w_ada, b_ada, w_query, b_query, w_key, b_key, w_value, b_value, w_out, b_out, w_up, b_up, w_down, b_down = params
    highest = lax.Precision.HIGHEST
    active = low(jax.nn.silu(time_feats))
    modulation = jnp.dot(active, w_ada, precision=highest) + b_ada
    shift_one, scale_one, gate_one, shift_two, scale_two, gate_two = jnp.split(modulation, 6)
    h_one = low(layer_norm(frame_row) * (1.0 + scale_one) + shift_one)
    queries = low_back(jnp.dot(h_one, w_query, precision=highest) + b_query)
    key_proj = low_back(jnp.dot(h_one, w_key, precision=highest) + b_key)
    values_proj = low(low_back(jnp.dot(h_one, w_value, precision=highest) + b_value))
    q_rot = low(rotate(queries, cosine, sine_table))
    k_rot = low(rotate(key_proj, cosine, sine_table))
    key_heads = k_rot.reshape(PACK, HEADS, HDIM)
    heads_v = values_proj.reshape(PACK, HEADS, HDIM)
    key_mask = jnp.arange(PACK, dtype=jnp.int32) < length
    block_size = math.gcd(PACK, 512)
    blocks = q_rot.reshape(PACK // block_size, block_size, HEADS, HDIM)
    step_fn = jax.checkpoint(attend_block)
    heads_out = lax.map(lambda q_block: step_fn(q_block, key_heads, heads_v, key_mask), blocks)
    heads_out = low(low_back(heads_out.reshape(PACK, D)))
    branch = low_back(jnp.dot(heads_out, w_out, precision=highest) + b_out) * key_mask[:, None].astype(jnp.float32)
    residual = frame_row + gate_one * branch
    h_two = low(layer_norm(residual) * (1.0 + scale_two) + shift_two)
    up_proj = low_back(jnp.dot(h_two, w_up, precision=highest) + b_up)
    hidden = low(gelu_tanh(up_proj))
    ff_out = low_back(jnp.dot(hidden, w_down, precision=highest) + b_down)
    return residual + gate_two * ff_out

def reference(frames, lengths, t_index, w_ada, b_ada, w_query, b_query, w_key, b_key, w_value, b_value, w_out, b_out, w_up, b_up, w_down, b_down, grad_out):
    params = tuple((member.astype(jnp.float32) for member in (w_ada, b_ada, w_query, b_query, w_key, b_key, w_value, b_value, w_out, b_out, w_up, b_up, w_down, b_down)))
    feats_all = time_features(t_index, D)
    cosine, sine_table = rotary_tables(0, PACK, HDIM)

    def one_row(running, inputs):
        frame_row, length, time_feats, cotangent = inputs

        def forward(row_input, *weights):
            return row_forward(weights, row_input, length, time_feats, cosine, sine_table)
        result, pullback = jax.vjp(forward, frame_row.astype(jnp.float32), *params)
        gradient = pullback(cotangent.astype(jnp.float32))
        running = tuple((before + after for before, after in zip(running, gradient[1:])))
        return (running, (result.astype(jnp.bfloat16), gradient[0].astype(jnp.bfloat16)))
    zero_grads = tuple((jnp.zeros(member.shape, jnp.float32) for member in params))
    totals, outputs = lax.scan(one_row, zero_grads, (frames, lengths, feats_all, grad_out))
    return (outputs[0], outputs[1], totals[0], totals[1], totals[2], totals[3], totals[4], totals[5], totals[6], totals[7], totals[8], totals[9], totals[10], totals[11], totals[12], totals[13])
```

```python
import functools
import math

import jax
import jax.numpy as jnp
from jax import lax
from jax.experimental import pallas as pl
from jax.experimental.pallas import tpu as pltpu
from jax.sharding import PartitionSpec as P

HDIM = 64
HALF = HDIM // 2
SCALE = HDIM ** (-0.5)
SCALE2 = SCALE * math.log2(math.e)
AXES = ("dp", "fsdp")
F32 = jnp.float32
BF16 = jnp.bfloat16


def dot(left_side, right_side, left_dim, right_dim):
    return lax.dot_general(
        left_side,
        right_side,
        (((left_dim,), (right_dim,)), ((), ())),
        preferred_element_type=F32,
    )


def pick_block(total, wanted):
    block = min(total, wanted)
    while total % block:
        block -= 128
    return block


def attend_kernel(parts, chunk, *refs):
    q_ref, bias_ref = refs[0], refs[1]
    k_refs, v_refs = refs[2 : 2 + parts], refs[2 + parts : 2 + 2 * parts]
    o_ref, lse_ref, k_aug, v_aug, q_aug = refs[2 + 2 * parts :]
    head, block = pl.program_id(0), pl.program_id(1)
    span = k_aug.shape[0]
    part = span // parts
    q_rows = q_ref.shape[1]

    @pl.when((head == 0) & (block == 0))
    def _():
        k_aug[:, HDIM:] = bias_ref[...]
        v_aug[HDIM:, :] = jnp.ones((16, span), BF16)
        q_aug[HDIM:, :] = jnp.ones((HDIM, q_rows), BF16)

    @pl.when(block == 0)
    def _():
        for i in range(parts):
            k_aug[i * part : (i + 1) * part, :HDIM] = k_refs[i][...].T
            v_aug[:HDIM, i * part : (i + 1) * part] = v_refs[i][...]

    q_aug[:HDIM, :] = q_ref[...]
    queries = q_aug[...]
    count = span // chunk

    def scores(i):
        return dot(k_aug[i * chunk : (i + 1) * chunk, :], queries, 1, 0)

    upcoming = scores(0)
    row_max = total = None
    for i in range(count):
        current = upcoming
        if i + 1 < count:
            upcoming = scores(i + 1)
        chunk_max = jnp.max(current, axis=0, keepdims=True) * SCALE2
        new_max = chunk_max if i == 0 else jnp.maximum(row_max, chunk_max)
        weights = jnp.exp2(current * SCALE2 - new_max).astype(BF16)
        update = dot(v_aug[:, i * chunk : (i + 1) * chunk], weights, 1, 0)
        total = update if i == 0 else total * jnp.exp2(row_max - new_max) + update
        row_max = new_max
    denominator = total[HDIM : HDIM + 1, :]
    o_ref[...] = (total[:HDIM, :] / denominator).astype(BF16)
    lse_ref[...] = (row_max + jnp.log2(denominator))[None]


def attend(q_rot, k_parts, v_parts, bias_columns):
    width, rows = q_rot.shape
    parts = len(k_parts)
    span = parts * rows
    heads = width // HDIM
    q_rows = pick_block(rows, 768)
    chunk = pick_block(span, 512)
    q_spec = pl.BlockSpec((HDIM, q_rows), lambda h, j: (h, j))
    k_spec = pl.BlockSpec((HDIM, rows), lambda h, j: (h, 0))
    return pl.pallas_call(
        functools.partial(attend_kernel, parts, chunk),
        grid=(heads, rows // q_rows),
        in_specs=[q_spec, pl.BlockSpec((span, HDIM), lambda h, j: (0, 0))] + [k_spec] * (2 * parts),
        out_specs=[q_spec, pl.BlockSpec((1, 1, q_rows), lambda h, j: (h, 0, j))],
        out_shape=[
            jax.ShapeDtypeStruct((width, rows), BF16),
            jax.ShapeDtypeStruct((heads, 1, rows), F32),
        ],
        scratch_shapes=[
            pltpu.VMEM((span, 2 * HDIM), BF16),
            pltpu.VMEM((HDIM + 16, span), BF16),
            pltpu.VMEM((2 * HDIM, q_rows), BF16),
        ],
        compiler_params=pltpu.CompilerParams(vmem_limit_bytes=40 << 20),
        cost_estimate=pl.CostEstimate(
            flops=16 * heads * rows * span * HDIM,
            bytes_accessed=2 * width * (2 * rows + 2 * span),
            transcendentals=heads * rows * span,
        ),
        name="attend",
    )(q_rot, bias_columns, *k_parts, *v_parts)


def in_three(values):
    first = values.astype(BF16)
    rest = values - first.astype(F32)
    second = rest.astype(BF16)
    return first.astype(F32), second.astype(F32), rest - second.astype(F32)


def unrotate(values, cosine, sine):
    low, high = values[:HALF], values[HALF:]
    return low * cosine + high * sine, high * cosine - low * sine


def attend_back_kernel(parts, chunk, *refs):
    q_ref, do_ref, o_ref, lse_ref, bias_ref, cos_ref, sin_ref = refs[:7]
    k_refs, v_refs = refs[7 : 7 + parts], refs[7 + parts : 7 + 2 * parts]
    dq_ref = refs[7 + 2 * parts]
    dk_refs = refs[8 + 2 * parts : 8 + 3 * parts]
    dv_refs = refs[8 + 3 * parts : 8 + 4 * parts]
    k_aug, v_aug, k_rows, q_aug, do_aug, dk_acc, dv_acc = refs[8 + 4 * parts :]
    head, block = pl.program_id(0), pl.program_id(1)
    span = k_aug.shape[1]
    part = span // parts
    q_rows = q_ref.shape[1]

    @pl.when((head == 0) & (block == 0))
    def _():
        row = lax.broadcasted_iota(jnp.int32, (HDIM, span), 0)
        ones = jnp.where(row < 4, 1.0, 0.0)
        k_aug[HDIM:, :] = jnp.where(row == 0, bias_ref[...], ones).astype(BF16)
        v_aug[HDIM:, :] = jnp.where(row < 3, 1.0, 0.0).astype(BF16)
        k_rows[:, HDIM:] = jnp.zeros((span, HDIM), BF16)

    @pl.when(block == 0)
    def _():
        for i in range(parts):
            at = slice(i * part, (i + 1) * part)
            keys = k_refs[i][...]
            k_aug[:HDIM, at] = keys
            v_aug[:HDIM, at] = v_refs[i][...]
            k_rows[at, :HDIM] = keys.T
        dk_acc[...] = jnp.zeros_like(dk_acc)
        dv_acc[...] = jnp.zeros_like(dv_acc)

    queries, d_heads = q_ref[...], do_ref[...]
    delta = jnp.sum(d_heads.astype(F32) * o_ref[...].astype(F32), axis=0, keepdims=True)
    row = lax.broadcasted_iota(jnp.int32, (HDIM, q_rows), 0)
    lse_a, lse_b, lse_c = in_three(lse_ref[0] * (-1.0 / SCALE2))
    del_a, del_b, del_c = in_three(-delta)
    q_extra = jnp.where(row == 2, lse_b, jnp.where(row == 3, lse_c, 0.0))
    q_extra = jnp.where(row == 0, 1.0, jnp.where(row == 1, lse_a, q_extra))
    do_extra = jnp.where(row == 1, del_b, jnp.where(row == 2, del_c, 0.0))
    do_extra = jnp.where(row == 0, del_a, do_extra)
    q_aug[:HDIM, :] = queries
    q_aug[HDIM:, :] = q_extra.astype(BF16)
    do_aug[:HDIM, :] = d_heads
    do_aug[HDIM:, :] = do_extra.astype(BF16)
    q_side, do_side = q_aug[...].T, do_aug[...].T
    count = span // chunk

    def products(i):
        at = slice(i * chunk, (i + 1) * chunk)
        return dot(q_side, k_aug[:, at], 1, 0), dot(do_side, v_aug[:, at], 1, 0)

    upcoming = products(0)
    d_query = None
    for i in range(count):
        at = slice(i * chunk, (i + 1) * chunk)
        scores, d_probs = upcoming
        if i + 1 < count:
            upcoming = products(i + 1)
        probs = jnp.exp2(scores * SCALE2)
        d_scores = (probs * d_probs).astype(BF16)
        dv_acc[:, at] += dot(d_heads, probs.astype(BF16), 1, 0)
        dk_acc[:, at] += dot(queries, d_scores, 1, 0)
        update = dot(d_scores, k_rows[at, :], 1, 0)
        d_query = update if i == 0 else d_query + update
    first = pl.multiple_of(block * q_rows, q_rows)
    low, high = unrotate(
        d_query.T[:HDIM, :] * SCALE, cos_ref[:, pl.ds(first, q_rows)], sin_ref[:, pl.ds(first, q_rows)]
    )
    dq_ref[:HALF, :] = low.astype(BF16)
    dq_ref[HALF:, :] = high.astype(BF16)

    @pl.when(block == pl.num_programs(1) - 1)
    def _():
        for i in range(parts):
            at = slice(i * part, (i + 1) * part)
            low, high = unrotate(dk_acc[:, at] * SCALE, cos_ref[:, at], sin_ref[:, at])
            dk_refs[i][:HALF, :] = low.astype(dk_refs[i].dtype)
            dk_refs[i][HALF:, :] = high.astype(dk_refs[i].dtype)
            dv_refs[i][...] = dv_acc[:, at].astype(dv_refs[i].dtype)


def attend_back(q_rot, k_parts, v_parts, d_heads, heads_out, lse, bias_row, cosine, sine, first, count):
    width, rows = q_rot.shape
    parts = len(k_parts)
    span = parts * rows
    q_rows = pick_block(rows, 1536)
    chunk = pick_block(span, 256)
    q_spec = pl.BlockSpec((HDIM, q_rows), lambda h, j: (h + first, j))
    k_spec = pl.BlockSpec((HDIM, rows), lambda h, j: (h + first, 0))
    whole = lambda array: pl.BlockSpec(array.shape, lambda h, j: (0, 0))
    part_out = pl.BlockSpec((HDIM, rows), lambda h, j: (h, 0))
    shape = lambda kind: jax.ShapeDtypeStruct((count * HDIM, rows), kind)
    part_kinds = [F32] + [BF16] * (parts - 1)
    out = pl.pallas_call(
        functools.partial(attend_back_kernel, parts, chunk),
        grid=(count, rows // q_rows),
        in_specs=[
            q_spec,
            q_spec,
            q_spec,
            pl.BlockSpec((1, 1, q_rows), lambda h, j: (h + first, 0, j)),
            whole(bias_row),
            whole(cosine),
            whole(sine),
        ]
        + [k_spec] * (2 * parts),
        out_specs=[pl.BlockSpec((HDIM, q_rows), lambda h, j: (h, j))] + [part_out] * (2 * parts),
        out_shape=[shape(BF16)] + [shape(kind) for kind in part_kinds * 2],
        scratch_shapes=[
            pltpu.VMEM((2 * HDIM, span), BF16),
            pltpu.VMEM((2 * HDIM, span), BF16),
            pltpu.VMEM((span, 2 * HDIM), BF16),
            pltpu.VMEM((2 * HDIM, q_rows), BF16),
            pltpu.VMEM((2 * HDIM, q_rows), BF16),
            pltpu.VMEM((HDIM, span), F32),
            pltpu.VMEM((HDIM, span), F32),
        ],
        compiler_params=pltpu.CompilerParams(vmem_limit_bytes=48 << 20),
        cost_estimate=pl.CostEstimate(
            flops=40 * count * rows * span * HDIM,
            bytes_accessed=2 * count * HDIM * (8 * rows + 4 * span),
            transcendentals=count * rows * span,
        ),
        name="attend_back",
    )(q_rot, d_heads, heads_out, lse, bias_row, cosine, sine, *k_parts, *v_parts)
    return out[0], out[1 : 1 + parts], out[1 + parts :]


def time_features(t_index, model_width):
    half_width = model_width // 2
    indices = jnp.arange(half_width).astype(F32)
    frequency = jnp.exp(indices * (-math.log(10000.0) / (half_width - 1)))
    angles = t_index.astype(F32)[:, None] * frequency[None, :]
    return jnp.concatenate([jnp.sin(angles), jnp.cos(angles)], axis=1)


def rotary_tables(places):
    inverse = jnp.exp(jnp.arange(HALF).astype(F32) * (-2.0 * math.log(10000.0) / HDIM))
    angles = inverse[:, None] * places.astype(F32)[None, :]
    return jnp.cos(angles), jnp.sin(angles)


def norm_parts(values):
    centered = values - jnp.mean(values, axis=-1, keepdims=True)
    scale = lax.rsqrt(jnp.mean(centered * centered, axis=-1, keepdims=True) + 1e-06)
    return centered * scale, scale


def norm_back(normed, scale, d_normed):
    return (
        d_normed
        - jnp.mean(d_normed, axis=-1, keepdims=True)
        - normed * jnp.mean(d_normed * normed, axis=-1, keepdims=True)
    ) * scale


def gelu_tanh(values):
    return 0.5 * values * (1.0 + jnp.tanh(0.7978845608028654 * (values + 0.044715 * values * values * values)))


def rotate(values, cosine, sine):
    width, rows = values.shape
    pieces = values.reshape(width // HDIM, 2, HALF, rows)
    low, high = pieces[:, 0], pieces[:, 1]
    turned = jnp.stack([low * cosine - high * sine, high * cosine + low * sine], axis=1)
    return turned.reshape(width, rows).astype(BF16)


def make_body(mesh):
    n_dp, n_fsdp = mesh.shape["dp"], mesh.shape["fsdp"]

    def shift(values, axis, size, by):
        return lax.ppermute(values, axis, [(i, (i + by) % size) for i in range(size)])

    def body(
        frames,
        lengths,
        t_index,
        w_ada,
        b_ada,
        w_query,
        b_query,
        w_key,
        b_key,
        w_value,
        b_value,
        w_out,
        b_out,
        w_up,
        b_up,
        w_down,
        b_down,
        grad_out,
    ):
        slots, local, width = frames.shape
        group = n_fsdp // slots
        hidden_width = w_up.shape[1]
        shard = w_query.shape[0]
        ada_width = w_ada.shape[1]
        dp, fsdp = lax.axis_index("dp"), lax.axis_index("fsdp")
        me = dp * n_fsdp + fsdp
        slot, place = fsdp // group, fsdp % group
        length = lax.dynamic_index_in_dim(lengths, slot, keepdims=False)

        def swap_in(values):
            pieces = [lax.dynamic_index_in_dim(values, slot, keepdims=False)]
            for by in range(1, slots):
                to_slot = (slot + by) % slots
                away = lax.dynamic_index_in_dim(values, to_slot, keepdims=False)
                pieces.append(shift(away, "fsdp", n_fsdp, by * group))
            return jnp.concatenate(pieces, axis=0)

        def swap_out(values):
            mine = [values[:local]]
            for by in range(1, slots):
                mine.append(shift(values[by * local : (by + 1) * local], "fsdp", n_fsdp, -by * group))
            order = [lax.rem(s - slot + slots, slots) for s in range(slots)]
            stacked = jnp.stack(mine)
            return jnp.concatenate([lax.dynamic_slice_in_dim(stacked, o, 1) for o in order], axis=0)

        def places_of(member):
            at = slot * group + member
            blocks = [((at - by * group) + n_fsdp) % n_fsdp for by in range(slots)]
            return jnp.concatenate([b * local + jnp.arange(local, dtype=jnp.int32) for b in blocks])

        ring = [(i, (i // group) * group + (i % group + 1) % group) for i in range(n_fsdp)]
        back = lambda by: [(i, (i // group) * group + (i % group - by) % group) for i in range(n_fsdp)]

        extras = [b_query[:, None], b_key[:, None], b_value[:, None], b_out[:, None], b_up.reshape(shard, -1), b_down[:, None]]
        extras = jnp.concatenate(extras, axis=1)
        extras = jnp.pad(extras, ((0, 0), (0, 128 - extras.shape[1])))
        packed = lax.all_gather(
            jnp.concatenate([w_query, w_key, w_value, extras], axis=1), AXES, axis=0, tiled=True
        )
        w_qkv, biases = packed[:, : 3 * width], packed[:, 3 * width :].astype(F32)
        out_up = lax.all_gather(jnp.concatenate([w_out, w_up], axis=1), AXES, axis=0, tiled=True)
        full_out, full_up = out_up[:, :width], out_up[:, width:]
        full_down = lax.all_gather(w_down, AXES, axis=0, tiled=True)
        up_cols = b_up.shape[0] // shard
        bias_out = biases[:, 3]
        bias_up = biases[:, 4 : 4 + up_cols].reshape(-1)
        bias_down = biases[:, 4 + up_cols]

        inputs = swap_in(frames)
        rows = inputs.shape[0]
        cotangent = swap_in(grad_out)

        t_parts = [t_index] + [shift(t_index, "dp", n_dp, by) for by in range(1, n_dp)]
        t_all = jnp.concatenate(t_parts)
        active = jax.nn.silu(time_features(t_all, width)).astype(BF16)
        active_mine = lax.dynamic_slice_in_dim(active, me * shard, shard, axis=1)
        partial = dot(active_mine, w_ada, 1, 0)
        b_mine = jnp.broadcast_to(b_ada.astype(F32)[None], (partial.shape[0], b_ada.shape[0]))
        at_b = me * b_ada.shape[0]
        partial = lax.dynamic_update_slice_in_dim(
            partial, lax.dynamic_slice_in_dim(partial, at_b, b_ada.shape[0], axis=1) + b_mine, at_b, axis=1
        )
        partial = partial.reshape(n_dp, slots, ada_width)
        summed = partial[0]
        for by in range(1, n_dp):
            summed = summed + shift(partial[by], "dp", n_dp, -by)
        modulation = lax.dynamic_index_in_dim(summed, slot, keepdims=True)
        for by in range(1, n_fsdp):
            target = ((fsdp + by) % n_fsdp) // group
            modulation = modulation + shift(
                lax.dynamic_index_in_dim(summed, target, keepdims=True), "fsdp", n_fsdp, by
            )
        shift_one, scale_one, gate_one, shift_two, scale_two, gate_two = jnp.split(modulation, 6, axis=1)

        key_places = jnp.concatenate([places_of((place - by + group) % group) for by in range(group)])
        cosine, sine = rotary_tables(key_places)
        key_bias = jnp.where(key_places < length, 0.0, -1e30)
        bias_columns = jnp.pad(key_bias.astype(BF16)[:, None], ((0, 0), (0, HDIM - 1)))
        keep = (key_places[:rows] < length).astype(F32)[:, None]

        inputs_f32 = inputs.astype(F32)
        normed_one, inv_one = norm_parts(inputs_f32)
        h_one = (normed_one * (1.0 + scale_one) + shift_one).astype(BF16)
        project = lambda at: dot(w_qkv[:, at * width : (at + 1) * width], h_one, 0, 1) + biases[:, at : at + 1]
        own_cos, own_sin = cosine[:, :rows], sine[:, :rows]
        k_parts = [rotate(project(1), own_cos, own_sin)]
        v_parts = [project(2).astype(BF16)]
        q_rot = rotate(project(0), own_cos, own_sin)
        for _ in range(1, group):
            k_parts.append(lax.ppermute(k_parts[-1], "fsdp", ring))
            v_parts.append(lax.ppermute(v_parts[-1], "fsdp", ring))
        heads_out, lse = attend(q_rot, k_parts, v_parts, bias_columns)
        branch = (dot(heads_out, full_out, 0, 0) + bias_out) * keep
        residual = inputs_f32 + gate_one * branch
        normed_two, inv_two = norm_parts(residual)
        h_two = (normed_two * (1.0 + scale_two) + shift_two).astype(BF16)
        up_proj = dot(h_two, full_up, 1, 0) + bias_up
        hidden = gelu_tanh(up_proj).astype(BF16)
        ff_out = dot(hidden, full_down, 1, 0) + bias_down
        mixed = swap_out((residual + gate_two * ff_out).astype(BF16))

        d_mixed = cotangent.astype(F32)
        d_gate_two = jnp.sum(d_mixed * ff_out, axis=0)
        d_ff = (d_mixed * gate_two).astype(BF16)
        g_w_down = dot(hidden, d_ff, 0, 0)
        g_b_down = jnp.sum(d_ff.astype(F32), axis=0)
        d_hidden = dot(d_ff, full_down, 1, 1)
        d_up = jax.vjp(gelu_tanh, up_proj)[1](d_hidden)[0].astype(BF16)
        g_w_up = dot(h_two, d_up, 0, 0)
        g_b_up = jnp.sum(d_up.astype(F32), axis=0)
        d_h_two = dot(d_up, full_up, 1, 1)
        d_shift_two = jnp.sum(d_h_two, axis=0)
        d_scale_two = jnp.sum(d_h_two * normed_two, axis=0)
        d_residual = d_mixed + norm_back(normed_two, inv_two, d_h_two * (1.0 + scale_two))
        d_gate_one = jnp.sum(d_residual * branch, axis=0)
        d_branch = (d_residual * gate_one * keep).astype(BF16)
        g_w_out = dot(heads_out, d_branch, 1, 0)
        g_b_out = jnp.sum(d_branch.astype(F32), axis=0)
        d_heads = dot(full_out, d_branch, 1, 1).astype(BF16)

        def reduce_rows(values):
            return lax.psum_scatter(values.astype(BF16), AXES, scatter_dimension=0, tiled=True).astype(F32)

        sum_out_up = reduce_rows(jnp.concatenate([g_w_out, g_w_up], axis=1))
        sum_down = reduce_rows(g_w_down)

        def gather_vectors(values):
            return lax.all_gather(values[None], AXES, axis=0, tiled=True)

        early = jnp.concatenate([d_gate_one, d_shift_two, d_scale_two, d_gate_two, g_b_out, g_b_up, g_b_down])
        early_all = gather_vectors(early)

        heads = width // HDIM
        steps = 2
        each = heads // steps
        d_h_one = None
        sums, d_biases = [], []
        for step in range(steps):
            dq, dk_parts, dv_parts = attend_back(
                q_rot, k_parts, v_parts, d_heads, heads_out, lse, key_bias[None], cosine, sine, step * each, each
            )
            d_key, d_value = dk_parts[0], dv_parts[0]
            for by in range(1, group):
                d_key = d_key + lax.ppermute(dk_parts[by], "fsdp", back(by)).astype(F32)
                d_value = d_value + lax.ppermute(dv_parts[by], "fsdp", back(by)).astype(F32)
            grads = [dq, d_key.astype(BF16), d_value.astype(BF16)]
            cols = slice(step * each * HDIM, (step + 1) * each * HDIM)
            weight_grads = []
            for at, grad in enumerate(grads):
                update = dot(grad, w_qkv[:, at * width : (at + 1) * width][:, cols], 0, 1)
                d_h_one = update if d_h_one is None else d_h_one + update
                weight_grads.append(dot(h_one, grad, 0, 1))
            sums.append(reduce_rows(jnp.concatenate(weight_grads, axis=1)))
            d_biases.append([jnp.sum(grad.astype(F32), axis=1) for grad in grads])
        d_shift_one = jnp.sum(d_h_one, axis=0)
        d_scale_one = jnp.sum(d_h_one * normed_one, axis=0)
        d_inputs = norm_back(normed_one, inv_one, d_h_one * (1.0 + scale_one))
        grad_frames = swap_out((d_residual + d_inputs).astype(BF16))
        g_b_qkv = [jnp.concatenate([part[at] for part in d_biases]) for at in range(3)]
        late_all = gather_vectors(jnp.concatenate([d_shift_one, d_scale_one] + g_b_qkv))

        t_order = lax.rem(dp - jnp.arange(n_dp) + n_dp, n_dp)
        active_of = active_mine.reshape(n_dp, slots, shard)[t_order]
        active_of = jnp.repeat(active_of[:, :, None], group, axis=2).reshape(n_dp * n_fsdp, shard)

        def ada_grad(vectors):
            return lax.dot_general(
                active_of.astype(F32),
                vectors,
                (((0,), (0,)), ((), ())),
                precision=lax.Precision.HIGHEST,
                preferred_element_type=F32,
            )

        g_w_ada = jnp.concatenate([ada_grad(late_all[:, : 2 * width]), ada_grad(early_all[:, : 4 * width])], axis=1)
        all_mod = jnp.concatenate(
            [jnp.sum(late_all[:, : 2 * width], axis=0), jnp.sum(early_all[:, : 4 * width], axis=0)]
        )
        mine = lambda vector: lax.dynamic_slice_in_dim(vector, me * (vector.shape[0] // (n_dp * n_fsdp)), vector.shape[0] // (n_dp * n_fsdp))
        early_sum = jnp.sum(early_all[:, 4 * width :], axis=0)
        late_sum = jnp.sum(late_all[:, 2 * width :], axis=0)
        columns = [s.reshape(shard, 3, each * HDIM) for s in sums]
        g_qkv = [jnp.concatenate([c[:, at] for c in columns], axis=1) for at in range(3)]
        return (
            mixed,
            grad_frames,
            g_w_ada,
            mine(all_mod),
            g_qkv[0],
            mine(late_sum[:width]),
            g_qkv[1],
            mine(late_sum[width : 2 * width]),
            g_qkv[2],
            mine(late_sum[2 * width :]),
            sum_out_up[:, :width],
            mine(early_sum[:width]),
            sum_out_up[:, width:],
            mine(early_sum[width : width + hidden_width]),
            sum_down,
            mine(early_sum[width + hidden_width :]),
        )

    return body


def solution(mesh):
    rows, vector, matrix = P("dp", "fsdp", None), P(AXES), P(AXES, None)
    return jax.shard_map(
        make_body(mesh),
        mesh=mesh,
        in_specs=(rows, P("dp"), P("dp")) + (matrix, vector) * 7 + (rows,),
        out_specs=(rows, rows) + (matrix, vector) * 7,
        check_vma=False,
    )
```

```python
import functools
import math

import jax
import jax.numpy as jnp
from jax import lax
from jax.experimental import pallas as pl
from jax.experimental.pallas import tpu as pltpu
from jax.sharding import PartitionSpec as P

HDIM = 64
HALF = HDIM // 2
SCALE = HDIM ** (-0.5)
SCALE2 = SCALE * math.log2(math.e)
AXES = ("dp", "fsdp")
VMEM_LIMIT = 62 << 20
F32 = jnp.float32
BF16 = jnp.bfloat16


def dot(left_side, right_side, left_dim, right_dim):
    return lax.dot_general(
        left_side,
        right_side,
        (((left_dim,), (right_dim,)), ((), ())),
        preferred_element_type=F32,
    )


def pick_block(total, wanted):
    block = min(total, wanted)
    while total % block:
        block -= 128
    return block


def attend_kernel(parts, chunk, *refs):
    q_ref, bias_ref = refs[0], refs[1]
    k_refs, v_refs = refs[2 : 2 + parts], refs[2 + parts : 2 + 2 * parts]
    o_ref, lse_ref, k_aug, v_aug, q_aug = refs[2 + 2 * parts :]
    head, block = pl.program_id(0), pl.program_id(1)
    span = k_aug.shape[0]
    part = span // parts
    q_rows = q_ref.shape[1]

    @pl.when((head == 0) & (block == 0))
    def _():
        k_aug[:, HDIM:] = bias_ref[...]
        v_aug[HDIM:, :] = jnp.ones((16, span), BF16)
        q_aug[HDIM:, :] = jnp.ones((HDIM, q_rows), BF16)

    @pl.when(block == 0)
    def _():
        for i in range(parts):
            k_aug[i * part : (i + 1) * part, :HDIM] = k_refs[i][...].T
            v_aug[:HDIM, i * part : (i + 1) * part] = v_refs[i][...]

    q_aug[:HDIM, :] = q_ref[...]
    queries = q_aug[...]
    count = span // chunk

    def scores(i):
        return dot(k_aug[i * chunk : (i + 1) * chunk, :], queries, 1, 0)

    upcoming = scores(0)
    row_max = total = None
    for i in range(count):
        current = upcoming
        if i + 1 < count:
            upcoming = scores(i + 1)
        chunk_max = jnp.max(current, axis=0, keepdims=True) * SCALE2
        new_max = chunk_max if i == 0 else jnp.maximum(row_max, chunk_max)
        weights = jnp.exp2(current * SCALE2 - new_max).astype(BF16)
        update = dot(v_aug[:, i * chunk : (i + 1) * chunk], weights, 1, 0)
        total = update if i == 0 else total * jnp.exp2(row_max - new_max) + update
        row_max = new_max
    denominator = total[HDIM : HDIM + 1, :]
    o_ref[...] = (total[:HDIM, :] / denominator).astype(BF16)
    lse_ref[...] = (row_max + jnp.log2(denominator))[None]


def attend(q_rot, k_parts, v_parts, bias_columns, first):
    width, rows = k_parts[0].shape
    parts = len(k_parts)
    span = parts * rows
    heads = width // HDIM
    q_rows = pick_block(rows, 768)
    chunk = pick_block(span, 512)
    q_spec = pl.BlockSpec((HDIM, q_rows), lambda h, j: (h + first, j))
    k_spec = pl.BlockSpec((HDIM, rows), lambda h, j: (h, 0))
    return pl.pallas_call(
        functools.partial(attend_kernel, parts, chunk),
        grid=(heads, rows // q_rows),
        in_specs=[q_spec, pl.BlockSpec((span, HDIM), lambda h, j: (0, 0))] + [k_spec] * (2 * parts),
        out_specs=[
            pl.BlockSpec((HDIM, q_rows), lambda h, j: (h, j)),
            pl.BlockSpec((1, 1, q_rows), lambda h, j: (h, 0, j)),
        ],
        out_shape=[
            jax.ShapeDtypeStruct((width, rows), BF16),
            jax.ShapeDtypeStruct((heads, 1, rows), F32),
        ],
        scratch_shapes=[
            pltpu.VMEM((span, 2 * HDIM), BF16),
            pltpu.VMEM((HDIM + 16, span), BF16),
            pltpu.VMEM((2 * HDIM, q_rows), BF16),
        ],
        compiler_params=pltpu.CompilerParams(vmem_limit_bytes=VMEM_LIMIT),
        cost_estimate=pl.CostEstimate(
            flops=16 * heads * rows * span * HDIM,
            bytes_accessed=2 * width * (2 * rows + 2 * span),
            transcendentals=heads * rows * span,
        ),
        name="attend",
    )(q_rot, bias_columns, *k_parts, *v_parts)


def in_three(values):
    first = values.astype(BF16)
    rest = values - first.astype(F32)
    second = rest.astype(BF16)
    return first.astype(F32), second.astype(F32), rest - second.astype(F32)


def unrotate(values, cosine, sine):
    low, high = values[:HALF], values[HALF:]
    return low * cosine + high * sine, high * cosine - low * sine


def attend_back_kernel(parts, chunk, *refs):
    q_ref, do_ref, o_ref, lse_ref, bias_ref, cos_ref, sin_ref = refs[:7]
    k_refs, v_refs = refs[7 : 7 + parts], refs[7 + parts : 7 + 2 * parts]
    dq_ref = refs[7 + 2 * parts]
    dk_refs = refs[8 + 2 * parts : 8 + 3 * parts]
    dv_refs = refs[8 + 3 * parts : 8 + 4 * parts]
    k_aug, v_aug, k_rows, q_aug, do_aug, dk_acc, dv_acc = refs[8 + 4 * parts :]
    head, block = pl.program_id(0), pl.program_id(1)
    span = k_aug.shape[1]
    part = span // parts
    q_rows = q_ref.shape[1]

    @pl.when((head == 0) & (block == 0))
    def _():
        row = lax.broadcasted_iota(jnp.int32, (HDIM, span), 0)
        ones = jnp.where(row < 4, 1.0, 0.0)
        k_aug[HDIM:, :] = jnp.where(row == 0, bias_ref[...], ones).astype(BF16)
        v_aug[HDIM:, :] = jnp.where(row < 3, 1.0, 0.0).astype(BF16)
        k_rows[:, HDIM:] = jnp.zeros((span, HDIM), BF16)

    @pl.when(block == 0)
    def _():
        for i in range(parts):
            at = slice(i * part, (i + 1) * part)
            keys = k_refs[i][...]
            k_aug[:HDIM, at] = keys
            v_aug[:HDIM, at] = v_refs[i][...]
            k_rows[at, :HDIM] = keys.T
        dk_acc[...] = jnp.zeros_like(dk_acc)
        dv_acc[...] = jnp.zeros_like(dv_acc)

    queries, d_heads = q_ref[...], do_ref[...]
    delta = jnp.sum(d_heads.astype(F32) * o_ref[...].astype(F32), axis=0, keepdims=True)
    row = lax.broadcasted_iota(jnp.int32, (HDIM, q_rows), 0)
    lse_a, lse_b, lse_c = in_three(lse_ref[0] * (-1.0 / SCALE2))
    del_a, del_b, del_c = in_three(-delta)
    q_extra = jnp.where(row == 2, lse_b, jnp.where(row == 3, lse_c, 0.0))
    q_extra = jnp.where(row == 0, 1.0, jnp.where(row == 1, lse_a, q_extra))
    do_extra = jnp.where(row == 1, del_b, jnp.where(row == 2, del_c, 0.0))
    do_extra = jnp.where(row == 0, del_a, do_extra)
    q_aug[:HDIM, :] = queries
    q_aug[HDIM:, :] = q_extra.astype(BF16)
    do_aug[:HDIM, :] = d_heads
    do_aug[HDIM:, :] = do_extra.astype(BF16)
    q_side, do_side = q_aug[...].T, do_aug[...].T
    count = span // chunk

    def products(i):
        at = slice(i * chunk, (i + 1) * chunk)
        return dot(q_side, k_aug[:, at], 1, 0), dot(do_side, v_aug[:, at], 1, 0)

    upcoming = products(0)
    d_query = None
    for i in range(count):
        at = slice(i * chunk, (i + 1) * chunk)
        scores, d_probs = upcoming
        if i + 1 < count:
            upcoming = products(i + 1)
        probs = jnp.exp2(scores * SCALE2)
        d_scores = (probs * d_probs).astype(BF16)
        dv_acc[:, at] += dot(d_heads, probs.astype(BF16), 1, 0)
        dk_acc[:, at] += dot(queries, d_scores, 1, 0)
        update = dot(d_scores, k_rows[at, :], 1, 0)
        d_query = update if i == 0 else d_query + update
    first = pl.multiple_of(block * q_rows, q_rows)
    low, high = unrotate(
        d_query.T[:HDIM, :] * SCALE, cos_ref[:, pl.ds(first, q_rows)], sin_ref[:, pl.ds(first, q_rows)]
    )
    dq_ref[:HALF, :] = low.astype(BF16)
    dq_ref[HALF:, :] = high.astype(BF16)

    @pl.when(block == pl.num_programs(1) - 1)
    def _():
        for i in range(parts):
            at = slice(i * part, (i + 1) * part)
            low, high = unrotate(dk_acc[:, at] * SCALE, cos_ref[:, at], sin_ref[:, at])
            dk_refs[i][:HALF, :] = low.astype(dk_refs[i].dtype)
            dk_refs[i][HALF:, :] = high.astype(dk_refs[i].dtype)
            dv_refs[i][...] = dv_acc[:, at].astype(dv_refs[i].dtype)


def attend_back(q_rot, k_parts, v_parts, d_heads, heads_out, lse, bias_row, cosine, sine, first, within, count):
    rows = q_rot.shape[1]
    parts = len(k_parts)
    span = parts * rows
    q_rows = pick_block(rows, 1536)
    chunk = pick_block(span, 256)
    q_spec = pl.BlockSpec((HDIM, q_rows), lambda h, j: (h + first, j))
    k_spec = pl.BlockSpec((HDIM, rows), lambda h, j: (h + within, 0))
    whole = lambda array: pl.BlockSpec(array.shape, lambda h, j: (0, 0))
    part_out = pl.BlockSpec((HDIM, rows), lambda h, j: (h, 0))
    shape = lambda kind: jax.ShapeDtypeStruct((count * HDIM, rows), kind)
    part_kinds = [F32] + [BF16] * (parts - 1)
    out = pl.pallas_call(
        functools.partial(attend_back_kernel, parts, chunk),
        grid=(count, rows // q_rows),
        in_specs=[
            q_spec,
            q_spec,
            pl.BlockSpec((HDIM, q_rows), lambda h, j: (h + within, j)),
            pl.BlockSpec((1, 1, q_rows), lambda h, j: (h + within, 0, j)),
            whole(bias_row),
            whole(cosine),
            whole(sine),
        ]
        + [k_spec] * (2 * parts),
        out_specs=[pl.BlockSpec((HDIM, q_rows), lambda h, j: (h, j))] + [part_out] * (2 * parts),
        out_shape=[shape(BF16)] + [shape(kind) for kind in part_kinds * 2],
        scratch_shapes=[
            pltpu.VMEM((2 * HDIM, span), BF16),
            pltpu.VMEM((2 * HDIM, span), BF16),
            pltpu.VMEM((span, 2 * HDIM), BF16),
            pltpu.VMEM((2 * HDIM, q_rows), BF16),
            pltpu.VMEM((2 * HDIM, q_rows), BF16),
            pltpu.VMEM((HDIM, span), F32),
            pltpu.VMEM((HDIM, span), F32),
        ],
        compiler_params=pltpu.CompilerParams(vmem_limit_bytes=VMEM_LIMIT),
        cost_estimate=pl.CostEstimate(
            flops=10 * count * rows * span * HDIM,
            bytes_accessed=2 * count * HDIM * (8 * rows + 4 * span),
            transcendentals=0,
        ),
        name="attend_back",
    )(q_rot, d_heads, heads_out, lse, bias_row, cosine, sine, *k_parts, *v_parts)
    return out[0], out[1 : 1 + parts], out[1 + parts :]


def norm_parts(values):
    centered = values - jnp.mean(values, axis=-1, keepdims=True)
    scale = lax.rsqrt(jnp.mean(centered * centered, axis=-1, keepdims=True) + 1e-06)
    return centered * scale, scale


def norm_back(normed, scale, d_normed):
    return (
        d_normed
        - jnp.mean(d_normed, axis=-1, keepdims=True)
        - normed * jnp.mean(d_normed * normed, axis=-1, keepdims=True)
    ) * scale


def gelu_both(values):
    square = values * values
    bend = jnp.tanh(0.7978845608028654 * (values + 0.044715 * values * square))
    half = 0.5 * (1.0 + bend)
    slope = 0.7978845608028654 * (1.0 + 3 * 0.044715 * square)
    return values * half, half + 0.5 * values * (1.0 - bend * bend) * slope


def add_rows(values):
    return jnp.sum(values, axis=0, keepdims=True)


def store_rotated(out_ref, values, cosine, sine):
    for at in range(0, out_ref.shape[0], HDIM):
        low, high = values[at : at + HALF], values[at + HALF : at + HDIM]
        out_ref[at : at + HALF, :] = (low * cosine - high * sine).astype(BF16)
        out_ref[at + HALF : at + HDIM, :] = (high * cosine + low * sine).astype(BF16)


def either(first_ref, second_ref):
    half = pl.num_programs(0) // 2
    return jnp.where(pl.program_id(0) < half, first_ref[...], second_ref[...])


def halves_spec(inputs, rows, block, width):
    if inputs[0].shape[0] == rows:
        return [pl.BlockSpec((block, width), lambda i: (i, 0))] * 2
    half = rows // 2 // block
    return [
        pl.BlockSpec((block, width), lambda i: (jnp.minimum(i, half - 1), 0)),
        pl.BlockSpec((block, width), lambda i: (jnp.maximum(i - half, 0), 0)),
    ]


def project_kv_kernel(groups, x_ref, y_ref, vectors_ref, w_ref, cos_ref, sin_ref, h_ref, *refs):
    k_refs, v_refs = refs[:groups], refs[groups:]
    width = x_ref.shape[1]
    tall = width // groups
    normed, _ = norm_parts(either(x_ref, y_ref).astype(F32))
    h_one = (normed * (1.0 + vectors_ref[1:2, :]) + vectors_ref[0:1, :]).astype(BF16)
    h_ref[...] = h_one
    keys = (dot(h_one, w_ref[:, :width], 1, 0) + vectors_ref[7:8, :]).T
    values = (dot(h_one, w_ref[:, width:], 1, 0) + vectors_ref[8:9, :]).astype(BF16).T
    for i in range(groups):
        store_rotated(k_refs[i], keys[i * tall : (i + 1) * tall], cos_ref[...], sin_ref[...])
        v_refs[i][...] = values[i * tall : (i + 1) * tall]


def project_q_kernel(h_ref, vectors_ref, w_ref, cos_ref, sin_ref, q_ref):
    queries = dot(h_ref[...], w_ref[...], 1, 0) + vectors_ref[6:7, :]
    store_rotated(q_ref, queries.T, cos_ref[...], sin_ref[...])


def whole_spec(shape, column=0):
    return pl.BlockSpec(shape, lambda i: (0, column), pipeline_mode=pl.Buffered(1))


def project(inputs, vectors, packed, cosine, sine, groups):
    width, rows = inputs[0].shape[1], cosine.shape[1]
    block = pick_block(inputs[0].shape[0], 256)
    tall = width // groups
    row_spec = pl.BlockSpec((block, width), lambda i: (i, 0))
    turned_spec = lambda height: pl.BlockSpec((height, block), lambda i: (0, i))
    turned = lambda height: jax.ShapeDtypeStruct((height, rows), BF16)
    table_spec = turned_spec(HALF)
    params = pltpu.CompilerParams(vmem_limit_bytes=VMEM_LIMIT)
    out = pl.pallas_call(
        functools.partial(project_kv_kernel, groups),
        grid=(rows // block,),
        in_specs=halves_spec(inputs, rows, block, width)
        + [whole_spec(vectors.shape), whole_spec((width, 2 * width)), table_spec, table_spec],
        out_specs=[row_spec] + [turned_spec(tall)] * (2 * groups),
        out_shape=[jax.ShapeDtypeStruct((rows, width), BF16)] + [turned(tall)] * (2 * groups),
        compiler_params=params,
        cost_estimate=pl.CostEstimate(
            flops=8 * rows * width * width, bytes_accessed=8 * rows * width + 4 * width * width, transcendentals=0
        ),
        name="project_kv",
    )(*inputs, vectors, packed, cosine, sine)
    h_one, keys, values = out[0], out[1 : 1 + groups], out[1 + groups :]
    queries = pl.pallas_call(
        project_q_kernel,
        grid=(rows // block,),
        in_specs=[row_spec, whole_spec(vectors.shape), whole_spec((width, width), 2), table_spec, table_spec],
        out_specs=turned_spec(width),
        out_shape=turned(width),
        compiler_params=params,
        cost_estimate=pl.CostEstimate(
            flops=4 * rows * width * width, bytes_accessed=4 * rows * width + 2 * width * width, transcendentals=0
        ),
        name="project_q",
    )(h_one, vectors, packed, cosine, sine)
    return h_one, queries, keys, values


def feed_forward_kernel(parts, pieces, shard, *refs):
    o_refs = refs[:parts]
    x_ref, y_ref, cot_ref, cot_y_ref, keep_ref, w_ou_ref, w_down_ref, vectors_ref = refs[parts : parts + 8]
    mixed_ref, d_res_ref, d_heads_ref, g_rows_ref, sums_ref, g_b_up_ref = refs[parts + 8 : parts + 14]
    acc_ou, acc_down, acc_rows, acc_b_up, slope_ref, hidden_ref, staged, sems = refs[parts + 14 :]
    step = pl.program_id(0)
    width, hidden_width = x_ref.shape[1], w_down_ref.shape[0]
    piece = hidden_width // pieces

    @pl.when(step == 0)
    def _():
        for acc in (acc_ou, acc_down, acc_rows, acc_b_up):
            acc[...] = jnp.zeros_like(acc)

    gate_one, shift_two, scale_two, gate_two, b_out, b_down = [vectors_ref[i : i + 1, :] for i in (2, 3, 4, 5, 9, 10)]
    keep = keep_ref[...]
    heads_out = jnp.concatenate([ref[...] for ref in o_refs], axis=0)
    branch = (dot(heads_out, w_ou_ref[:, :width], 0, 0) + b_out) * keep
    residual = either(x_ref, y_ref).astype(F32) + gate_one * branch
    normed, inverse = norm_parts(residual)
    h_two = (normed * (1.0 + scale_two) + shift_two).astype(BF16)
    ff_out = b_down
    for i in range(pieces):
        at = slice(i * piece, (i + 1) * piece)
        value, slope = gelu_both(dot(h_two, w_ou_ref[:, width + i * piece : width + (i + 1) * piece], 1, 0) + vectors_ref[11 + i : 12 + i, :])
        slope_ref[:, at] = slope
        hidden = value.astype(BF16)
        hidden_ref[:, at] = hidden
        ff_out = ff_out + dot(hidden, w_down_ref[at, :], 1, 0)
    mixed_ref[...] = (residual + gate_two * ff_out).astype(BF16)
    d_mixed = either(cot_ref, cot_y_ref).astype(F32)
    acc_rows[3:4, :] += add_rows(d_mixed * ff_out)
    d_ff = (d_mixed * gate_two).astype(BF16)
    acc_rows[5:6, :] += add_rows(d_ff.astype(F32))
    d_h_two = None
    for i in range(pieces):
        at = slice(i * piece, (i + 1) * piece)
        up_at = slice(width + i * piece, width + (i + 1) * piece)
        acc_down[at, :] += dot(hidden_ref[:, at], d_ff, 0, 0)
        d_up = (dot(d_ff, w_down_ref[at, :], 1, 1) * slope_ref[:, at]).astype(BF16)
        acc_b_up[:, at] += add_rows(d_up.astype(F32))
        acc_ou[:, up_at] += dot(h_two, d_up, 0, 0)
        update = dot(d_up, w_ou_ref[:, up_at], 1, 1)
        d_h_two = update if i == 0 else d_h_two + update
    acc_rows[1:2, :] += add_rows(d_h_two)
    acc_rows[2:3, :] += add_rows(d_h_two * normed)
    d_residual = d_mixed + norm_back(normed, inverse, d_h_two * (1.0 + scale_two))
    d_res_ref[...] = d_residual
    acc_rows[0:1, :] += add_rows(d_residual * branch)
    d_branch = (d_residual * gate_one * keep).astype(BF16)
    acc_rows[4:5, :] += add_rows(d_branch.astype(F32))
    acc_ou[:, :width] += dot(heads_out, d_branch, 1, 0)
    d_heads_ref[...] = dot(w_ou_ref[:, :width], d_branch, 1, 1).astype(BF16)

    @pl.when(step == pl.num_programs(0) - 1)
    def _():
        sums_ref[...] = acc_rows[...]
        g_b_up_ref[...] = acc_b_up[...]
        tall = staged.shape[1]
        wide = acc_ou.shape[1]
        ups = hidden_width // width
        copies = []
        for i in range(width // tall):
            slot = i % 2
            if i >= 2:
                copies[i - 2].wait()
            staged[slot, :, :wide] = acc_ou[i * tall : (i + 1) * tall, :].astype(BF16)
            for up in range(ups):
                at = slice(wide + up * width, wide + (up + 1) * width)
                if shard % 16 == 0:
                    for j in range(0, tall, shard):
                        first = (i * tall + j) * ups + up * shard
                        staged[slot, j : j + shard, at] = acc_down[first : first + shard, :].astype(BF16)
                else:
                    first = up * width + i * tall
                    staged[slot, :, at] = acc_down[first : first + tall, :].astype(BF16)
            copies.append(pltpu.make_async_copy(staged.at[slot], g_rows_ref.at[pl.ds(i * tall, tall), :], sems.at[slot]))
            copies[i].start()
        for copy in copies[-2:]:
            copy.wait()


def feed_forward(inputs, heads_out, cotangent, keep, out_up, full_down, vectors, shard):
    rows, width = heads_out[0].shape[1], inputs[0].shape[1]
    hidden_width = full_down.shape[0]
    block = pick_block(inputs[0].shape[0], 256)
    row_spec = pl.BlockSpec((block, width), lambda i: (i, 0))
    turned_spec = lambda array: pl.BlockSpec((array, block), lambda i: (0, i))
    kinds = jax.ShapeDtypeStruct
    ou_shape, down_shape = out_up.shape, full_down.shape
    wide = ou_shape[1] + hidden_width
    return pl.pallas_call(
        functools.partial(feed_forward_kernel, len(heads_out), hidden_width // width, shard),
        grid=(rows // block,),
        in_specs=[turned_spec(part.shape[0]) for part in heads_out]
        + halves_spec(inputs, rows, block, width) * 2
        + [
            pl.BlockSpec((block, 1), lambda i: (i, 0)),
            whole_spec(ou_shape),
            whole_spec(down_shape),
            whole_spec(vectors.shape),
        ],
        out_specs=[
            row_spec,
            row_spec,
            turned_spec(width),
            pl.BlockSpec(memory_space=pl.ANY),
            whole_spec((8, width)),
            whole_spec((1, hidden_width)),
        ],
        out_shape=[
            kinds((rows, width), BF16),
            kinds((rows, width), F32),
            kinds((width, rows), BF16),
            kinds((width, wide), BF16),
            kinds((8, width), F32),
            kinds((1, hidden_width), F32),
        ],
        scratch_shapes=[
            pltpu.VMEM(ou_shape, F32),
            pltpu.VMEM(down_shape, F32),
            pltpu.VMEM((8, width), F32),
            pltpu.VMEM((1, hidden_width), F32),
            pltpu.VMEM((block, hidden_width), F32),
            pltpu.VMEM((block, hidden_width), BF16),
            pltpu.VMEM((2, pick_block(width, 256), wide), BF16),
            pltpu.SemaphoreType.DMA((2,)),
        ],
        compiler_params=pltpu.CompilerParams(vmem_limit_bytes=VMEM_LIMIT),
        cost_estimate=pl.CostEstimate(
            flops=2 * 6 * rows * width * (width + 2 * hidden_width),
            bytes_accessed=8 * rows * width + 4 * width * (width + 2 * hidden_width),
            transcendentals=rows * hidden_width,
        ),
        name="feed_forward",
    )(*heads_out, *inputs, *cotangent, keep, out_up, full_down, vectors)


def weight_grads_kernel(pieces, parts, h_ref, *refs):
    count = pieces * (1 + 2 * parts)
    per_piece = [refs[i * (1 + 2 * parts) : (i + 1) * (1 + 2 * parts)] for i in range(pieces)]
    dq_out, dk_out, dv_out, weight_ref, bias_ref = refs[count:]

    def summed(which):
        columns = []
        for piece in per_piece:
            total = piece[which][...]
            for i in range(1, parts):
                total = total + piece[which + i][...].astype(F32)
            columns.append(total.astype(BF16))
        return jnp.concatenate(columns, axis=0)

    grads = [
        jnp.concatenate([piece[0][...] for piece in per_piece], axis=0),
        summed(1),
        summed(1 + parts),
    ]
    for ref, grad in zip((dq_out, dk_out, dv_out), grads):
        ref[...] = grad
    weight_ref[...] = dot(jnp.concatenate(grads, axis=0), h_ref[...], 1, 0).T.astype(BF16)
    for i, grad in enumerate(grads):
        bias_ref[:, i : i + 1] = jnp.sum(grad.astype(F32), axis=1, keepdims=True)


def weight_grads(h_one, pieces):
    rows, width = h_one.shape
    heights = [piece[0].shape[0] for piece in pieces]
    tall = sum(heights)
    parts = len(pieces[0][1])
    kinds = jax.ShapeDtypeStruct
    whole = lambda shape: pl.BlockSpec(shape, lambda: (0, 0))
    flat = [array for piece in pieces for array in (piece[0], *piece[1], *piece[2])]
    return pl.pallas_call(
        functools.partial(weight_grads_kernel, len(pieces), parts),
        in_specs=[whole(array.shape) for array in (h_one, *flat)],
        out_specs=[whole((tall, rows))] * 3 + [whole((width, 3 * tall)), whole((tall, 128))],
        out_shape=[kinds((tall, rows), BF16)] * 3 + [kinds((width, 3 * tall), BF16), kinds((tall, 128), F32)],
        compiler_params=pltpu.CompilerParams(vmem_limit_bytes=VMEM_LIMIT),
        cost_estimate=pl.CostEstimate(
            flops=6 * rows * width * tall, bytes_accessed=16 * rows * tall + 2 * rows * width, transcendentals=0
        ),
        name="weight_grads",
    )(h_one, *flat)


def input_grads_kernel(groups, x_ref, d_res_ref, vectors_ref, w_ref, *refs):
    grad_refs, (out_ref, sums_ref) = refs[: 3 * groups], refs[3 * groups :]
    width = x_ref.shape[1]

    @pl.when(pl.program_id(0) == 0)
    def _():
        sums_ref[...] = jnp.zeros_like(sums_ref)

    turned = None
    for kind in range(3):
        first = (2, 0, 1)[kind] * width
        grad = jnp.concatenate([grad_refs[3 * g + kind][...] for g in range(groups)], axis=0)
        update = dot(w_ref[:, first : first + width], grad, 1, 0)
        turned = update if turned is None else turned + update
    d_h_one = turned.T
    normed, inverse = norm_parts(x_ref[...].astype(F32))
    sums_ref[0:1, :] += add_rows(d_h_one)
    sums_ref[1:2, :] += add_rows(d_h_one * normed)
    out_ref[...] = (d_res_ref[...] + norm_back(normed, inverse, d_h_one * (1.0 + vectors_ref[1:2, :]))).astype(BF16)


def input_grads(inputs, half, d_residual, vectors, packed, grads):
    rows, width = inputs.shape
    block = pick_block(rows, 256)
    first = half * (rows // block)
    row_spec = pl.BlockSpec((block, width), lambda i: (i, 0))
    flat = [grad for group in grads for grad in group]
    return pl.pallas_call(
        functools.partial(input_grads_kernel, len(grads)),
        grid=(rows // block,),
        in_specs=[
            row_spec,
            pl.BlockSpec((block, width), lambda i: (i + first, 0)),
            whole_spec(vectors.shape),
            whole_spec((width, 3 * width)),
        ]
        + [pl.BlockSpec((grad.shape[0], block), lambda i: (0, i + first)) for grad in flat],
        out_specs=[row_spec, whole_spec((8, width))],
        out_shape=[jax.ShapeDtypeStruct((rows, width), BF16), jax.ShapeDtypeStruct((8, width), F32)],
        compiler_params=pltpu.CompilerParams(vmem_limit_bytes=VMEM_LIMIT),
        cost_estimate=pl.CostEstimate(
            flops=6 * rows * width * width, bytes_accessed=14 * rows * width + 6 * width * width, transcendentals=0
        ),
        name="input_grads",
    )(inputs, d_residual, vectors, packed, *flat)


def time_features(t_index, model_width):
    half_width = model_width // 2
    indices = jnp.arange(half_width).astype(F32)
    frequency = jnp.exp(indices * (-math.log(10000.0) / (half_width - 1)))
    angles = t_index.astype(F32)[:, None] * frequency[None, :]
    return jnp.concatenate([jnp.sin(angles), jnp.cos(angles)], axis=1)


def rotary_tables(places):
    inverse = jnp.exp(jnp.arange(HALF).astype(F32) * (-2.0 * math.log(10000.0) / HDIM))
    angles = inverse[:, None] * places.astype(F32)[None, :]
    return jnp.cos(angles), jnp.sin(angles)


def after(values, *others):
    return lax.optimization_barrier((values,) + others)[0]


def make_body(mesh):
    n_dp, n_fsdp = mesh.shape["dp"], mesh.shape["fsdp"]
    n_pairs = n_fsdp // 2

    def shift(values, axis, size, by):
        return lax.ppermute(values, axis, [(i, (i + by) % size) for i in range(size)])

    def pick(values, index, axis=0):
        return lax.dynamic_index_in_dim(values, index, axis, keepdims=False)

    def body(
        frames,
        lengths,
        t_index,
        w_ada,
        b_ada,
        w_query,
        b_query,
        w_key,
        b_key,
        w_value,
        b_value,
        w_out,
        b_out,
        w_up,
        b_up,
        w_down,
        b_down,
        grad_out,
    ):
        slots, local, width = frames.shape
        group = n_fsdp // slots
        hidden_width = w_up.shape[1]
        shard = w_query.shape[0]
        ada_width = w_ada.shape[1]
        dp, fsdp = lax.axis_index("dp"), lax.axis_index("fsdp")
        me = dp * n_fsdp + fsdp
        slot, place = fsdp // group, fsdp % group
        other = 1 - slot
        core, pair = fsdp % 2, fsdp // 2
        side, deep, far = dp % 2, dp // 2, n_dp // 2
        length = pick(lengths, slot)

        def picked(values):
            return pick(values, slot), pick(values, other)

        split = local % 128 == 0

        def swap_in(own, away):
            parts = own, shift(away, "fsdp", n_fsdp, group)
            return parts if split else (jnp.concatenate(parts),) * 2

        def swap_out(own, away):
            whole = jnp.zeros((slots, local, width), own.dtype)
            whole = lax.dynamic_update_index_in_dim(whole, own, slot, 0)
            arrived = shift(away, "fsdp", n_fsdp, group)
            return lax.dynamic_update_index_in_dim(whole, arrived, other, 0)

        def places_of(member):
            at = slot * group + member
            blocks = [((at - by * group) + n_fsdp) % n_fsdp for by in range(slots)]
            return jnp.concatenate([b * local + jnp.arange(local, dtype=jnp.int32) for b in blocks])

        ring = lambda by: [(i, (i // group) * group + (i % group + by) % group) for i in range(n_fsdp)]

        def swap(values, axis, size):
            return lax.ppermute(values, axis, [(i, i ^ 1) for i in range(size)])

        def sum_core(values):
            values = values.reshape(n_dp, n_pairs, 2, shard, values.shape[1])
            arrived = swap(pick(values, 1 - core, 2), "fsdp", n_fsdp)
            return (pick(values, core, 2).astype(F32) + arrived.astype(F32)).astype(BF16)

        def sum_pairs(values):
            total = pick(values, pair, 1).astype(F32)
            for by in range(1, n_pairs):
                arrived = shift(pick(values, (pair + by) % n_pairs, 1), "fsdp", n_fsdp, 2 * by)
                total = total + arrived.astype(F32)
            return total.astype(BF16)

        def sum_side(values):
            values = values.reshape((far, 2) + values.shape[1:])
            arrived = swap(pick(values, 1 - side, 1), "dp", n_dp)
            return (pick(values, side, 1).astype(F32) + arrived.astype(F32)).astype(BF16)

        def sum_far(values):
            total = pick(values, deep).astype(F32)
            for by in range(1, far):
                arrived = shift(pick(values, (deep + by) % far), "dp", n_dp, 2 * by)
                total = total + arrived.astype(F32)
            return total

        def gather_dp(values):
            values = jnp.stack([values] + [shift(values, "dp", n_dp, 2 * by) for by in range(1, far)])
            return jnp.stack([values, swap(values, "dp", n_dp)])

        packed = lax.all_gather(jnp.concatenate([w_key, w_value, w_query], axis=1), AXES, axis=0, tiled=True)
        out_up = lax.all_gather(jnp.concatenate([w_out, w_up], axis=1), AXES, axis=0, tiled=True)
        full_down = lax.all_gather(w_down, AXES, axis=0, tiled=True)

        inputs = swap_in(*picked(frames))
        rows = slots * local
        own_grad, away_grad = picked(grad_out)

        t_all = gather_dp(t_index).reshape(-1)
        active = jax.nn.silu(time_features(t_all, width)).astype(BF16)
        active_mine = lax.dynamic_slice_in_dim(active, me * shard, shard, axis=1)
        partial = [dot(active_mine, w_ada, 1, 0)]
        for bias in (b_query, b_key, b_value, b_out, b_down, b_up):
            size = bias.shape[0]
            zeros = jnp.zeros((1, size * n_dp * n_fsdp), F32)
            placed = lax.dynamic_update_slice_in_dim(zeros, bias.astype(F32)[None], me * size, axis=1)
            partial.append(jnp.broadcast_to(placed, (n_dp * slots, placed.shape[1])))
        placed = lax.dynamic_update_slice_in_dim(
            jnp.zeros((1, ada_width), F32), b_ada.astype(F32)[None], me * b_ada.shape[0], axis=1
        )
        partial[0] = partial[0] + placed
        partial = jnp.concatenate(partial, axis=1).reshape(2, far, slots, -1)
        partial = partial[0] + swap(partial[1], "dp", n_dp)
        summed = partial[0]
        for by in range(1, far):
            summed = summed + shift(partial[by], "dp", n_dp, -2 * by)
        one = pick(summed, slot) + shift(pick(summed, other), "fsdp", n_fsdp, group)
        vectors = one
        for by in range(1, group):
            vectors = vectors + lax.ppermute(one, "fsdp", ring(by))
        vectors = vectors.reshape(-1, width)
        vectors = jnp.pad(vectors, ((0, -vectors.shape[0] % 8), (0, 0)))

        key_places = jnp.concatenate([places_of((place - by + group) % group) for by in range(group)])
        cosine, sine = rotary_tables(key_places)
        key_bias = jnp.where(key_places < length, 0.0, -1e30)
        bias_columns = jnp.pad(key_bias.astype(BF16)[:, None], ((0, 0), (0, HDIM - 1)))
        keep = (key_places[:rows] < length).astype(F32)[:, None]

        wide = 2
        vectors, cosine, sine, key_bias, bias_columns, keep, own_grad, away_grad = lax.optimization_barrier(
            (vectors, cosine, sine, key_bias, bias_columns, keep, own_grad, away_grad)
        )
        h_one, q_rot, keys, values = project(inputs, vectors, packed, cosine[:, :rows], sine[:, :rows], wide)
        cotangent = swap_in(own_grad, after(away_grad, keys[0]))
        heads = width // HDIM
        tall = heads // wide
        with_ring = lambda own: [own] + [lax.ppermute(own, "fsdp", ring(by)) for by in range(1, group)]
        k_parts, v_parts = [with_ring(own) for own in keys], [with_ring(own) for own in values]
        heads_out, lses = [], []
        for at in range(wide):
            out, lse = attend(q_rot, k_parts[at], v_parts[at], bias_columns, at * tall)
            heads_out.append(out)
            lses.append(lse)
        mixed, d_residual, d_heads, g_rows, sums_two, g_b_up = feed_forward(
            inputs, heads_out, cotangent, keep, out_up, full_down, vectors, shard
        )
        mixed = swap_out(mixed[:local], mixed[local:])

        if shard % 16:
            first = width + hidden_width
            g_down = jnp.concatenate([g_rows[:, first + i * width : first + (i + 1) * width] for i in range(hidden_width // width)])
            g_down = g_down.reshape(n_dp * n_fsdp, -1, shard, width)
            g_down = [g_down[:, i].reshape(-1, width) for i in range(g_down.shape[1])]
            g_rows = jnp.concatenate([g_rows[:, :first]] + g_down, axis=1)
        sum_rows = lax.psum_scatter(g_rows, AXES, scatter_dimension=0, tiled=True).astype(F32)

        grads, d_biases, moving = [], [], []
        stages = [sum_core, sum_pairs, sum_side, sum_far]

        def start_sum(pieces):
            dq, dk, dv, weight_grad, bias_grad = weight_grads(h_one, pieces)
            grads.append((dq, dk, dv))
            d_biases.append(bias_grad[:, :3])
            moving.append([0, weight_grad])
            return weight_grad

        def move_on(pick_from):
            for item in pick_from:
                if item[0] < len(stages):
                    item[1] = stages[item[0]](item[1])
                    item[0] += 1
            return [item[1] for item in pick_from]

        counts = (4, 4, 2, 2, 2, 2)
        joined = (1, 1, 2, 2)
        steps = len(counts)
        waiting, ready, first, next_sum = [], d_heads, 0, 0
        for step, each in enumerate(counts):
            part, within = first // tall, first % tall
            dq, dk_parts, dv_parts = attend_back(
                q_rot,
                k_parts[part],
                v_parts[part],
                ready,
                heads_out[part],
                lses[part],
                key_bias[None],
                cosine,
                sine,
                first,
                within,
                each,
            )
            first += each
            done = move_on(moving)
            if len(waiting) >= joined[next_sum]:
                done.append(start_sum(waiting[: joined[next_sum]]))
                waiting = waiting[joined[next_sum] :]
                next_sum += 1
            dk_parts = [dk_parts[0]] + [lax.ppermute(dk_parts[by], "fsdp", ring(-by)) for by in range(1, group)]
            dv_parts = [dv_parts[0]] + [lax.ppermute(dv_parts[by], "fsdp", ring(-by)) for by in range(1, group)]
            waiting.append((dq, dk_parts, dv_parts))
            if done and step + 1 < steps:
                ready = after(d_heads, dq, *done)
        last = start_sum(waiting)
        if split:
            rest = after(d_residual, last)
            away_frames, sums_away = input_grads(inputs[1], 1, rest, vectors, packed, grads)
            done = move_on(moving)
            rest, away_frames = lax.optimization_barrier((d_residual, away_frames, *done))[:2]
            own_frames, sums_own = input_grads(inputs[0], 0, rest, vectors, packed, grads)
            sums_one = sums_own + sums_away
        else:
            both, sums_one = input_grads(inputs[0], 0, d_residual, vectors, packed, grads)
            own_frames, away_frames = both[:local], both[local:]
        grad_frames = swap_out(own_frames, away_frames)
        for _ in stages:
            move_on(moving)
        sums = [item[1] for item in moving]

        vector = jnp.concatenate(
            [sums_one[:2], sums_two[:6], g_b_up.reshape(-1, width), jnp.concatenate(d_biases).T]
        )
        for_slot = 6
        total = vector
        for by in range(1, group):
            total = total + lax.ppermute(vector, "fsdp", ring(by))
        packs = gather_dp(total).reshape(n_dp, -1, width)
        pack = jnp.concatenate([packs[:, :for_slot].reshape(-1, width), jnp.sum(packs[:, for_slot:], axis=0)])
        across = shift(pack, "fsdp", n_fsdp, group)
        count = n_dp * for_slot
        d_mod = jnp.stack([jnp.where(slot == s, pack[:count], across[:count]).reshape(n_dp, -1) for s in range(slots)], axis=1)
        d_mod = d_mod.reshape(n_dp * slots, for_slot * width)
        d_vectors = pack[count:] + across[count:]

        g_w_ada = lax.dot_general(
            active_mine.astype(F32),
            d_mod,
            (((0,), (0,)), ((), ())),
            precision=lax.Precision.HIGHEST,
            preferred_element_type=F32,
        )

        def mine(vector):
            vector = vector.reshape(-1)
            size = vector.shape[0] // (n_dp * n_fsdp)
            return lax.dynamic_slice_in_dim(vector, me * size, size)

        ups = hidden_width // width
        columns = [values.reshape(shard, 3, -1) for values in sums]
        g_qkv = [jnp.concatenate([values[:, i] for values in columns], axis=1) for i in range(3)]
        g_down = sum_rows[:, width + hidden_width :].reshape(shard, -1, width)
        return (
            mixed,
            grad_frames,
            g_w_ada,
            mine(jnp.sum(d_mod, axis=0)),
            g_qkv[0],
            mine(d_vectors[2 + ups]),
            g_qkv[1],
            mine(d_vectors[3 + ups]),
            g_qkv[2],
            mine(d_vectors[4 + ups]),
            sum_rows[:, :width],
            mine(d_vectors[0]),
            sum_rows[:, width : width + hidden_width],
            mine(d_vectors[2 : 2 + ups]),
            jnp.swapaxes(g_down, 0, 1).reshape(w_down.shape),
            mine(d_vectors[1]),
        )

    return body


def solution(mesh):
    rows, vector, matrix = P("dp", "fsdp", None), P(AXES), P(AXES, None)
    return jax.shard_map(
        make_body(mesh),
        mesh=mesh,
        in_specs=(rows, P("dp"), P("dp")) + (matrix, vector) * 7 + (rows,),
        out_specs=(rows, rows) + (matrix, vector) * 7,
        check_vma=False,
    )
```

```python
import functools
import math

import jax
import jax.numpy as jnp
from jax import lax
from jax.experimental import pallas as pl
from jax.experimental.pallas import tpu as pltpu
from jax.sharding import PartitionSpec as P

HDIM = 64
HALF = HDIM // 2
SCALE = HDIM ** (-0.5)
SCALE2 = SCALE * math.log2(math.e)
AXES = ("dp", "fsdp")
VMEM_LIMIT = 62 << 20
F32 = jnp.float32
BF16 = jnp.bfloat16


def dot(left_side, right_side, left_dim, right_dim):
    return lax.dot_general(
        left_side,
        right_side,
        (((left_dim,), (right_dim,)), ((), ())),
        preferred_element_type=F32,
    )


def pick_block(total, wanted):
    block = min(total, wanted)
    while total % block:
        block -= 128
    return block


def attend_kernel(parts, chunk, *refs):
    q_ref, bias_ref = refs[0], refs[1]
    k_refs, v_refs = refs[2 : 2 + parts], refs[2 + parts : 2 + 2 * parts]
    o_ref, lse_ref, k_aug, v_aug, q_aug = refs[2 + 2 * parts :]
    head, block = pl.program_id(0), pl.program_id(1)
    span = k_aug.shape[0]
    part = span // parts
    q_rows = q_ref.shape[1]

    @pl.when((head == 0) & (block == 0))
    def _():
        k_aug[:, HDIM:] = bias_ref[...]
        v_aug[HDIM:, :] = jnp.ones((16, span), BF16)
        q_aug[HDIM:, :] = jnp.ones((HDIM, q_rows), BF16)

    @pl.when(block == 0)
    def _():
        for i in range(parts):
            k_aug[i * part : (i + 1) * part, :HDIM] = k_refs[i][...].T
            v_aug[:HDIM, i * part : (i + 1) * part] = v_refs[i][...]

    q_aug[:HDIM, :] = q_ref[...]
    queries = q_aug[...]
    count = span // chunk

    def scores(i):
        return dot(k_aug[i * chunk : (i + 1) * chunk, :], queries, 1, 0)

    upcoming = scores(0)
    row_max = total = None
    for i in range(count):
        current = upcoming
        if i + 1 < count:
            upcoming = scores(i + 1)
        chunk_max = jnp.max(current, axis=0, keepdims=True) * SCALE2
        new_max = chunk_max if i == 0 else jnp.maximum(row_max, chunk_max)
        weights = jnp.exp2(current * SCALE2 - new_max).astype(BF16)
        update = dot(v_aug[:, i * chunk : (i + 1) * chunk], weights, 1, 0)
        total = update if i == 0 else total * jnp.exp2(row_max - new_max) + update
        row_max = new_max
    denominator = total[HDIM : HDIM + 1, :]
    o_ref[...] = (total[:HDIM, :] / denominator).astype(BF16)
    lse_ref[...] = (row_max + jnp.log2(denominator))[None]


def attend(q_rot, k_parts, v_parts, bias_columns, first):
    width, rows = k_parts[0].shape
    parts = len(k_parts)
    span = parts * rows
    heads = width // HDIM
    q_rows = pick_block(rows, 768)
    chunk = pick_block(span, 512)
    q_spec = pl.BlockSpec((HDIM, q_rows), lambda h, j: (h + first, j))
    k_spec = pl.BlockSpec((HDIM, rows), lambda h, j: (h, 0))
    return pl.pallas_call(
        functools.partial(attend_kernel, parts, chunk),
        grid=(heads, rows // q_rows),
        in_specs=[q_spec, pl.BlockSpec((span, HDIM), lambda h, j: (0, 0))] + [k_spec] * (2 * parts),
        out_specs=[
            pl.BlockSpec((HDIM, q_rows), lambda h, j: (h, j)),
            pl.BlockSpec((1, 1, q_rows), lambda h, j: (h, 0, j)),
        ],
        out_shape=[
            jax.ShapeDtypeStruct((width, rows), BF16),
            jax.ShapeDtypeStruct((heads, 1, rows), F32),
        ],
        scratch_shapes=[
            pltpu.VMEM((span, 2 * HDIM), BF16),
            pltpu.VMEM((HDIM + 16, span), BF16),
            pltpu.VMEM((2 * HDIM, q_rows), BF16),
        ],
        compiler_params=pltpu.CompilerParams(vmem_limit_bytes=VMEM_LIMIT),
        cost_estimate=pl.CostEstimate(
            flops=16 * heads * rows * span * HDIM,
            bytes_accessed=2 * width * (2 * rows + 2 * span),
            transcendentals=heads * rows * span,
        ),
        name="attend",
    )(q_rot, bias_columns, *k_parts, *v_parts)


def in_three(values):
    first = values.astype(BF16)
    rest = values - first.astype(F32)
    second = rest.astype(BF16)
    return first.astype(F32), second.astype(F32), rest - second.astype(F32)


def unrotate(values, cosine, sine):
    low, high = values[:HALF], values[HALF:]
    return low * cosine + high * sine, high * cosine - low * sine


def attend_back_kernel(parts, chunk, *refs):
    q_ref, do_ref, o_ref, lse_ref, bias_ref, cos_ref, sin_ref = refs[:7]
    k_refs, v_refs = refs[7 : 7 + parts], refs[7 + parts : 7 + 2 * parts]
    dq_ref = refs[7 + 2 * parts]
    dk_refs = refs[8 + 2 * parts : 8 + 3 * parts]
    dv_refs = refs[8 + 3 * parts : 8 + 4 * parts]
    k_aug, v_aug, k_rows, q_aug, do_aug, dk_acc, dv_acc = refs[8 + 4 * parts :]
    head, block = pl.program_id(0), pl.program_id(1)
    span = k_aug.shape[1]
    part = span // parts
    q_rows = q_ref.shape[1]

    @pl.when((head == 0) & (block == 0))
    def _():
        row = lax.broadcasted_iota(jnp.int32, (HDIM, span), 0)
        ones = jnp.where(row < 4, 1.0, 0.0)
        k_aug[HDIM:, :] = jnp.where(row == 0, bias_ref[...], ones).astype(BF16)
        v_aug[HDIM:, :] = jnp.where(row < 3, 1.0, 0.0).astype(BF16)
        k_rows[:, HDIM:] = jnp.zeros((span, HDIM), BF16)

    @pl.when(block == 0)
    def _():
        for i in range(parts):
            at = slice(i * part, (i + 1) * part)
            keys = k_refs[i][...]
            k_aug[:HDIM, at] = keys
            v_aug[:HDIM, at] = v_refs[i][...]
            k_rows[at, :HDIM] = keys.T
        dk_acc[...] = jnp.zeros_like(dk_acc)
        dv_acc[...] = jnp.zeros_like(dv_acc)

    queries, d_heads = q_ref[...], do_ref[...]
    delta = jnp.sum(d_heads.astype(F32) * o_ref[...].astype(F32), axis=0, keepdims=True)
    row = lax.broadcasted_iota(jnp.int32, (HDIM, q_rows), 0)
    lse_a, lse_b, lse_c = in_three(lse_ref[0] * (-1.0 / SCALE2))
    del_a, del_b, del_c = in_three(-delta)
    q_extra = jnp.where(row == 2, lse_b, jnp.where(row == 3, lse_c, 0.0))
    q_extra = jnp.where(row == 0, 1.0, jnp.where(row == 1, lse_a, q_extra))
    do_extra = jnp.where(row == 1, del_b, jnp.where(row == 2, del_c, 0.0))
    do_extra = jnp.where(row == 0, del_a, do_extra)
    q_aug[:HDIM, :] = queries
    q_aug[HDIM:, :] = q_extra.astype(BF16)
    do_aug[:HDIM, :] = d_heads
    do_aug[HDIM:, :] = do_extra.astype(BF16)
    q_side, do_side = q_aug[...].T, do_aug[...].T
    count = span // chunk

    def products(i):
        at = slice(i * chunk, (i + 1) * chunk)
        return dot(q_side, k_aug[:, at], 1, 0), dot(do_side, v_aug[:, at], 1, 0)

    upcoming = products(0)
    d_query = None
    for i in range(count):
        at = slice(i * chunk, (i + 1) * chunk)
        scores, d_probs = upcoming
        if i + 1 < count:
            upcoming = products(i + 1)
        probs = jnp.exp2(scores * SCALE2)
        d_scores = (probs * d_probs).astype(BF16)
        dv_acc[:, at] += dot(d_heads, probs.astype(BF16), 1, 0)
        dk_acc[:, at] += dot(queries, d_scores, 1, 0)
        update = dot(d_scores, k_rows[at, :], 1, 0)
        d_query = update if i == 0 else d_query + update
    first = pl.multiple_of(block * q_rows, q_rows)
    low, high = unrotate(
        d_query.T[:HDIM, :] * SCALE, cos_ref[:, pl.ds(first, q_rows)], sin_ref[:, pl.ds(first, q_rows)]
    )
    dq_ref[:HALF, :] = low.astype(BF16)
    dq_ref[HALF:, :] = high.astype(BF16)

    @pl.when(block == pl.num_programs(1) - 1)
    def _():
        for i in range(parts):
            at = slice(i * part, (i + 1) * part)
            low, high = unrotate(dk_acc[:, at] * SCALE, cos_ref[:, at], sin_ref[:, at])
            dk_refs[i][:HALF, :] = low.astype(dk_refs[i].dtype)
            dk_refs[i][HALF:, :] = high.astype(dk_refs[i].dtype)
            dv_refs[i][...] = dv_acc[:, at].astype(dv_refs[i].dtype)


def attend_back(q_rot, k_parts, v_parts, d_heads, heads_out, lse, bias_row, cosine, sine, first, within, count):
    rows = q_rot.shape[1]
    parts = len(k_parts)
    span = parts * rows
    q_rows = pick_block(rows, 1536)
    chunk = pick_block(span, 256)
    q_spec = pl.BlockSpec((HDIM, q_rows), lambda h, j: (h + first, j))
    k_spec = pl.BlockSpec((HDIM, rows), lambda h, j: (h + within, 0))
    whole = lambda array: pl.BlockSpec(array.shape, lambda h, j: (0, 0))
    part_out = pl.BlockSpec((HDIM, rows), lambda h, j: (h, 0))
    shape = lambda kind: jax.ShapeDtypeStruct((count * HDIM, rows), kind)
    part_kinds = [F32] + [BF16] * (parts - 1)
    out = pl.pallas_call(
        functools.partial(attend_back_kernel, parts, chunk),
        grid=(count, rows // q_rows),
        in_specs=[
            q_spec,
            q_spec,
            pl.BlockSpec((HDIM, q_rows), lambda h, j: (h + within, j)),
            pl.BlockSpec((1, 1, q_rows), lambda h, j: (h + within, 0, j)),
            whole(bias_row),
            whole(cosine),
            whole(sine),
        ]
        + [k_spec] * (2 * parts),
        out_specs=[pl.BlockSpec((HDIM, q_rows), lambda h, j: (h, j))] + [part_out] * (2 * parts),
        out_shape=[shape(BF16)] + [shape(kind) for kind in part_kinds * 2],
        scratch_shapes=[
            pltpu.VMEM((2 * HDIM, span), BF16),
            pltpu.VMEM((2 * HDIM, span), BF16),
            pltpu.VMEM((span, 2 * HDIM), BF16),
            pltpu.VMEM((2 * HDIM, q_rows), BF16),
            pltpu.VMEM((2 * HDIM, q_rows), BF16),
            pltpu.VMEM((HDIM, span), F32),
            pltpu.VMEM((HDIM, span), F32),
        ],
        compiler_params=pltpu.CompilerParams(vmem_limit_bytes=VMEM_LIMIT),
        cost_estimate=pl.CostEstimate(
            flops=10 * count * rows * span * HDIM,
            bytes_accessed=2 * count * HDIM * (8 * rows + 4 * span),
            transcendentals=0,
        ),
        name="attend_back",
    )(q_rot, d_heads, heads_out, lse, bias_row, cosine, sine, *k_parts, *v_parts)
    return out[0], out[1 : 1 + parts], out[1 + parts :]


def norm_parts(values):
    centered = values - jnp.mean(values, axis=-1, keepdims=True)
    scale = lax.rsqrt(jnp.mean(centered * centered, axis=-1, keepdims=True) + 1e-06)
    return centered * scale, scale


def norm_back(normed, scale, d_normed):
    return (
        d_normed
        - jnp.mean(d_normed, axis=-1, keepdims=True)
        - normed * jnp.mean(d_normed * normed, axis=-1, keepdims=True)
    ) * scale


def gelu_both(values):
    square = values * values
    bend = jnp.tanh(0.7978845608028654 * (values + 0.044715 * values * square))
    half = 0.5 * (1.0 + bend)
    slope = 0.7978845608028654 * (1.0 + 3 * 0.044715 * square)
    return values * half, half + 0.5 * values * (1.0 - bend * bend) * slope


def add_rows(values):
    return jnp.sum(values, axis=0, keepdims=True)


def store_rotated(out_ref, values, cosine, sine):
    for at in range(0, out_ref.shape[0], HDIM):
        low, high = values[at : at + HALF], values[at + HALF : at + HDIM]
        out_ref[at : at + HALF, :] = (low * cosine - high * sine).astype(BF16)
        out_ref[at + HALF : at + HDIM, :] = (high * cosine + low * sine).astype(BF16)


def either(first_ref, second_ref):
    half = pl.num_programs(0) // 2
    return jnp.where(pl.program_id(0) < half, first_ref[...], second_ref[...])


def halves_spec(inputs, rows, block, width):
    if inputs[0].shape[0] == rows:
        return [pl.BlockSpec((block, width), lambda i, *_: (i, 0))] * 2
    half = rows // 2 // block
    return [
        pl.BlockSpec((block, width), lambda i, *_: (jnp.minimum(i, half - 1), 0)),
        pl.BlockSpec((block, width), lambda i, *_: (jnp.maximum(i - half, 0), 0)),
    ]


def project_kv_kernel(groups, x_ref, y_ref, vectors_ref, w_ref, cos_ref, sin_ref, h_ref, *refs):
    k_refs, v_refs = refs[:groups], refs[groups:]
    width = x_ref.shape[1]
    tall = width // groups
    normed, _ = norm_parts(either(x_ref, y_ref).astype(F32))
    h_one = (normed * (1.0 + vectors_ref[1:2, :]) + vectors_ref[0:1, :]).astype(BF16)
    h_ref[...] = h_one
    keys = (dot(h_one, w_ref[:, :width], 1, 0) + vectors_ref[7:8, :]).T
    values = (dot(h_one, w_ref[:, width:], 1, 0) + vectors_ref[8:9, :]).astype(BF16).T
    for i in range(groups):
        store_rotated(k_refs[i], keys[i * tall : (i + 1) * tall], cos_ref[...], sin_ref[...])
        v_refs[i][...] = values[i * tall : (i + 1) * tall]


def project_q_kernel(h_ref, vectors_ref, w_ref, cos_ref, sin_ref, q_ref):
    queries = dot(h_ref[...], w_ref[...], 1, 0) + vectors_ref[6:7, :]
    store_rotated(q_ref, queries.T, cos_ref[...], sin_ref[...])


def whole_spec(shape, column=0):
    return pl.BlockSpec(shape, lambda i, *_: (0, column), pipeline_mode=pl.Buffered(1))


def project(inputs, vectors, packed, cosine, sine, groups):
    width, rows = inputs[0].shape[1], cosine.shape[1]
    block = pick_block(inputs[0].shape[0], 256)
    tall = width // groups
    row_spec = pl.BlockSpec((block, width), lambda i: (i, 0))
    turned_spec = lambda height: pl.BlockSpec((height, block), lambda i: (0, i))
    turned = lambda height: jax.ShapeDtypeStruct((height, rows), BF16)
    table_spec = turned_spec(HALF)
    params = pltpu.CompilerParams(vmem_limit_bytes=VMEM_LIMIT)
    out = pl.pallas_call(
        functools.partial(project_kv_kernel, groups),
        grid=(rows // block,),
        in_specs=halves_spec(inputs, rows, block, width)
        + [whole_spec(vectors.shape), whole_spec((width, 2 * width)), table_spec, table_spec],
        out_specs=[row_spec] + [turned_spec(tall)] * (2 * groups),
        out_shape=[jax.ShapeDtypeStruct((rows, width), BF16)] + [turned(tall)] * (2 * groups),
        compiler_params=params,
        cost_estimate=pl.CostEstimate(
            flops=8 * rows * width * width, bytes_accessed=8 * rows * width + 4 * width * width, transcendentals=0
        ),
        name="project_kv",
    )(*inputs, vectors, packed, cosine, sine)
    h_one, keys, values = out[0], out[1 : 1 + groups], out[1 + groups :]
    queries = pl.pallas_call(
        project_q_kernel,
        grid=(rows // block,),
        in_specs=[row_spec, whole_spec(vectors.shape), whole_spec((width, width), 2), table_spec, table_spec],
        out_specs=turned_spec(width),
        out_shape=turned(width),
        compiler_params=params,
        cost_estimate=pl.CostEstimate(
            flops=4 * rows * width * width, bytes_accessed=4 * rows * width + 2 * width * width, transcendentals=0
        ),
        name="project_q",
    )(h_one, vectors, packed, cosine, sine)
    return h_one, queries, keys, values


def feed_forward_kernel(parts, pieces, split, slot_ref, *refs):
    o_refs = refs[:parts]
    x_ref, y_ref, cot_ref, cot_y_ref, keep_ref, w_ref, vectors_ref = refs[parts : parts + 7]
    own_ref, away_ref, d_res_ref, d_heads_ref, g_rows_ref, sums_ref = refs[parts + 7 : parts + 13]
    acc, acc_rows, slope_ref, hidden_ref, staged, sems = refs[parts + 13 :]
    step, count = pl.program_id(0), pl.num_programs(0)
    width = x_ref.shape[1]

    @pl.when(step == 0)
    def _():
        acc[...] = jnp.zeros_like(acc)
        acc_rows[...] = jnp.zeros_like(acc_rows)

    gate_one, shift_two, scale_two, gate_two, b_out, b_down = [vectors_ref[i : i + 1, :] for i in (2, 3, 4, 5, 9, 10)]
    out_at = slice(0, width)
    up_at = [slice((1 + i) * width, (2 + i) * width) for i in range(pieces)]
    down_at = [slice((1 + pieces + i) * width, (2 + pieces + i) * width) for i in range(pieces)]
    keep = keep_ref[...]
    heads_out = jnp.concatenate([ref[...] for ref in o_refs], axis=0)
    branch = (dot(heads_out, w_ref[:, out_at], 0, 0) + b_out) * keep
    residual = either(x_ref, y_ref).astype(F32) + gate_one * branch
    normed, inverse = norm_parts(residual)
    h_two = (normed * (1.0 + scale_two) + shift_two).astype(BF16)
    ff_out = b_down
    for i in range(pieces):
        value, slope = gelu_both(dot(h_two, w_ref[:, up_at[i]], 1, 0) + vectors_ref[11 + i : 12 + i, :])
        slope_ref[i] = slope
        hidden = value.astype(BF16)
        hidden_ref[i] = hidden
        ff_out = ff_out + dot(hidden, w_ref[:, down_at[i]], 1, 0)
    mixed = (residual + gate_two * ff_out).astype(BF16)
    if split:

        @pl.when(step < count // 2)
        def _():
            own_ref[0] = mixed

        @pl.when(step >= count // 2)
        def _():
            away_ref[...] = mixed
    else:
        own_ref[...] = mixed
    d_mixed = either(cot_ref, cot_y_ref).astype(F32)
    acc_rows[3:4, :] += add_rows(d_mixed * ff_out)
    d_ff = (d_mixed * gate_two).astype(BF16)
    acc_rows[5:6, :] += add_rows(d_ff.astype(F32))
    d_h_two = None
    for i in range(pieces):
        acc[:, down_at[i]] += dot(hidden_ref[i], d_ff, 0, 0)
        d_up = (dot(d_ff, w_ref[:, down_at[i]], 1, 1) * slope_ref[i]).astype(BF16)
        acc_rows[6 + i : 7 + i, :] += add_rows(d_up.astype(F32))
        acc[:, up_at[i]] += dot(h_two, d_up, 0, 0)
        update = dot(d_up, w_ref[:, up_at[i]], 1, 1)
        d_h_two = update if i == 0 else d_h_two + update
    acc_rows[1:2, :] += add_rows(d_h_two)
    acc_rows[2:3, :] += add_rows(d_h_two * normed)
    d_residual = d_mixed + norm_back(normed, inverse, d_h_two * (1.0 + scale_two))
    d_res_ref[...] = d_residual
    acc_rows[0:1, :] += add_rows(d_residual * branch)
    d_branch = (d_residual * gate_one * keep).astype(BF16)
    acc_rows[4:5, :] += add_rows(d_branch.astype(F32))
    acc[:, out_at] += dot(heads_out, d_branch, 1, 0)
    d_heads_ref[...] = dot(w_ref[:, out_at], d_branch, 1, 1).astype(BF16)

    @pl.when(step == count - 1)
    def _():
        sums_ref[...] = acc_rows[...]
        tall = staged.shape[1]
        copies = []
        for i in range(width // tall):
            slot = i % 2
            if i >= 2:
                copies[i - 2].wait()
            staged[slot] = acc[i * tall : (i + 1) * tall, :].astype(BF16)
            copies.append(pltpu.make_async_copy(staged.at[slot], g_rows_ref.at[pl.ds(i * tall, tall), :], sems.at[slot]))
            copies[i].start()
        for copy in copies[-2:]:
            copy.wait()


def feed_forward(slot, inputs, heads_out, cotangent, keep, packed, vectors, slots):
    rows, width = heads_out[0].shape[1], inputs[0].shape[1]
    pieces = (packed.shape[1] // width - 1) // 2
    block = pick_block(inputs[0].shape[0], 256)
    local = rows // slots
    split = inputs[0].shape[0] == local
    half = local // block
    row_spec = pl.BlockSpec((block, width), lambda i, *_: (i, 0))
    turned_spec = lambda height: pl.BlockSpec((height, block), lambda i, *_: (0, i))
    kinds = jax.ShapeDtypeStruct
    if split:
        mixed_specs = [
            pl.BlockSpec((1, block, width), lambda i, at: (at[0], jnp.minimum(i, half - 1), 0)),
            pl.BlockSpec((block, width), lambda i, *_: (jnp.maximum(i - half, 0), 0)),
        ]
        mixed_shapes = [kinds((slots, local, width), BF16), kinds((local, width), BF16)]
    else:
        mixed_specs = [row_spec, whole_spec((8, 128))]
        mixed_shapes = [kinds((rows, width), BF16), kinds((8, 128), BF16)]
    return pl.pallas_call(
        functools.partial(feed_forward_kernel, len(heads_out), pieces, split),
        grid_spec=pltpu.PrefetchScalarGridSpec(
            num_scalar_prefetch=1,
            grid=(rows // block,),
            in_specs=[turned_spec(part.shape[0]) for part in heads_out]
            + halves_spec(inputs, rows, block, width) * 2
            + [
                pl.BlockSpec((block, 1), lambda i, *_: (i, 0)),
                whole_spec(packed.shape),
                whole_spec(vectors.shape),
            ],
            out_specs=mixed_specs
            + [
                row_spec,
                turned_spec(width),
                pl.BlockSpec(memory_space=pl.ANY),
                whole_spec((8, width)),
            ],
            scratch_shapes=[
                pltpu.VMEM(packed.shape, F32),
                pltpu.VMEM((8, width), F32),
                pltpu.VMEM((pieces, block, width), F32),
                pltpu.VMEM((pieces, block, width), BF16),
                pltpu.VMEM((2, pick_block(width, 256), packed.shape[1]), BF16),
                pltpu.SemaphoreType.DMA((2,)),
            ],
        ),
        out_shape=mixed_shapes
        + [
            kinds((rows, width), F32),
            kinds((width, rows), BF16),
            kinds(packed.shape, BF16),
            kinds((8, width), F32),
        ],
        compiler_params=pltpu.CompilerParams(vmem_limit_bytes=VMEM_LIMIT),
        cost_estimate=pl.CostEstimate(
            flops=6 * rows * width * packed.shape[1],
            bytes_accessed=8 * rows * width + 4 * width * packed.shape[1],
            transcendentals=0,
        ),
        name="feed_forward",
    )(slot, *heads_out, *inputs, *cotangent, keep, packed, vectors)


def weight_grads_kernel(pieces, parts, h_ref, *refs):
    count = pieces * (1 + 2 * parts)
    per_piece = [refs[i * (1 + 2 * parts) : (i + 1) * (1 + 2 * parts)] for i in range(pieces)]
    dk_out, dv_out, weight_ref, bias_ref, grads_ref = refs[count:]
    tall = dk_out.shape[0]

    @pl.when(pl.program_id(0) == 0)
    def _():
        first = 0
        for piece in per_piece:
            height = piece[0].shape[0]
            for kind in range(3):
                start = (0, 1, 1 + parts)[kind]
                total = piece[start][...]
                for i in range(1, parts if kind else 1):
                    total = total + piece[start + i][...].astype(F32)
                total = total.astype(BF16)
                grads_ref[kind * tall + first : kind * tall + first + height, :] = total
                bias_ref[first : first + height, kind : kind + 1] = jnp.sum(total.astype(F32), axis=1, keepdims=True)
            first += height
        dk_out[...] = grads_ref[tall : 2 * tall, :]
        dv_out[...] = grads_ref[2 * tall :, :]

    weight_ref[...] = dot(grads_ref[...], h_ref[...], 1, 0).T.astype(BF16)


def weight_grads(h_one, pieces):
    rows, width = h_one.shape
    tall = sum(piece[0].shape[0] for piece in pieces)
    parts = len(pieces[0][1])
    block = pick_block(width, 256)
    kinds = jax.ShapeDtypeStruct
    flat = [array for piece in pieces for array in (piece[0], *piece[1], *piece[2])]
    return pl.pallas_call(
        functools.partial(weight_grads_kernel, len(pieces), parts),
        grid=(width // block,),
        in_specs=[pl.BlockSpec((rows, block), lambda i: (0, i))] + [whole_spec(array.shape) for array in flat],
        out_specs=[whole_spec((tall, rows))] * 2
        + [pl.BlockSpec((block, 3 * tall), lambda i: (i, 0)), whole_spec((tall, 128))],
        out_shape=[kinds((tall, rows), BF16)] * 2 + [kinds((width, 3 * tall), BF16), kinds((tall, 128), F32)],
        scratch_shapes=[pltpu.VMEM((3 * tall, rows), BF16)],
        compiler_params=pltpu.CompilerParams(vmem_limit_bytes=VMEM_LIMIT),
        cost_estimate=pl.CostEstimate(
            flops=6 * rows * width * tall, bytes_accessed=16 * rows * tall + 2 * rows * width, transcendentals=0
        ),
        name="weight_grads",
    )(h_one, *flat)


def input_grads_kernel(counts, slot_ref, x_ref, d_res_ref, vectors_ref, w_ref, *refs):
    grad_refs, (out_ref, sums_ref) = refs[:-2], refs[-2:]
    width = x_ref.shape[1]

    @pl.when(pl.program_id(0) == 0)
    def _():
        sums_ref[...] = jnp.zeros_like(sums_ref)

    turned = None
    used = 0
    for kind in range(3):
        first = (2, 0, 1)[kind] * width
        grad = jnp.concatenate([ref[...] for ref in grad_refs[used : used + counts[kind]]], axis=0)
        used += counts[kind]
        update = dot(w_ref[:, first : first + width], grad, 1, 0)
        turned = update if turned is None else turned + update
    d_h_one = turned.T
    normed, inverse = norm_parts(x_ref[...].astype(F32))
    sums_ref[0:1, :] += add_rows(d_h_one)
    sums_ref[1:2, :] += add_rows(d_h_one * normed)
    grad = (d_res_ref[...] + norm_back(normed, inverse, d_h_one * (1.0 + vectors_ref[1:2, :]))).astype(BF16)
    out_ref[...] = grad.reshape(out_ref.shape)


def input_grads(slot, slots, inputs, half, d_residual, vectors, packed, grads):
    rows, width = inputs.shape
    block = pick_block(rows, 256)
    first = half * (rows // block)
    row_spec = pl.BlockSpec((block, width), lambda i, *_: (i, 0))
    flat = [grad for kind in grads for grad in kind]
    out_spec, out_shape = row_spec, (rows, width)
    if slots:
        out_spec = pl.BlockSpec((1, block, width), lambda i, at: (at[0], i, 0))
        out_shape = (slots, rows, width)
    return pl.pallas_call(
        functools.partial(input_grads_kernel, [len(kind) for kind in grads]),
        grid_spec=pltpu.PrefetchScalarGridSpec(
            num_scalar_prefetch=1,
            grid=(rows // block,),
            in_specs=[
                row_spec,
                pl.BlockSpec((block, width), lambda i, *_: (i + first, 0)),
                whole_spec(vectors.shape),
                whole_spec((width, 3 * width)),
            ]
            + [pl.BlockSpec((grad.shape[0], block), lambda i, *_: (0, i + first)) for grad in flat],
            out_specs=[out_spec, whole_spec((8, width))],
        ),
        out_shape=[jax.ShapeDtypeStruct(out_shape, BF16), jax.ShapeDtypeStruct((8, width), F32)],
        compiler_params=pltpu.CompilerParams(vmem_limit_bytes=VMEM_LIMIT),
        cost_estimate=pl.CostEstimate(
            flops=6 * rows * width * width, bytes_accessed=14 * rows * width + 6 * width * width, transcendentals=0
        ),
        name="input_grads",
    )(slot, inputs, d_residual, vectors, packed, *flat)


def time_features(t_index, model_width):
    half_width = model_width // 2
    indices = jnp.arange(half_width).astype(F32)
    frequency = jnp.exp(indices * (-math.log(10000.0) / (half_width - 1)))
    angles = t_index.astype(F32)[:, None] * frequency[None, :]
    return jnp.concatenate([jnp.sin(angles), jnp.cos(angles)], axis=1)


def rotary_tables(places):
    inverse = jnp.exp(jnp.arange(HALF).astype(F32) * (-2.0 * math.log(10000.0) / HDIM))
    angles = inverse[:, None] * places.astype(F32)[None, :]
    return jnp.cos(angles), jnp.sin(angles)


def after(values, *others):
    return lax.optimization_barrier((values,) + others)[0]


def make_body(mesh):
    n_dp, n_fsdp = mesh.shape["dp"], mesh.shape["fsdp"]
    n_pairs = n_fsdp // 2

    def shift(values, axis, size, by):
        return lax.ppermute(values, axis, [(i, (i + by) % size) for i in range(size)])

    def pick(values, index, axis=0):
        return lax.dynamic_index_in_dim(values, index, axis, keepdims=False)

    def body(
        frames,
        lengths,
        t_index,
        w_ada,
        b_ada,
        w_query,
        b_query,
        w_key,
        b_key,
        w_value,
        b_value,
        w_out,
        b_out,
        w_up,
        b_up,
        w_down,
        b_down,
        grad_out,
    ):
        slots, local, width = frames.shape
        group = n_fsdp // slots
        hidden_width = w_up.shape[1]
        shard = w_query.shape[0]
        ada_width = w_ada.shape[1]
        dp, fsdp = lax.axis_index("dp"), lax.axis_index("fsdp")
        me = dp * n_fsdp + fsdp
        slot, place = fsdp // group, fsdp % group
        other = 1 - slot
        core, pair = fsdp % 2, fsdp // 2
        side, deep, far = dp % 2, dp // 2, n_dp // 2
        length = pick(lengths, slot)

        def picked(values):
            return pick(values, slot), pick(values, other)

        split = local % 128 == 0

        def swap_in(own, away):
            parts = own, shift(away, "fsdp", n_fsdp, group)
            return parts if split else (jnp.concatenate(parts),) * 2

        def swap_out(whole, away):
            arrived = shift(away, "fsdp", n_fsdp, group)
            return lax.dynamic_update_index_in_dim(whole, arrived, other, 0), arrived

        def placed_own(own):
            return lax.dynamic_update_index_in_dim(jnp.zeros((slots, local, width), own.dtype), own, slot, 0)

        def places_of(member):
            at = slot * group + member
            blocks = [((at - by * group) + n_fsdp) % n_fsdp for by in range(slots)]
            return jnp.concatenate([b * local + jnp.arange(local, dtype=jnp.int32) for b in blocks])

        ring = lambda by: [(i, (i // group) * group + (i % group + by) % group) for i in range(n_fsdp)]

        def swap(values, axis, size):
            return lax.ppermute(values, axis, [(i, i ^ 1) for i in range(size)])

        def sum_core(values):
            values = values.reshape(n_dp, n_pairs, 2, shard, values.shape[1])
            arrived = swap(pick(values, 1 - core, 2), "fsdp", n_fsdp)
            return pick(values, core, 2).astype(F32) + arrived.astype(F32)

        def sum_pairs(values):
            axis = values.ndim - 3
            total = pick(values, pair, axis).astype(F32)
            for by in range(1, n_pairs):
                arrived = shift(pick(values, (pair + by) % n_pairs, axis), "fsdp", n_fsdp, 2 * by)
                total = total + arrived.astype(F32)
            return total

        def sum_side(values):
            values = values.reshape((far, 2) + values.shape[1:])
            arrived = swap(pick(values, 1 - side, 1), "dp", n_dp)
            return pick(values, side, 1).astype(F32) + arrived.astype(F32)

        def sum_far(values):
            total = pick(values, deep).astype(F32)
            for by in range(1, far):
                arrived = shift(pick(values, (deep + by) % far), "dp", n_dp, 2 * by)
                total = total + arrived.astype(F32)
            return total

        def gather_dp(values):
            values = jnp.stack([values] + [shift(values, "dp", n_dp, 2 * by) for by in range(1, far)])
            return jnp.stack([values, swap(values, "dp", n_dp)])

        packed = lax.all_gather(jnp.concatenate([w_key, w_value, w_query], axis=1), AXES, axis=0, tiled=True)
        ups = hidden_width // width
        w_up_turned = w_up.reshape(shard, n_dp * n_fsdp, ups, shard).swapaxes(1, 2).reshape(w_up.shape)
        downs = [w_down[i * shard : (i + 1) * shard] for i in range(ups)]
        packed_two = lax.all_gather(jnp.concatenate([w_out, w_up_turned, *downs], axis=1), AXES, axis=0, tiled=True)

        inputs = swap_in(*picked(frames))
        rows = slots * local
        own_grad, away_grad = picked(grad_out)

        t_all = gather_dp(t_index).reshape(-1)
        active = jax.nn.silu(time_features(t_all, width)).astype(BF16)
        active_mine = lax.dynamic_slice_in_dim(active, me * shard, shard, axis=1)
        partial = [dot(active_mine, w_ada, 1, 0)]
        for bias in (b_query, b_key, b_value, b_out, b_down, *jnp.split(b_up, ups)):
            size = bias.shape[0]
            zeros = jnp.zeros((1, size * n_dp * n_fsdp), F32)
            placed = lax.dynamic_update_slice_in_dim(zeros, bias.astype(F32)[None], me * size, axis=1)
            partial.append(jnp.broadcast_to(placed, (n_dp * slots, placed.shape[1])))
        placed = lax.dynamic_update_slice_in_dim(
            jnp.zeros((1, ada_width), F32), b_ada.astype(F32)[None], me * b_ada.shape[0], axis=1
        )
        partial[0] = partial[0] + placed
        partial = jnp.concatenate(partial, axis=1).reshape(2, far, slots, -1)
        partial = partial[0] + swap(partial[1], "dp", n_dp)
        summed = partial[0]
        for by in range(1, far):
            summed = summed + shift(partial[by], "dp", n_dp, -2 * by)
        one = pick(summed, slot) + shift(pick(summed, other), "fsdp", n_fsdp, group)
        vectors = one
        for by in range(1, group):
            vectors = vectors + lax.ppermute(one, "fsdp", ring(by))
        vectors = vectors.reshape(-1, width)
        vectors = jnp.pad(vectors, ((0, -vectors.shape[0] % 8), (0, 0)))

        key_places = jnp.concatenate([places_of((place - by + group) % group) for by in range(group)])
        cosine, sine = rotary_tables(key_places)
        key_bias = jnp.where(key_places < length, 0.0, -1e30)
        bias_columns = jnp.pad(key_bias.astype(BF16)[:, None], ((0, 0), (0, HDIM - 1)))
        keep = (key_places[:rows] < length).astype(F32)[:, None]

        wide = 2
        vectors, cosine, sine, key_bias, bias_columns, keep, own_grad, away_grad = lax.optimization_barrier(
            (vectors, cosine, sine, key_bias, bias_columns, keep, own_grad, away_grad)
        )
        h_one, q_rot, keys, values = project(inputs, vectors, packed, cosine[:, :rows], sine[:, :rows], wide)
        cotangent = swap_in(own_grad, after(away_grad, keys[0]))
        heads = width // HDIM
        tall = heads // wide
        with_ring = lambda own: [own] + [lax.ppermute(own, "fsdp", ring(by)) for by in range(1, group)]
        k_parts, v_parts = [with_ring(own) for own in keys], [with_ring(own) for own in values]
        heads_out, lses = [], []
        for at in range(wide):
            out, lse = attend(q_rot, k_parts[at], v_parts[at], bias_columns, at * tall)
            heads_out.append(out)
            lses.append(lse)
        at_slot = slot.reshape(1).astype(jnp.int32)
        mixed, away_mixed, d_residual, d_heads, g_rows, sums_two = feed_forward(
            at_slot, inputs, heads_out, cotangent, keep, packed_two, vectors, slots
        )
        if not split:
            mixed, away_mixed = placed_own(mixed[:local]), mixed[local:]
        mixed, _ = swap_out(mixed, away_mixed)

        sum_rows = lax.psum_scatter(g_rows, AXES, scatter_dimension=0, tiled=True).astype(F32)
        g_out = sum_rows[:, :width]
        g_up = sum_rows[:, width : width + hidden_width].reshape(shard, ups, n_dp * n_fsdp, shard)
        g_up = g_up.swapaxes(1, 2).reshape(w_up.shape)
        g_down = jnp.concatenate([sum_rows[:, (1 + ups + i) * width : (2 + ups + i) * width] for i in range(ups)])

        grads, d_biases, moving = ([], [], []), [], []

        def start_sum(pieces, stages):
            dk, dv, weight_grad, bias_grad = weight_grads(h_one, pieces)
            grads[0].extend(piece[0] for piece in pieces)
            grads[1].append(dk)
            grads[2].append(dv)
            d_biases.append(bias_grad[:, :3])
            moving.append([list(stages), weight_grad])
            return weight_grad

        def move_on():
            for item in moving:
                if item[0]:
                    item[1] = item[0].pop(0)(item[1])
                    if item[0]:
                        item[1] = item[1].astype(BF16)
            return [item[1] for item in moving]

        first_pairs = (sum_core, sum_pairs, sum_side, sum_far)
        last_pairs = (sum_core, sum_side, sum_far, sum_pairs)
        counts = (4, 4, 2, 2, 2, 2)
        joined = (1, 1, 2, 2)
        steps = len(counts)
        waiting, ready, first, next_sum = [], d_heads, 0, 0
        for step, each in enumerate(counts):
            part, within = first // tall, first % tall
            dq, dk_parts, dv_parts = attend_back(
                q_rot,
                k_parts[part],
                v_parts[part],
                ready,
                heads_out[part],
                lses[part],
                key_bias[None],
                cosine,
                sine,
                first,
                within,
                each,
            )
            first += each
            done = move_on()
            if len(waiting) >= joined[next_sum]:
                done.append(start_sum(waiting[: joined[next_sum]], first_pairs))
                waiting = waiting[joined[next_sum] :]
                next_sum += 1
            dk_parts = [dk_parts[0]] + [lax.ppermute(dk_parts[by], "fsdp", ring(-by)) for by in range(1, group)]
            dv_parts = [dv_parts[0]] + [lax.ppermute(dv_parts[by], "fsdp", ring(-by)) for by in range(1, group)]
            waiting.append((dq, dk_parts, dv_parts))
            if step == steps - 2:
                done += [g_out, g_up, g_down]
            if done and step + 1 < steps:
                ready = after(d_heads, dq, *done)
        last = start_sum(waiting, last_pairs)
        if split:
            rest = after(d_residual, last)
            away_frames, sums_away = input_grads(at_slot, 0, inputs[1], 1, rest, vectors, packed, grads)
            rest, away_frames = lax.optimization_barrier((d_residual, away_frames, *move_on()))[:2]
            own_frames, sums_own = input_grads(at_slot, slots, inputs[0], 0, rest, vectors, packed, grads)
            sums_one = sums_own + sums_away
        else:
            both, sums_one = input_grads(at_slot, 0, inputs[0], 0, d_residual, vectors, packed, grads)
            own_frames, away_frames = placed_own(both[:local]), both[local:]
        grad_frames, arrived = swap_out(own_frames, away_frames)
        for _ in first_pairs:
            move_on()
        sums = [item[1] for item in moving]

        vector = jnp.concatenate(
            [sums_one[:2], sums_two[: 6 + ups], jnp.concatenate(d_biases).T]
        )
        for_slot = 6
        total = vector
        for by in range(1, group):
            total = total + lax.ppermute(vector, "fsdp", ring(by))
        packs = gather_dp(total).reshape(n_dp, -1, width)
        pack = jnp.concatenate([packs[:, :for_slot].reshape(-1, width), jnp.sum(packs[:, for_slot:], axis=0)])
        across = shift(after(pack, arrived), "fsdp", n_fsdp, group)
        count = n_dp * for_slot
        d_mod = jnp.stack([jnp.where(slot == s, pack[:count], across[:count]).reshape(n_dp, -1) for s in range(slots)], axis=1)
        d_mod = d_mod.reshape(n_dp * slots, for_slot * width)
        d_vectors = pack[count:] + across[count:]

        g_w_ada = lax.dot_general(
            active_mine.astype(F32),
            d_mod,
            (((0,), (0,)), ((), ())),
            precision=lax.Precision.HIGHEST,
            preferred_element_type=F32,
        )

        def mine(vector):
            vector = vector.reshape(-1)
            size = vector.shape[0] // (n_dp * n_fsdp)
            return lax.dynamic_slice_in_dim(vector, me * size, size)

        columns = [values.reshape(shard, 3, -1) for values in sums]
        g_qkv = [jnp.concatenate([values[:, i] for values in columns], axis=1) for i in range(3)]
        return (
            mixed,
            grad_frames,
            g_w_ada,
            mine(jnp.sum(d_mod, axis=0)),
            g_qkv[0],
            mine(d_vectors[2 + ups]),
            g_qkv[1],
            mine(d_vectors[3 + ups]),
            g_qkv[2],
            mine(d_vectors[4 + ups]),
            g_out,
            mine(d_vectors[0]),
            g_up,
            jnp.concatenate([mine(d_vectors[2 + i]) for i in range(ups)]),
            g_down,
            mine(d_vectors[1]),
        )

    return body


def solution(mesh):
    rows, vector, matrix = P("dp", "fsdp", None), P(AXES), P(AXES, None)
    return jax.shard_map(
        make_body(mesh),
        mesh=mesh,
        in_specs=(rows, P("dp"), P("dp")) + (matrix, vector) * 7 + (rows,),
        out_specs=(rows, rows) + (matrix, vector) * 7,
        check_vma=False,
    )
```

```python
import functools
import math

import jax
import jax.numpy as jnp
from jax import lax
from jax.experimental import pallas as pl
from jax.experimental.pallas import tpu as pltpu
from jax.sharding import PartitionSpec as P

HDIM = 64
HALF = HDIM // 2
SCALE = HDIM ** (-0.5)
SCALE2 = SCALE * math.log2(math.e)
AXES = ("dp", "fsdp")
VMEM_LIMIT = 62 << 20
F32 = jnp.float32
BF16 = jnp.bfloat16


def dot(left_side, right_side, left_dim, right_dim):
    return lax.dot_general(
        left_side,
        right_side,
        (((left_dim,), (right_dim,)), ((), ())),
        preferred_element_type=F32,
    )


def pick_block(total, wanted):
    block = min(total, wanted)
    while total % block:
        block -= 128
    return block


def attend_kernel(parts, chunk, *refs):
    q_ref, bias_ref = refs[0], refs[1]
    k_refs, v_refs = refs[2 : 2 + parts], refs[2 + parts : 2 + 2 * parts]
    o_ref, lse_ref, k_aug, v_aug, q_aug = refs[2 + 2 * parts :]
    head, block = pl.program_id(0), pl.program_id(1)
    span = k_aug.shape[0]
    part = span // parts
    q_rows = q_ref.shape[1]

    @pl.when((head == 0) & (block == 0))
    def _():
        k_aug[:, HDIM:] = bias_ref[...]
        v_aug[HDIM:, :] = jnp.ones((16, span), BF16)
        q_aug[HDIM:, :] = jnp.ones((HDIM, q_rows), BF16)

    @pl.when(block == 0)
    def _():
        for i in range(parts):
            k_aug[i * part : (i + 1) * part, :HDIM] = k_refs[i][...].T
            v_aug[:HDIM, i * part : (i + 1) * part] = v_refs[i][...]

    q_aug[:HDIM, :] = q_ref[...]
    queries = q_aug[...]
    count = span // chunk

    def scores(i):
        return dot(k_aug[i * chunk : (i + 1) * chunk, :], queries, 1, 0)

    upcoming = scores(0)
    row_max = total = None
    for i in range(count):
        current = upcoming
        if i + 1 < count:
            upcoming = scores(i + 1)
        chunk_max = jnp.max(current, axis=0, keepdims=True) * SCALE2
        new_max = chunk_max if i == 0 else jnp.maximum(row_max, chunk_max)
        weights = jnp.exp2(current * SCALE2 - new_max).astype(BF16)
        update = dot(v_aug[:, i * chunk : (i + 1) * chunk], weights, 1, 0)
        total = update if i == 0 else total * jnp.exp2(row_max - new_max) + update
        row_max = new_max
    denominator = total[HDIM : HDIM + 1, :]
    o_ref[...] = (total[:HDIM, :] / denominator).astype(BF16)
    lse_ref[...] = (row_max + jnp.log2(denominator))[None]


def attend(q_rot, k_parts, v_parts, bias_columns, first):
    width, rows = k_parts[0].shape
    parts = len(k_parts)
    span = parts * rows
    heads = width // HDIM
    q_rows = pick_block(rows, 768)
    chunk = pick_block(span, 512)
    q_spec = pl.BlockSpec((HDIM, q_rows), lambda h, j: (h + first, j))
    k_spec = pl.BlockSpec((HDIM, rows), lambda h, j: (h, 0))
    return pl.pallas_call(
        functools.partial(attend_kernel, parts, chunk),
        grid=(heads, rows // q_rows),
        in_specs=[q_spec, pl.BlockSpec((span, HDIM), lambda h, j: (0, 0))] + [k_spec] * (2 * parts),
        out_specs=[
            pl.BlockSpec((HDIM, q_rows), lambda h, j: (h, j)),
            pl.BlockSpec((1, 1, q_rows), lambda h, j: (h, 0, j)),
        ],
        out_shape=[
            jax.ShapeDtypeStruct((width, rows), BF16),
            jax.ShapeDtypeStruct((heads, 1, rows), F32),
        ],
        scratch_shapes=[
            pltpu.VMEM((span, 2 * HDIM), BF16),
            pltpu.VMEM((HDIM + 16, span), BF16),
            pltpu.VMEM((2 * HDIM, q_rows), BF16),
        ],
        compiler_params=pltpu.CompilerParams(vmem_limit_bytes=VMEM_LIMIT),
        cost_estimate=pl.CostEstimate(
            flops=16 * heads * rows * span * HDIM,
            bytes_accessed=2 * width * (2 * rows + 2 * span),
            transcendentals=heads * rows * span,
        ),
        name="attend",
    )(q_rot, bias_columns, *k_parts, *v_parts)


def in_three(values):
    first = values.astype(BF16)
    rest = values - first.astype(F32)
    second = rest.astype(BF16)
    return first.astype(F32), second.astype(F32), rest - second.astype(F32)


def unrotate(values, cosine, sine):
    low, high = values[:HALF], values[HALF:]
    return low * cosine + high * sine, high * cosine - low * sine


def attend_back_kernel(parts, chunk, *refs):
    q_ref, do_ref, o_ref, lse_ref, bias_ref, cos_ref, sin_ref = refs[:7]
    k_refs, v_refs = refs[7 : 7 + parts], refs[7 + parts : 7 + 2 * parts]
    dq_ref = refs[7 + 2 * parts]
    dk_refs = refs[8 + 2 * parts : 8 + 3 * parts]
    dv_refs = refs[8 + 3 * parts : 8 + 4 * parts]
    k_aug, v_aug, k_rows, q_aug, do_aug, dk_acc, dv_acc = refs[8 + 4 * parts :]
    head, block = pl.program_id(0), pl.program_id(1)
    span = k_aug.shape[1]
    part = span // parts
    q_rows = q_ref.shape[1]

    @pl.when((head == 0) & (block == 0))
    def _():
        row = lax.broadcasted_iota(jnp.int32, (HDIM, span), 0)
        ones = jnp.where(row < 4, 1.0, 0.0)
        k_aug[HDIM:, :] = jnp.where(row == 0, bias_ref[...], ones).astype(BF16)
        v_aug[HDIM:, :] = jnp.where(row < 3, 1.0, 0.0).astype(BF16)
        k_rows[:, HDIM:] = jnp.zeros((span, HDIM), BF16)

    @pl.when(block == 0)
    def _():
        for i in range(parts):
            at = slice(i * part, (i + 1) * part)
            keys = k_refs[i][...]
            k_aug[:HDIM, at] = keys
            v_aug[:HDIM, at] = v_refs[i][...]
            k_rows[at, :HDIM] = keys.T
        dk_acc[...] = jnp.zeros_like(dk_acc)
        dv_acc[...] = jnp.zeros_like(dv_acc)

    queries, d_heads = q_ref[...], do_ref[...]
    delta = jnp.sum(d_heads.astype(F32) * o_ref[...].astype(F32), axis=0, keepdims=True)
    row = lax.broadcasted_iota(jnp.int32, (HDIM, q_rows), 0)
    lse_a, lse_b, lse_c = in_three(lse_ref[0] * (-1.0 / SCALE2))
    del_a, del_b, del_c = in_three(-delta)
    q_extra = jnp.where(row == 2, lse_b, jnp.where(row == 3, lse_c, 0.0))
    q_extra = jnp.where(row == 0, 1.0, jnp.where(row == 1, lse_a, q_extra))
    do_extra = jnp.where(row == 1, del_b, jnp.where(row == 2, del_c, 0.0))
    do_extra = jnp.where(row == 0, del_a, do_extra)
    q_aug[:HDIM, :] = queries
    q_aug[HDIM:, :] = q_extra.astype(BF16)
    do_aug[:HDIM, :] = d_heads
    do_aug[HDIM:, :] = do_extra.astype(BF16)
    q_side, do_side = q_aug[...].T, do_aug[...].T
    count = span // chunk

    def products(i):
        at = slice(i * chunk, (i + 1) * chunk)
        return dot(q_side, k_aug[:, at], 1, 0), dot(do_side, v_aug[:, at], 1, 0)

    upcoming = products(0)
    d_query = None
    for i in range(count):
        at = slice(i * chunk, (i + 1) * chunk)
        scores, d_probs = upcoming
        if i + 1 < count:
            upcoming = products(i + 1)
        probs = jnp.exp2(scores * SCALE2)
        d_scores = (probs * d_probs).astype(BF16)
        dv_acc[:, at] += dot(d_heads, probs.astype(BF16), 1, 0)
        dk_acc[:, at] += dot(queries, d_scores, 1, 0)
        update = dot(d_scores, k_rows[at, :], 1, 0)
        d_query = update if i == 0 else d_query + update
    first = pl.multiple_of(block * q_rows, q_rows)
    low, high = unrotate(
        d_query.T[:HDIM, :] * SCALE, cos_ref[:, pl.ds(first, q_rows)], sin_ref[:, pl.ds(first, q_rows)]
    )
    dq_ref[:HALF, :] = low.astype(BF16)
    dq_ref[HALF:, :] = high.astype(BF16)

    @pl.when(block == pl.num_programs(1) - 1)
    def _():
        for i in range(parts):
            at = slice(i * part, (i + 1) * part)
            low, high = unrotate(dk_acc[:, at] * SCALE, cos_ref[:, at], sin_ref[:, at])
            dk_refs[i][:HALF, :] = low.astype(dk_refs[i].dtype)
            dk_refs[i][HALF:, :] = high.astype(dk_refs[i].dtype)
            dv_refs[i][...] = dv_acc[:, at].astype(dv_refs[i].dtype)


def attend_back(q_rot, k_parts, v_parts, d_heads, heads_out, lse, bias_row, cosine, sine, first, within, count):
    rows = q_rot.shape[1]
    parts = len(k_parts)
    span = parts * rows
    q_rows = pick_block(rows, 1536)
    chunk = pick_block(span, 256)
    q_spec = pl.BlockSpec((HDIM, q_rows), lambda h, j: (h + first, j))
    k_spec = pl.BlockSpec((HDIM, rows), lambda h, j: (h + within, 0))
    whole = lambda array: pl.BlockSpec(array.shape, lambda h, j: (0, 0))
    part_out = pl.BlockSpec((HDIM, rows), lambda h, j: (h, 0))
    shape = lambda kind: jax.ShapeDtypeStruct((count * HDIM, rows), kind)
    part_kinds = [F32] + [BF16] * (parts - 1)
    out = pl.pallas_call(
        functools.partial(attend_back_kernel, parts, chunk),
        grid=(count, rows // q_rows),
        in_specs=[
            q_spec,
            q_spec,
            pl.BlockSpec((HDIM, q_rows), lambda h, j: (h + within, j)),
            pl.BlockSpec((1, 1, q_rows), lambda h, j: (h + within, 0, j)),
            whole(bias_row),
            whole(cosine),
            whole(sine),
        ]
        + [k_spec] * (2 * parts),
        out_specs=[pl.BlockSpec((HDIM, q_rows), lambda h, j: (h, j))] + [part_out] * (2 * parts),
        out_shape=[shape(BF16)] + [shape(kind) for kind in part_kinds * 2],
        scratch_shapes=[
            pltpu.VMEM((2 * HDIM, span), BF16),
            pltpu.VMEM((2 * HDIM, span), BF16),
            pltpu.VMEM((span, 2 * HDIM), BF16),
            pltpu.VMEM((2 * HDIM, q_rows), BF16),
            pltpu.VMEM((2 * HDIM, q_rows), BF16),
            pltpu.VMEM((HDIM, span), F32),
            pltpu.VMEM((HDIM, span), F32),
        ],
        compiler_params=pltpu.CompilerParams(vmem_limit_bytes=VMEM_LIMIT),
        cost_estimate=pl.CostEstimate(
            flops=40 * count * rows * span * HDIM,
            bytes_accessed=2 * count * HDIM * (8 * rows + 4 * span),
            transcendentals=0,
        ),
        name="attend_back",
    )(q_rot, d_heads, heads_out, lse, bias_row, cosine, sine, *k_parts, *v_parts)
    return out[0], out[1 : 1 + parts], out[1 + parts :]


def norm_parts(values):
    centered = values - jnp.mean(values, axis=-1, keepdims=True)
    scale = lax.rsqrt(jnp.mean(centered * centered, axis=-1, keepdims=True) + 1e-06)
    return centered * scale, scale


def norm_back(normed, scale, d_normed):
    return (
        d_normed
        - jnp.mean(d_normed, axis=-1, keepdims=True)
        - normed * jnp.mean(d_normed * normed, axis=-1, keepdims=True)
    ) * scale


def gelu_both(values):
    square = values * values
    bend = jnp.tanh(0.7978845608028654 * (values + 0.044715 * values * square))
    half = 0.5 * (1.0 + bend)
    slope = 0.7978845608028654 * (1.0 + 3 * 0.044715 * square)
    return values * half, half + 0.5 * values * (1.0 - bend * bend) * slope


def add_rows(values):
    return jnp.sum(values, axis=0, keepdims=True)


def store_rotated(out_ref, values, cosine, sine):
    for at in range(0, out_ref.shape[0], HDIM):
        low, high = values[at : at + HALF], values[at + HALF : at + HDIM]
        out_ref[at : at + HALF, :] = (low * cosine - high * sine).astype(BF16)
        out_ref[at + HALF : at + HDIM, :] = (high * cosine + low * sine).astype(BF16)


def either(first_ref, second_ref):
    half = pl.num_programs(0) // 2
    return jnp.where(pl.program_id(0) < half, first_ref[...], second_ref[...])


def halves_spec(inputs, rows, block, width):
    if inputs[0].shape[0] == rows:
        return [pl.BlockSpec((block, width), lambda i, *_: (i, 0))] * 2
    half = rows // 2 // block
    return [
        pl.BlockSpec((block, width), lambda i, *_: (jnp.minimum(i, half - 1), 0)),
        pl.BlockSpec((block, width), lambda i, *_: (jnp.maximum(i - half, 0), 0)),
    ]


def project_kv_kernel(groups, x_ref, y_ref, vectors_ref, w_ref, cos_ref, sin_ref, h_ref, *refs):
    k_refs, v_refs = refs[:groups], refs[groups:]
    width = x_ref.shape[1]
    tall = width // groups
    normed, _ = norm_parts(either(x_ref, y_ref).astype(F32))
    h_one = (normed * (1.0 + vectors_ref[1:2, :]) + vectors_ref[0:1, :]).astype(BF16)
    h_ref[...] = h_one
    keys = (dot(h_one, w_ref[:, :width], 1, 0) + vectors_ref[7:8, :]).T
    values = (dot(h_one, w_ref[:, width:], 1, 0) + vectors_ref[8:9, :]).astype(BF16).T
    for i in range(groups):
        store_rotated(k_refs[i], keys[i * tall : (i + 1) * tall], cos_ref[...], sin_ref[...])
        v_refs[i][...] = values[i * tall : (i + 1) * tall]


def project_q_kernel(h_ref, vectors_ref, w_ref, cos_ref, sin_ref, q_ref):
    queries = dot(h_ref[...], w_ref[...], 1, 0) + vectors_ref[6:7, :]
    store_rotated(q_ref, queries.T, cos_ref[...], sin_ref[...])


def whole_spec(shape, column=0):
    return pl.BlockSpec(shape, lambda i, *_: (0, column), pipeline_mode=pl.Buffered(1))


def project(inputs, vectors, packed, cosine, sine, groups):
    width, rows = inputs[0].shape[1], cosine.shape[1]
    block = pick_block(inputs[0].shape[0], 256)
    tall = width // groups
    row_spec = pl.BlockSpec((block, width), lambda i: (i, 0))
    turned_spec = lambda height: pl.BlockSpec((height, block), lambda i: (0, i))
    turned = lambda height: jax.ShapeDtypeStruct((height, rows), BF16)
    table_spec = turned_spec(HALF)
    params = pltpu.CompilerParams(vmem_limit_bytes=VMEM_LIMIT)
    out = pl.pallas_call(
        functools.partial(project_kv_kernel, groups),
        grid=(rows // block,),
        in_specs=halves_spec(inputs, rows, block, width)
        + [whole_spec(vectors.shape), whole_spec((width, 2 * width)), table_spec, table_spec],
        out_specs=[row_spec] + [turned_spec(tall)] * (2 * groups),
        out_shape=[jax.ShapeDtypeStruct((rows, width), BF16)] + [turned(tall)] * (2 * groups),
        compiler_params=params,
        cost_estimate=pl.CostEstimate(
            flops=8 * rows * width * width, bytes_accessed=8 * rows * width + 4 * width * width, transcendentals=0
        ),
        name="project_kv",
    )(*inputs, vectors, packed, cosine, sine)
    h_one, keys, values = out[0], out[1 : 1 + groups], out[1 + groups :]
    queries = pl.pallas_call(
        project_q_kernel,
        grid=(rows // block,),
        in_specs=[row_spec, whole_spec(vectors.shape), whole_spec((width, width), 2), table_spec, table_spec],
        out_specs=turned_spec(width),
        out_shape=turned(width),
        compiler_params=params,
        cost_estimate=pl.CostEstimate(
            flops=4 * rows * width * width, bytes_accessed=4 * rows * width + 2 * width * width, transcendentals=0
        ),
        name="project_q",
    )(h_one, vectors, packed, cosine, sine)
    return h_one, queries, keys, values


def feed_forward_kernel(parts, pieces, split, slot_ref, *refs):
    o_refs = refs[:parts]
    x_ref, y_ref, cot_ref, cot_y_ref, keep_ref, w_ref, vectors_ref = refs[parts : parts + 7]
    own_ref, away_ref, d_res_ref, d_heads_ref, g_rows_ref, sums_ref = refs[parts + 7 : parts + 13]
    acc, acc_rows, slope_ref, hidden_ref, staged, sems = refs[parts + 13 :]
    step, count = pl.program_id(0), pl.num_programs(0)
    width = x_ref.shape[1]

    @pl.when(step == 0)
    def _():
        acc[...] = jnp.zeros_like(acc)
        acc_rows[...] = jnp.zeros_like(acc_rows)

    gate_one, shift_two, scale_two, gate_two, b_out, b_down = [vectors_ref[i : i + 1, :] for i in (2, 3, 4, 5, 9, 10)]
    out_at = slice(0, width)
    up_at = [slice((1 + i) * width, (2 + i) * width) for i in range(pieces)]
    down_at = [slice((1 + pieces + i) * width, (2 + pieces + i) * width) for i in range(pieces)]
    keep = keep_ref[...]
    heads_out = jnp.concatenate([ref[...] for ref in o_refs], axis=0)
    branch = (dot(heads_out, w_ref[:, out_at], 0, 0) + b_out) * keep
    residual = either(x_ref, y_ref).astype(F32) + gate_one * branch
    normed, inverse = norm_parts(residual)
    h_two = (normed * (1.0 + scale_two) + shift_two).astype(BF16)
    ff_out = b_down
    for i in range(pieces):
        value, slope = gelu_both(dot(h_two, w_ref[:, up_at[i]], 1, 0) + vectors_ref[11 + i : 12 + i, :])
        slope_ref[i] = slope
        hidden = value.astype(BF16)
        hidden_ref[i] = hidden
        ff_out = ff_out + dot(hidden, w_ref[:, down_at[i]], 1, 0)
    mixed = (residual + gate_two * ff_out).astype(BF16)
    if split:

        @pl.when(step < count // 2)
        def _():
            own_ref[0] = mixed

        @pl.when(step >= count // 2)
        def _():
            away_ref[...] = mixed
    else:
        own_ref[...] = mixed
    d_mixed = either(cot_ref, cot_y_ref).astype(F32)
    acc_rows[3:4, :] += add_rows(d_mixed * ff_out)
    d_ff = (d_mixed * gate_two).astype(BF16)
    acc_rows[5:6, :] += add_rows(d_ff.astype(F32))
    d_h_two = None
    for i in range(pieces):
        acc[:, down_at[i]] += dot(hidden_ref[i], d_ff, 0, 0)
        d_up = (dot(d_ff, w_ref[:, down_at[i]], 1, 1) * slope_ref[i]).astype(BF16)
        acc_rows[6 + i : 7 + i, :] += add_rows(d_up.astype(F32))
        acc[:, up_at[i]] += dot(h_two, d_up, 0, 0)
        update = dot(d_up, w_ref[:, up_at[i]], 1, 1)
        d_h_two = update if i == 0 else d_h_two + update
    acc_rows[1:2, :] += add_rows(d_h_two)
    acc_rows[2:3, :] += add_rows(d_h_two * normed)
    d_residual = d_mixed + norm_back(normed, inverse, d_h_two * (1.0 + scale_two))
    d_res_ref[...] = d_residual
    acc_rows[0:1, :] += add_rows(d_residual * branch)
    d_branch = (d_residual * gate_one * keep).astype(BF16)
    acc_rows[4:5, :] += add_rows(d_branch.astype(F32))
    acc[:, out_at] += dot(heads_out, d_branch, 1, 0)
    d_heads_ref[...] = dot(w_ref[:, out_at], d_branch, 1, 1).astype(BF16)

    @pl.when(step == count - 1)
    def _():
        sums_ref[...] = acc_rows[...]
        tall = staged.shape[1]
        copies = []
        for i in range(width // tall):
            slot = i % 2
            if i >= 2:
                copies[i - 2].wait()
            staged[slot] = acc[i * tall : (i + 1) * tall, :].astype(BF16)
            copies.append(pltpu.make_async_copy(staged.at[slot], g_rows_ref.at[pl.ds(i * tall, tall), :], sems.at[slot]))
            copies[i].start()
        for copy in copies[-2:]:
            copy.wait()


def feed_forward(slot, inputs, heads_out, cotangent, keep, packed, vectors, slots):
    rows, width = heads_out[0].shape[1], inputs[0].shape[1]
    pieces = (packed.shape[1] // width - 1) // 2
    block = pick_block(inputs[0].shape[0], 256)
    local = rows // slots
    split = inputs[0].shape[0] == local
    half = local // block
    row_spec = pl.BlockSpec((block, width), lambda i, *_: (i, 0))
    turned_spec = lambda height: pl.BlockSpec((height, block), lambda i, *_: (0, i))
    kinds = jax.ShapeDtypeStruct
    if split:
        mixed_specs = [
            pl.BlockSpec((1, block, width), lambda i, at: (at[0], jnp.minimum(i, half - 1), 0)),
            pl.BlockSpec((block, width), lambda i, *_: (jnp.maximum(i - half, 0), 0)),
        ]
        mixed_shapes = [kinds((slots, local, width), BF16), kinds((local, width), BF16)]
    else:
        mixed_specs = [row_spec, whole_spec((8, 128))]
        mixed_shapes = [kinds((rows, width), BF16), kinds((8, 128), BF16)]
    return pl.pallas_call(
        functools.partial(feed_forward_kernel, len(heads_out), pieces, split),
        grid_spec=pltpu.PrefetchScalarGridSpec(
            num_scalar_prefetch=1,
            grid=(rows // block,),
            in_specs=[turned_spec(part.shape[0]) for part in heads_out]
            + halves_spec(inputs, rows, block, width) * 2
            + [
                pl.BlockSpec((block, 1), lambda i, *_: (i, 0)),
                whole_spec(packed.shape),
                whole_spec(vectors.shape),
            ],
            out_specs=mixed_specs
            + [
                row_spec,
                turned_spec(width),
                pl.BlockSpec(memory_space=pl.ANY),
                whole_spec((8, width)),
            ],
            scratch_shapes=[
                pltpu.VMEM(packed.shape, F32),
                pltpu.VMEM((8, width), F32),
                pltpu.VMEM((pieces, block, width), F32),
                pltpu.VMEM((pieces, block, width), BF16),
                pltpu.VMEM((2, pick_block(width, 256), packed.shape[1]), BF16),
                pltpu.SemaphoreType.DMA((2,)),
            ],
        ),
        out_shape=mixed_shapes
        + [
            kinds((rows, width), F32),
            kinds((width, rows), BF16),
            kinds(packed.shape, BF16),
            kinds((8, width), F32),
        ],
        compiler_params=pltpu.CompilerParams(vmem_limit_bytes=VMEM_LIMIT),
        cost_estimate=pl.CostEstimate(
            flops=6 * rows * width * packed.shape[1],
            bytes_accessed=8 * rows * width + 4 * width * packed.shape[1],
            transcendentals=0,
        ),
        name="feed_forward",
    )(slot, *heads_out, *inputs, *cotangent, keep, packed, vectors)


def weight_grads_kernel(parts, h_ref, dq_ref, *refs):
    dk_refs, dv_refs = refs[:parts], refs[parts : 2 * parts]
    dk_out, dv_out, weight_ref, bias_ref = refs[2 * parts :]

    def summed(pieces):
        total = pieces[0][...]
        for ref in pieces[1:]:
            total = total + ref[...].astype(F32)
        return total.astype(BF16)

    grads = [dq_ref[...], summed(dk_refs), summed(dv_refs)]
    dk_out[...] = grads[1]
    dv_out[...] = grads[2]
    weight_ref[...] = dot(jnp.concatenate(grads, axis=0), h_ref[...], 1, 0).T.astype(BF16)
    for i, grad in enumerate(grads):
        bias_ref[:, i : i + 1] = jnp.sum(grad.astype(F32), axis=1, keepdims=True)


def weight_grads(h_one, d_query, dk_parts, dv_parts):
    rows, width = h_one.shape
    tall = d_query.shape[0]
    block = pick_block(tall, 128)
    spec = pl.BlockSpec((block, rows), lambda i: (i, 0))
    kinds = jax.ShapeDtypeStruct
    parts = len(dk_parts)
    return pl.pallas_call(
        functools.partial(weight_grads_kernel, parts),
        grid=(tall // block,),
        in_specs=[whole_spec((rows, width))] + [spec] * (1 + 2 * parts),
        out_specs=[
            spec,
            spec,
            pl.BlockSpec((width, 3 * block), lambda i: (0, i)),
            pl.BlockSpec((block, 128), lambda i: (i, 0)),
        ],
        out_shape=[
            kinds((tall, rows), BF16),
            kinds((tall, rows), BF16),
            kinds((width, 3 * tall), BF16),
            kinds((tall, 128), F32),
        ],
        compiler_params=pltpu.CompilerParams(vmem_limit_bytes=VMEM_LIMIT),
        cost_estimate=pl.CostEstimate(flops=0, bytes_accessed=0, transcendentals=0),
        name="weight_grads",
    )(h_one, d_query, *dk_parts, *dv_parts)


def input_grads_kernel(counts, slot_ref, x_ref, d_res_ref, vectors_ref, w_ref, *refs):
    grad_refs, (out_ref, sums_ref) = refs[:-2], refs[-2:]
    width = x_ref.shape[1]

    @pl.when(pl.program_id(0) == 0)
    def _():
        sums_ref[...] = jnp.zeros_like(sums_ref)

    turned = None
    used = 0
    for kind in range(3):
        first = (2, 0, 1)[kind] * width
        grad = jnp.concatenate([ref[...] for ref in grad_refs[used : used + counts[kind]]], axis=0)
        used += counts[kind]
        update = dot(w_ref[:, first : first + width], grad, 1, 0)
        turned = update if turned is None else turned + update
    d_h_one = turned.T
    normed, inverse = norm_parts(x_ref[...].astype(F32))
    sums_ref[0:1, :] += add_rows(d_h_one)
    sums_ref[1:2, :] += add_rows(d_h_one * normed)
    grad = (d_res_ref[...] + norm_back(normed, inverse, d_h_one * (1.0 + vectors_ref[1:2, :]))).astype(BF16)
    out_ref[...] = grad.reshape(out_ref.shape)


def input_grads(slot, slots, inputs, half, d_residual, vectors, packed, grads):
    rows, width = inputs.shape
    block = pick_block(rows, 256)
    first = half * (rows // block)
    row_spec = pl.BlockSpec((block, width), lambda i, *_: (i, 0))
    flat = [grad for kind in grads for grad in kind]
    out_spec, out_shape = row_spec, (rows, width)
    if slots:
        out_spec = pl.BlockSpec((1, block, width), lambda i, at: (at[0], i, 0))
        out_shape = (slots, rows, width)
    return pl.pallas_call(
        functools.partial(input_grads_kernel, [len(kind) for kind in grads]),
        grid_spec=pltpu.PrefetchScalarGridSpec(
            num_scalar_prefetch=1,
            grid=(rows // block,),
            in_specs=[
                row_spec,
                pl.BlockSpec((block, width), lambda i, *_: (i + first, 0)),
                whole_spec(vectors.shape),
                whole_spec((width, 3 * width)),
            ]
            + [pl.BlockSpec((grad.shape[0], block), lambda i, *_: (0, i + first)) for grad in flat],
            out_specs=[out_spec, whole_spec((8, width))],
        ),
        out_shape=[jax.ShapeDtypeStruct(out_shape, BF16), jax.ShapeDtypeStruct((8, width), F32)],
        compiler_params=pltpu.CompilerParams(vmem_limit_bytes=VMEM_LIMIT),
        cost_estimate=pl.CostEstimate(flops=0, bytes_accessed=0, transcendentals=0),
        name="input_grads",
    )(slot, inputs, d_residual, vectors, packed, *flat)


def time_features(t_index, model_width):
    half_width = model_width // 2
    indices = jnp.arange(half_width).astype(F32)
    frequency = jnp.exp(indices * (-math.log(10000.0) / (half_width - 1)))
    angles = t_index.astype(F32)[:, None] * frequency[None, :]
    return jnp.concatenate([jnp.sin(angles), jnp.cos(angles)], axis=1)


def rotary_tables(places):
    inverse = jnp.exp(jnp.arange(HALF).astype(F32) * (-2.0 * math.log(10000.0) / HDIM))
    angles = inverse[:, None] * places.astype(F32)[None, :]
    return jnp.cos(angles), jnp.sin(angles)


def after(values, *others):
    return lax.optimization_barrier((values,) + others)[0]


def make_body(mesh):
    n_dp, n_fsdp = mesh.shape["dp"], mesh.shape["fsdp"]
    n_pairs = n_fsdp // 2

    def shift(values, axis, size, by):
        return lax.ppermute(values, axis, [(i, (i + by) % size) for i in range(size)])

    def pick(values, index, axis=0):
        return lax.dynamic_index_in_dim(values, index, axis, keepdims=False)

    def body(
        frames,
        lengths,
        t_index,
        w_ada,
        b_ada,
        w_query,
        b_query,
        w_key,
        b_key,
        w_value,
        b_value,
        w_out,
        b_out,
        w_up,
        b_up,
        w_down,
        b_down,
        grad_out,
    ):
        slots, local, width = frames.shape
        group = n_fsdp // slots
        hidden_width = w_up.shape[1]
        shard = w_query.shape[0]
        ada_width = w_ada.shape[1]
        dp, fsdp = lax.axis_index("dp"), lax.axis_index("fsdp")
        me = dp * n_fsdp + fsdp
        slot, place = fsdp // group, fsdp % group
        other = 1 - slot
        core, pair = fsdp % 2, fsdp // 2
        side, deep, far = dp % 2, dp // 2, n_dp // 2
        length = pick(lengths, slot)

        def picked(values):
            return pick(values, slot), pick(values, other)

        split = local % 128 == 0

        def swap_in(own, away):
            parts = own, shift(away, "fsdp", n_fsdp, group)
            return parts if split else (jnp.concatenate(parts),) * 2

        def swap_out(whole, away):
            arrived = shift(away, "fsdp", n_fsdp, group)
            return lax.dynamic_update_index_in_dim(whole, arrived, other, 0), arrived

        def placed_own(own):
            return lax.dynamic_update_index_in_dim(jnp.zeros((slots, local, width), own.dtype), own, slot, 0)

        def places_of(member):
            at = slot * group + member
            blocks = [((at - by * group) + n_fsdp) % n_fsdp for by in range(slots)]
            return jnp.concatenate([b * local + jnp.arange(local, dtype=jnp.int32) for b in blocks])

        ring = lambda by: [(i, (i // group) * group + (i % group + by) % group) for i in range(n_fsdp)]

        def swap(values, axis, size):
            return lax.ppermute(values, axis, [(i, i ^ 1) for i in range(size)])

        def sum_core(values):
            values = values.reshape(n_dp, n_pairs, 2, shard, values.shape[1])
            arrived = swap(pick(values, 1 - core, 2), "fsdp", n_fsdp)
            return pick(values, core, 2).astype(F32) + arrived.astype(F32)

        def sum_pairs(values):
            axis = values.ndim - 3
            total = pick(values, pair, axis).astype(F32)
            for by in range(1, n_pairs):
                arrived = shift(pick(values, (pair + by) % n_pairs, axis), "fsdp", n_fsdp, 2 * by)
                total = total + arrived.astype(F32)
            return total

        def sum_side(values):
            values = values.reshape((far, 2) + values.shape[1:])
            arrived = swap(pick(values, 1 - side, 1), "dp", n_dp)
            return pick(values, side, 1).astype(F32) + arrived.astype(F32)

        def sum_far(values):
            total = pick(values, deep).astype(F32)
            for by in range(1, far):
                arrived = shift(pick(values, (deep + by) % far), "dp", n_dp, 2 * by)
                total = total + arrived.astype(F32)
            return total

        def gather_dp(values):
            values = jnp.stack([values] + [shift(values, "dp", n_dp, 2 * by) for by in range(1, far)])
            return jnp.stack([values, swap(values, "dp", n_dp)])

        packed = lax.all_gather(jnp.concatenate([w_key, w_value, w_query], axis=1), AXES, axis=0, tiled=True)
        ups = hidden_width // width
        w_up_turned = w_up.reshape(shard, n_dp * n_fsdp, ups, shard).swapaxes(1, 2).reshape(w_up.shape)
        downs = [w_down[i * shard : (i + 1) * shard] for i in range(ups)]
        packed_two = lax.all_gather(jnp.concatenate([w_out, w_up_turned, *downs], axis=1), AXES, axis=0, tiled=True)

        inputs = swap_in(*picked(frames))
        rows = slots * local
        own_grad, away_grad = picked(grad_out)

        t_all = gather_dp(t_index).reshape(-1)
        active = jax.nn.silu(time_features(t_all, width)).astype(BF16)
        active_mine = lax.dynamic_slice_in_dim(active, me * shard, shard, axis=1)
        partial = [dot(active_mine, w_ada, 1, 0)]
        for bias in (b_query, b_key, b_value, b_out, b_down, *jnp.split(b_up, ups)):
            size = bias.shape[0]
            zeros = jnp.zeros((1, size * n_dp * n_fsdp), F32)
            placed = lax.dynamic_update_slice_in_dim(zeros, bias.astype(F32)[None], me * size, axis=1)
            partial.append(jnp.broadcast_to(placed, (n_dp * slots, placed.shape[1])))
        placed = lax.dynamic_update_slice_in_dim(
            jnp.zeros((1, ada_width), F32), b_ada.astype(F32)[None], me * b_ada.shape[0], axis=1
        )
        partial[0] = partial[0] + placed
        partial = jnp.concatenate(partial, axis=1).reshape(2, far, slots, -1)
        partial = partial[0] + swap(partial[1], "dp", n_dp)
        summed = partial[0]
        for by in range(1, far):
            summed = summed + shift(partial[by], "dp", n_dp, -2 * by)
        one = pick(summed, slot) + shift(pick(summed, other), "fsdp", n_fsdp, group)
        vectors = one
        for by in range(1, group):
            vectors = vectors + lax.ppermute(one, "fsdp", ring(by))
        vectors = vectors.reshape(-1, width)
        vectors = jnp.pad(vectors, ((0, -vectors.shape[0] % 8), (0, 0)))

        key_places = jnp.concatenate([places_of((place - by + group) % group) for by in range(group)])
        cosine, sine = rotary_tables(key_places)
        key_bias = jnp.where(key_places < length, 0.0, -1e30)
        bias_columns = jnp.pad(key_bias.astype(BF16)[:, None], ((0, 0), (0, HDIM - 1)))
        keep = (key_places[:rows] < length).astype(F32)[:, None]

        wide = 2
        vectors, cosine, sine, key_bias, bias_columns, keep, own_grad, away_grad = lax.optimization_barrier(
            (vectors, cosine, sine, key_bias, bias_columns, keep, own_grad, away_grad)
        )
        h_one, q_rot, keys, values = project(inputs, vectors, packed, cosine[:, :rows], sine[:, :rows], wide)
        cotangent = swap_in(own_grad, after(away_grad, keys[0]))
        heads = width // HDIM
        tall = heads // wide
        with_ring = lambda own: [own] + [lax.ppermute(own, "fsdp", ring(by)) for by in range(1, group)]
        k_parts, v_parts = [with_ring(own) for own in keys], [with_ring(own) for own in values]
        heads_out, lses = [], []
        for at in range(wide):
            out, lse = attend(q_rot, k_parts[at], v_parts[at], bias_columns, at * tall)
            heads_out.append(out)
            lses.append(lse)
        at_slot = slot.reshape(1).astype(jnp.int32)
        mixed, away_mixed, d_residual, d_heads, g_rows, sums_two = feed_forward(
            at_slot, inputs, heads_out, cotangent, keep, packed_two, vectors, slots
        )
        if not split:
            mixed, away_mixed = placed_own(mixed[:local]), mixed[local:]
        mixed, _ = swap_out(mixed, away_mixed)

        sum_rows = lax.psum_scatter(g_rows, AXES, scatter_dimension=0, tiled=True).astype(F32)
        g_out = sum_rows[:, :width]
        g_up = sum_rows[:, width : width + hidden_width].reshape(shard, ups, n_dp * n_fsdp, shard)
        g_up = g_up.swapaxes(1, 2).reshape(w_up.shape)
        g_down = jnp.concatenate([sum_rows[:, (1 + ups + i) * width : (2 + ups + i) * width] for i in range(ups)])

        grads, d_biases, weight_sums = ([], [], []), [], []

        def sum_parts(dq, dk_parts, dv_parts):
            dk, dv, weight_grad, bias_grad = weight_grads(h_one, dq, dk_parts, dv_parts)
            for kind, grad in zip(grads, (dq, dk, dv)):
                kind.append(grad)
            d_biases.append(bias_grad[:, :3])
            return weight_grad

        counts = (tall, tall // 2, tall // 2)
        first, ready, arrived = 0, d_heads, []
        for step, each in enumerate(counts):
            part, within = first // tall, first % tall
            dq, dk_parts, dv_parts = attend_back(
                q_rot,
                k_parts[part],
                v_parts[part],
                ready,
                heads_out[part],
                lses[part],
                key_bias[None],
                cosine,
                sine,
                first,
                within,
                each,
            )
            first += each
            dk_parts = [dk_parts[0]] + [lax.ppermute(dk_parts[by], "fsdp", ring(-by)) for by in range(1, group)]
            dv_parts = [dv_parts[0]] + [lax.ppermute(dv_parts[by], "fsdp", ring(-by)) for by in range(1, group)]
            arrived.append((dq, dk_parts, dv_parts))
            if step == 1:
                arrived[0][1][0] = after(arrived[0][1][0], dq)
                weight_sums.append(sum_parts(*arrived[0]))
                ready = after(d_heads, dq, weight_sums[0])
        early_sum = lax.psum_scatter(weight_sums[0], AXES, scatter_dimension=0, tiled=True).astype(F32)
        weight_sums.append(sum_parts(*arrived[1]))
        halves = [sum_core(weight_sums[1])]
        arrived[2][1][0] = after(arrived[2][1][0], weight_sums[1])
        weight_sums.append(sum_parts(*arrived[2]))
        halves.append(sum_core(weight_sums[2]))
        if split:
            rest = after(d_residual, weight_sums[2])
            away_frames, sums_away = input_grads(at_slot, 0, inputs[1], 1, rest, vectors, packed, grads)
            core_sums = jnp.concatenate(halves, axis=-1).astype(BF16)
            rest, away_frames, core_sums = lax.optimization_barrier((d_residual, away_frames, core_sums))
            own_frames, sums_own = input_grads(at_slot, slots, inputs[0], 0, rest, vectors, packed, grads)
            sums_one = sums_own + sums_away
        else:
            core_sums = jnp.concatenate(halves, axis=-1).astype(BF16)
            both, sums_one = input_grads(at_slot, 0, inputs[0], 0, d_residual, vectors, packed, grads)
            own_frames, away_frames = placed_own(both[:local]), both[local:]
        grad_frames, frames_arrived = swap_out(own_frames, away_frames)
        side_sums = sum_side(core_sums).astype(BF16)
        late_sum = sum_pairs(sum_far(side_sums).astype(BF16))
        sums = [early_sum, late_sum]

        vector = jnp.concatenate(
            [sums_one[:2], sums_two[: 6 + ups], jnp.concatenate(d_biases).T]
        )
        for_slot = 6
        total = vector
        for by in range(1, group):
            total = total + lax.ppermute(vector, "fsdp", ring(by))
        packs = gather_dp(total).reshape(n_dp, -1, width)
        pack = jnp.concatenate([packs[:, :for_slot].reshape(-1, width), jnp.sum(packs[:, for_slot:], axis=0)])
        pack, g_out, g_up, g_down, _ = lax.optimization_barrier((pack, g_out, g_up, g_down, frames_arrived))
        across = shift(pack, "fsdp", n_fsdp, group)
        count = n_dp * for_slot
        d_mod = jnp.stack([jnp.where(slot == s, pack[:count], across[:count]).reshape(n_dp, -1) for s in range(slots)], axis=1)
        d_mod = d_mod.reshape(n_dp * slots, for_slot * width)
        d_vectors = pack[count:] + across[count:]

        g_w_ada = lax.dot_general(
            active_mine.astype(F32),
            d_mod,
            (((0,), (0,)), ((), ())),
            precision=lax.Precision.HIGHEST,
            preferred_element_type=F32,
        )

        def mine(vector):
            vector = vector.reshape(-1)
            size = vector.shape[0] // (n_dp * n_fsdp)
            return lax.dynamic_slice_in_dim(vector, me * size, size)

        columns = jnp.concatenate(sums, axis=1).reshape(shard, -1, 3, pick_block(tall // 2 * HDIM, 128))
        g_qkv = [columns[:, :, i].reshape(shard, width) for i in range(3)]
        return (
            mixed,
            grad_frames,
            g_w_ada,
            mine(jnp.sum(d_mod, axis=0)),
            g_qkv[0],
            mine(d_vectors[2 + ups]),
            g_qkv[1],
            mine(d_vectors[3 + ups]),
            g_qkv[2],
            mine(d_vectors[4 + ups]),
            g_out,
            mine(d_vectors[0]),
            g_up,
            jnp.concatenate([mine(d_vectors[2 + i]) for i in range(ups)]),
            g_down,
            mine(d_vectors[1]),
        )

    return body


def solution(mesh):
    rows, vector, matrix = P("dp", "fsdp", None), P(AXES), P(AXES, None)
    return jax.shard_map(
        make_body(mesh),
        mesh=mesh,
        in_specs=(rows, P("dp"), P("dp")) + (matrix, vector) * 7 + (rows,),
        out_specs=(rows, rows) + (matrix, vector) * 7,
        check_vma=False,
    )
```

```python
import functools
import math

import jax
import jax.numpy as jnp
from jax import lax
from jax.experimental import pallas as pl
from jax.experimental.pallas import tpu as pltpu
from jax.sharding import PartitionSpec as P

HDIM = 64
HALF = HDIM // 2
SCALE = HDIM ** (-0.5)
SCALE2 = SCALE * math.log2(math.e)
AXES = ("dp", "fsdp")
VMEM_LIMIT = 62 << 20
F32 = jnp.float32
BF16 = jnp.bfloat16


def dot(left_side, right_side, left_dim, right_dim):
    return lax.dot_general(
        left_side,
        right_side,
        (((left_dim,), (right_dim,)), ((), ())),
        preferred_element_type=F32,
    )


def pick_block(total, wanted):
    block = min(total, wanted)
    while total % block:
        block -= 128
    return block


def attend_kernel(parts, chunk, *refs):
    q_ref, bias_ref = refs[0], refs[1]
    k_refs, v_refs = refs[2 : 2 + parts], refs[2 + parts : 2 + 2 * parts]
    o_ref, lse_ref, k_aug, v_aug, q_aug = refs[2 + 2 * parts :]
    head, block = pl.program_id(0), pl.program_id(1)
    span = k_aug.shape[0]
    part = span // parts
    q_rows = q_ref.shape[1]

    @pl.when((head == 0) & (block == 0))
    def _():
        k_aug[:, HDIM:] = bias_ref[...]
        v_aug[HDIM:, :] = jnp.ones((16, span), BF16)
        q_aug[HDIM:, :] = jnp.ones((HDIM, q_rows), BF16)

    @pl.when(block == 0)
    def _():
        for i in range(parts):
            k_aug[i * part : (i + 1) * part, :HDIM] = k_refs[i][...].T
            v_aug[:HDIM, i * part : (i + 1) * part] = v_refs[i][...]

    q_aug[:HDIM, :] = q_ref[...]
    queries = q_aug[...]
    count = span // chunk

    def scores(i):
        return dot(k_aug[i * chunk : (i + 1) * chunk, :], queries, 1, 0)

    upcoming = scores(0)
    row_max = total = None
    for i in range(count):
        current = upcoming
        if i + 1 < count:
            upcoming = scores(i + 1)
        chunk_max = jnp.max(current, axis=0, keepdims=True) * SCALE2
        new_max = chunk_max if i == 0 else jnp.maximum(row_max, chunk_max)
        weights = jnp.exp2(current * SCALE2 - new_max).astype(BF16)
        update = dot(v_aug[:, i * chunk : (i + 1) * chunk], weights, 1, 0)
        total = update if i == 0 else total * jnp.exp2(row_max - new_max) + update
        row_max = new_max
    denominator = total[HDIM : HDIM + 1, :]
    o_ref[...] = (total[:HDIM, :] / denominator).astype(BF16)
    lse_ref[...] = (row_max + jnp.log2(denominator))[None]


def attend(q_rot, k_parts, v_parts, bias_columns, first):
    width, rows = k_parts[0].shape
    parts = len(k_parts)
    span = parts * rows
    heads = width // HDIM
    q_rows = pick_block(rows, 768)
    chunk = pick_block(span, 512)
    q_spec = pl.BlockSpec((HDIM, q_rows), lambda h, j: (h + first, j))
    k_spec = pl.BlockSpec((HDIM, rows), lambda h, j: (h, 0))
    return pl.pallas_call(
        functools.partial(attend_kernel, parts, chunk),
        grid=(heads, rows // q_rows),
        in_specs=[q_spec, pl.BlockSpec((span, HDIM), lambda h, j: (0, 0))] + [k_spec] * (2 * parts),
        out_specs=[
            pl.BlockSpec((HDIM, q_rows), lambda h, j: (h, j)),
            pl.BlockSpec((1, 1, q_rows), lambda h, j: (h, 0, j)),
        ],
        out_shape=[
            jax.ShapeDtypeStruct((width, rows), BF16),
            jax.ShapeDtypeStruct((heads, 1, rows), F32),
        ],
        scratch_shapes=[
            pltpu.VMEM((span, 2 * HDIM), BF16),
            pltpu.VMEM((HDIM + 16, span), BF16),
            pltpu.VMEM((2 * HDIM, q_rows), BF16),
        ],
        compiler_params=pltpu.CompilerParams(vmem_limit_bytes=VMEM_LIMIT),
        cost_estimate=pl.CostEstimate(
            flops=16 * heads * rows * span * HDIM,
            bytes_accessed=2 * width * (2 * rows + 2 * span),
            transcendentals=heads * rows * span,
        ),
        name="attend",
    )(q_rot, bias_columns, *k_parts, *v_parts)


def in_three(values):
    first = values.astype(BF16)
    rest = values - first.astype(F32)
    second = rest.astype(BF16)
    return first.astype(F32), second.astype(F32), rest - second.astype(F32)


def unrotate(values, cosine, sine):
    low, high = values[:HALF], values[HALF:]
    return low * cosine + high * sine, high * cosine - low * sine


def attend_back_kernel(parts, chunk, *refs):
    q_ref, do_ref, o_ref, lse_ref, bias_ref, cos_ref, sin_ref = refs[:7]
    k_refs, v_refs = refs[7 : 7 + parts], refs[7 + parts : 7 + 2 * parts]
    dq_ref = refs[7 + 2 * parts]
    dk_refs = refs[8 + 2 * parts : 8 + 3 * parts]
    dv_refs = refs[8 + 3 * parts : 8 + 4 * parts]
    k_aug, v_aug, k_rows, q_aug, do_aug, dk_acc, dv_acc = refs[8 + 4 * parts :]
    head, block = pl.program_id(0), pl.program_id(1)
    span = k_aug.shape[1]
    part = span // parts
    q_rows = q_ref.shape[1]

    @pl.when((head == 0) & (block == 0))
    def _():
        row = lax.broadcasted_iota(jnp.int32, (HDIM, span), 0)
        ones = jnp.where(row < 4, 1.0, 0.0)
        k_aug[HDIM:, :] = jnp.where(row == 0, bias_ref[...], ones).astype(BF16)
        v_aug[HDIM:, :] = jnp.where(row < 3, 1.0, 0.0).astype(BF16)
        k_rows[:, HDIM:] = jnp.zeros((span, HDIM), BF16)

    @pl.when(block == 0)
    def _():
        for i in range(parts):
            at = slice(i * part, (i + 1) * part)
            keys = k_refs[i][...]
            k_aug[:HDIM, at] = keys
            v_aug[:HDIM, at] = v_refs[i][...]
            k_rows[at, :HDIM] = keys.T
        dk_acc[...] = jnp.zeros_like(dk_acc)
        dv_acc[...] = jnp.zeros_like(dv_acc)

    queries, d_heads = q_ref[...], do_ref[...]
    delta = jnp.sum(d_heads.astype(F32) * o_ref[...].astype(F32), axis=0, keepdims=True)
    row = lax.broadcasted_iota(jnp.int32, (HDIM, q_rows), 0)
    lse_a, lse_b, lse_c = in_three(lse_ref[0] * (-1.0 / SCALE2))
    del_a, del_b, del_c = in_three(-delta)
    q_extra = jnp.where(row == 2, lse_b, jnp.where(row == 3, lse_c, 0.0))
    q_extra = jnp.where(row == 0, 1.0, jnp.where(row == 1, lse_a, q_extra))
    do_extra = jnp.where(row == 1, del_b, jnp.where(row == 2, del_c, 0.0))
    do_extra = jnp.where(row == 0, del_a, do_extra)
    q_aug[:HDIM, :] = queries
    q_aug[HDIM:, :] = q_extra.astype(BF16)
    do_aug[:HDIM, :] = d_heads
    do_aug[HDIM:, :] = do_extra.astype(BF16)
    q_side, do_side = q_aug[...].T, do_aug[...].T
    count = span // chunk

    def products(i):
        at = slice(i * chunk, (i + 1) * chunk)
        return dot(q_side, k_aug[:, at], 1, 0), dot(do_side, v_aug[:, at], 1, 0)

    upcoming = products(0)
    d_query = None
    for i in range(count):
        at = slice(i * chunk, (i + 1) * chunk)
        scores, d_probs = upcoming
        if i + 1 < count:
            upcoming = products(i + 1)
        probs = jnp.exp2(scores * SCALE2)
        d_scores = (probs * d_probs).astype(BF16)
        dv_acc[:, at] += dot(d_heads, probs.astype(BF16), 1, 0)
        dk_acc[:, at] += dot(queries, d_scores, 1, 0)
        update = dot(d_scores, k_rows[at, :], 1, 0)
        d_query = update if i == 0 else d_query + update
    first = pl.multiple_of(block * q_rows, q_rows)
    low, high = unrotate(
        d_query.T[:HDIM, :] * SCALE, cos_ref[:, pl.ds(first, q_rows)], sin_ref[:, pl.ds(first, q_rows)]
    )
    dq_ref[:HALF, :] = low.astype(BF16)
    dq_ref[HALF:, :] = high.astype(BF16)

    @pl.when(block == pl.num_programs(1) - 1)
    def _():
        for i in range(parts):
            at = slice(i * part, (i + 1) * part)
            low, high = unrotate(dk_acc[:, at] * SCALE, cos_ref[:, at], sin_ref[:, at])
            dk_refs[i][:HALF, :] = low.astype(dk_refs[i].dtype)
            dk_refs[i][HALF:, :] = high.astype(dk_refs[i].dtype)
            dv_refs[i][...] = dv_acc[:, at].astype(dv_refs[i].dtype)


def attend_back(q_rot, k_parts, v_parts, d_heads, heads_out, lse, bias_row, cosine, sine, first, within, count):
    rows = q_rot.shape[1]
    parts = len(k_parts)
    span = parts * rows
    q_rows = pick_block(rows, 1536)
    chunk = pick_block(span, 256)
    q_spec = pl.BlockSpec((HDIM, q_rows), lambda h, j: (h + first, j))
    k_spec = pl.BlockSpec((HDIM, rows), lambda h, j: (h + within, 0))
    whole = lambda array: pl.BlockSpec(array.shape, lambda h, j: (0, 0))
    part_out = pl.BlockSpec((HDIM, rows), lambda h, j: (h, 0))
    shape = lambda kind: jax.ShapeDtypeStruct((count * HDIM, rows), kind)
    part_kinds = [F32] + [BF16] * (parts - 1)
    out = pl.pallas_call(
        functools.partial(attend_back_kernel, parts, chunk),
        grid=(count, rows // q_rows),
        in_specs=[
            q_spec,
            q_spec,
            pl.BlockSpec((HDIM, q_rows), lambda h, j: (h + within, j)),
            pl.BlockSpec((1, 1, q_rows), lambda h, j: (h + within, 0, j)),
            whole(bias_row),
            whole(cosine),
            whole(sine),
        ]
        + [k_spec] * (2 * parts),
        out_specs=[pl.BlockSpec((HDIM, q_rows), lambda h, j: (h, j))] + [part_out] * (2 * parts),
        out_shape=[shape(BF16)] + [shape(kind) for kind in part_kinds * 2],
        scratch_shapes=[
            pltpu.VMEM((2 * HDIM, span), BF16),
            pltpu.VMEM((2 * HDIM, span), BF16),
            pltpu.VMEM((span, 2 * HDIM), BF16),
            pltpu.VMEM((2 * HDIM, q_rows), BF16),
            pltpu.VMEM((2 * HDIM, q_rows), BF16),
            pltpu.VMEM((HDIM, span), F32),
            pltpu.VMEM((HDIM, span), F32),
        ],
        compiler_params=pltpu.CompilerParams(vmem_limit_bytes=VMEM_LIMIT),
        cost_estimate=pl.CostEstimate(
            flops=5 * count * rows * span * HDIM,
            bytes_accessed=0,
            transcendentals=0,
        ),
        name="attend_back",
    )(q_rot, d_heads, heads_out, lse, bias_row, cosine, sine, *k_parts, *v_parts)
    return out[0], out[1 : 1 + parts], out[1 + parts :]


def norm_parts(values):
    centered = values - jnp.mean(values, axis=-1, keepdims=True)
    scale = lax.rsqrt(jnp.mean(centered * centered, axis=-1, keepdims=True) + 1e-06)
    return centered * scale, scale


def norm_back(normed, scale, d_normed):
    return (
        d_normed
        - jnp.mean(d_normed, axis=-1, keepdims=True)
        - normed * jnp.mean(d_normed * normed, axis=-1, keepdims=True)
    ) * scale


def gelu_both(values):
    square = values * values
    bend = jnp.tanh(0.7978845608028654 * (values + 0.044715 * values * square))
    half = 0.5 * (1.0 + bend)
    slope = 0.7978845608028654 * (1.0 + 3 * 0.044715 * square)
    return values * half, half + 0.5 * values * (1.0 - bend * bend) * slope


def add_rows(values):
    return jnp.sum(values, axis=0, keepdims=True)


def store_rotated(out_ref, values, cosine, sine):
    for at in range(0, out_ref.shape[0], HDIM):
        low, high = values[at : at + HALF], values[at + HALF : at + HDIM]
        out_ref[at : at + HALF, :] = (low * cosine - high * sine).astype(BF16)
        out_ref[at + HALF : at + HDIM, :] = (high * cosine + low * sine).astype(BF16)


def either(first_ref, second_ref):
    half = pl.num_programs(0) // 2
    return jnp.where(pl.program_id(0) < half, first_ref[...], second_ref[...])


def halves_spec(inputs, rows, block, width):
    if inputs[0].shape[0] == rows:
        return [pl.BlockSpec((block, width), lambda i, *_: (i, 0))] * 2
    half = rows // 2 // block
    return [
        pl.BlockSpec((block, width), lambda i, *_: (jnp.minimum(i, half - 1), 0)),
        pl.BlockSpec((block, width), lambda i, *_: (jnp.maximum(i - half, 0), 0)),
    ]


def project_kv_kernel(groups, x_ref, y_ref, vectors_ref, w_ref, cos_ref, sin_ref, h_ref, *refs):
    k_refs, v_refs = refs[:groups], refs[groups:]
    width = x_ref.shape[1]
    tall = width // groups
    normed, _ = norm_parts(either(x_ref, y_ref).astype(F32))
    h_one = (normed * (1.0 + vectors_ref[1:2, :]) + vectors_ref[0:1, :]).astype(BF16)
    h_ref[...] = h_one
    keys = (dot(h_one, w_ref[:, :width], 1, 0) + vectors_ref[7:8, :]).T
    values = (dot(h_one, w_ref[:, width:], 1, 0) + vectors_ref[8:9, :]).astype(BF16).T
    for i in range(groups):
        store_rotated(k_refs[i], keys[i * tall : (i + 1) * tall], cos_ref[...], sin_ref[...])
        v_refs[i][...] = values[i * tall : (i + 1) * tall]


def project_q_kernel(h_ref, vectors_ref, w_ref, cos_ref, sin_ref, q_ref):
    queries = dot(h_ref[...], w_ref[...], 1, 0) + vectors_ref[6:7, :]
    store_rotated(q_ref, queries.T, cos_ref[...], sin_ref[...])


def whole_spec(shape, column=0):
    return pl.BlockSpec(shape, lambda i, *_: (0, column), pipeline_mode=pl.Buffered(1))


def project(inputs, vectors, packed, cosine, sine, groups):
    width, rows = inputs[0].shape[1], cosine.shape[1]
    block = pick_block(inputs[0].shape[0], 256)
    tall = width // groups
    row_spec = pl.BlockSpec((block, width), lambda i: (i, 0))
    turned_spec = lambda height: pl.BlockSpec((height, block), lambda i: (0, i))
    turned = lambda height: jax.ShapeDtypeStruct((height, rows), BF16)
    table_spec = turned_spec(HALF)
    params = pltpu.CompilerParams(vmem_limit_bytes=VMEM_LIMIT)
    out = pl.pallas_call(
        functools.partial(project_kv_kernel, groups),
        grid=(rows // block,),
        in_specs=halves_spec(inputs, rows, block, width)
        + [whole_spec(vectors.shape), whole_spec((width, 2 * width)), table_spec, table_spec],
        out_specs=[row_spec] + [turned_spec(tall)] * (2 * groups),
        out_shape=[jax.ShapeDtypeStruct((rows, width), BF16)] + [turned(tall)] * (2 * groups),
        compiler_params=params,
        cost_estimate=pl.CostEstimate(
            flops=8 * rows * width * width, bytes_accessed=8 * rows * width + 4 * width * width, transcendentals=0
        ),
        name="project_kv",
    )(*inputs, vectors, packed, cosine, sine)
    h_one, keys, values = out[0], out[1 : 1 + groups], out[1 + groups :]
    queries = pl.pallas_call(
        project_q_kernel,
        grid=(rows // block,),
        in_specs=[row_spec, whole_spec(vectors.shape), whole_spec((width, width), 2), table_spec, table_spec],
        out_specs=turned_spec(width),
        out_shape=turned(width),
        compiler_params=params,
        cost_estimate=pl.CostEstimate(
            flops=4 * rows * width * width, bytes_accessed=4 * rows * width + 2 * width * width, transcendentals=0
        ),
        name="project_q",
    )(h_one, vectors, packed, cosine, sine)
    return h_one, queries, keys, values


def feed_forward_kernel(parts, pieces, split, slot_ref, *refs):
    o_refs = refs[:parts]
    x_ref, y_ref, cot_ref, cot_y_ref, keep_ref, w_ref, vectors_ref = refs[parts : parts + 7]
    own_ref, away_ref, d_res_ref, d_heads_ref, g_rows_ref, sums_ref = refs[parts + 7 : parts + 13]
    acc, acc_rows, slope_ref, hidden_ref, staged, sems = refs[parts + 13 :]
    step, count = pl.program_id(0), pl.num_programs(0)
    width = x_ref.shape[1]

    @pl.when(step == 0)
    def _():
        acc[...] = jnp.zeros_like(acc)
        acc_rows[...] = jnp.zeros_like(acc_rows)

    gate_one, shift_two, scale_two, gate_two, b_out, b_down = [vectors_ref[i : i + 1, :] for i in (2, 3, 4, 5, 9, 10)]
    out_at = slice(0, width)
    up_at = [slice((1 + i) * width, (2 + i) * width) for i in range(pieces)]
    down_at = [slice((1 + pieces + i) * width, (2 + pieces + i) * width) for i in range(pieces)]
    keep = keep_ref[...]
    heads_out = jnp.concatenate([ref[...] for ref in o_refs], axis=0)
    branch = (dot(heads_out, w_ref[:, out_at], 0, 0) + b_out) * keep
    residual = either(x_ref, y_ref).astype(F32) + gate_one * branch
    normed, inverse = norm_parts(residual)
    h_two = (normed * (1.0 + scale_two) + shift_two).astype(BF16)
    ff_out = b_down
    for i in range(pieces):
        value, slope = gelu_both(dot(h_two, w_ref[:, up_at[i]], 1, 0) + vectors_ref[11 + i : 12 + i, :])
        slope_ref[i] = slope
        hidden = value.astype(BF16)
        hidden_ref[i] = hidden
        ff_out = ff_out + dot(hidden, w_ref[:, down_at[i]], 1, 0)
    mixed = (residual + gate_two * ff_out).astype(BF16)
    if split:

        @pl.when(step < count // 2)
        def _():
            own_ref[0] = mixed

        @pl.when(step >= count // 2)
        def _():
            away_ref[...] = mixed
    else:
        own_ref[...] = mixed
    d_mixed = either(cot_ref, cot_y_ref).astype(F32)
    acc_rows[3:4, :] += add_rows(d_mixed * ff_out)
    d_ff = (d_mixed * gate_two).astype(BF16)
    acc_rows[5:6, :] += add_rows(d_ff.astype(F32))
    d_h_two = None
    for i in range(pieces):
        acc[:, down_at[i]] += dot(hidden_ref[i], d_ff, 0, 0)
        d_up = (dot(d_ff, w_ref[:, down_at[i]], 1, 1) * slope_ref[i]).astype(BF16)
        acc_rows[6 + i : 7 + i, :] += add_rows(d_up.astype(F32))
        acc[:, up_at[i]] += dot(h_two, d_up, 0, 0)
        update = dot(d_up, w_ref[:, up_at[i]], 1, 1)
        d_h_two = update if i == 0 else d_h_two + update
    acc_rows[1:2, :] += add_rows(d_h_two)
    acc_rows[2:3, :] += add_rows(d_h_two * normed)
    d_residual = d_mixed + norm_back(normed, inverse, d_h_two * (1.0 + scale_two))
    d_res_ref[...] = d_residual
    acc_rows[0:1, :] += add_rows(d_residual * branch)
    d_branch = (d_residual * gate_one * keep).astype(BF16)
    acc_rows[4:5, :] += add_rows(d_branch.astype(F32))
    acc[:, out_at] += dot(heads_out, d_branch, 1, 0)
    d_heads_ref[...] = dot(w_ref[:, out_at], d_branch, 1, 1).astype(BF16)

    @pl.when(step == count - 1)
    def _():
        sums_ref[...] = acc_rows[...]
        tall = staged.shape[1]
        copies = []
        for i in range(width // tall):
            slot = i % 2
            if i >= 2:
                copies[i - 2].wait()
            staged[slot] = acc[i * tall : (i + 1) * tall, :].astype(BF16)
            copies.append(pltpu.make_async_copy(staged.at[slot], g_rows_ref.at[pl.ds(i * tall, tall), :], sems.at[slot]))
            copies[i].start()
        for copy in copies[-2:]:
            copy.wait()


def feed_forward(slot, inputs, heads_out, cotangent, keep, packed, vectors, slots):
    rows, width = heads_out[0].shape[1], inputs[0].shape[1]
    pieces = (packed.shape[1] // width - 1) // 2
    block = pick_block(inputs[0].shape[0], 256)
    local = rows // slots
    split = inputs[0].shape[0] == local
    half = local // block
    row_spec = pl.BlockSpec((block, width), lambda i, *_: (i, 0))
    turned_spec = lambda height: pl.BlockSpec((height, block), lambda i, *_: (0, i))
    kinds = jax.ShapeDtypeStruct
    if split:
        mixed_specs = [
            pl.BlockSpec((1, block, width), lambda i, at: (at[0], jnp.minimum(i, half - 1), 0)),
            pl.BlockSpec((block, width), lambda i, *_: (jnp.maximum(i - half, 0), 0)),
        ]
        mixed_shapes = [kinds((slots, local, width), BF16), kinds((local, width), BF16)]
    else:
        mixed_specs = [row_spec, whole_spec((8, 128))]
        mixed_shapes = [kinds((rows, width), BF16), kinds((8, 128), BF16)]
    return pl.pallas_call(
        functools.partial(feed_forward_kernel, len(heads_out), pieces, split),
        grid_spec=pltpu.PrefetchScalarGridSpec(
            num_scalar_prefetch=1,
            grid=(rows // block,),
            in_specs=[turned_spec(part.shape[0]) for part in heads_out]
            + halves_spec(inputs, rows, block, width) * 2
            + [
                pl.BlockSpec((block, 1), lambda i, *_: (i, 0)),
                whole_spec(packed.shape),
                whole_spec(vectors.shape),
            ],
            out_specs=mixed_specs
            + [
                row_spec,
                turned_spec(width),
                pl.BlockSpec(memory_space=pl.ANY),
                whole_spec((8, width)),
            ],
            scratch_shapes=[
                pltpu.VMEM(packed.shape, F32),
                pltpu.VMEM((8, width), F32),
                pltpu.VMEM((pieces, block, width), F32),
                pltpu.VMEM((pieces, block, width), BF16),
                pltpu.VMEM((2, pick_block(width, 256), packed.shape[1]), BF16),
                pltpu.SemaphoreType.DMA((2,)),
            ],
        ),
        out_shape=mixed_shapes
        + [
            kinds((rows, width), F32),
            kinds((width, rows), BF16),
            kinds(packed.shape, BF16),
            kinds((8, width), F32),
        ],
        compiler_params=pltpu.CompilerParams(vmem_limit_bytes=VMEM_LIMIT),
        cost_estimate=pl.CostEstimate(
            flops=6 * rows * width * packed.shape[1],
            bytes_accessed=8 * rows * width + 4 * width * packed.shape[1],
            transcendentals=0,
        ),
        name="feed_forward",
    )(slot, *heads_out, *inputs, *cotangent, keep, packed, vectors)


def weight_grads_kernel(parts, h_ref, dq_ref, *refs):
    dk_refs, dv_refs = refs[:parts], refs[parts : 2 * parts]
    dk_out, dv_out, weight_ref, bias_ref = refs[2 * parts :]

    def summed(pieces):
        total = pieces[0][...]
        for ref in pieces[1:]:
            total = total + ref[...].astype(F32)
        return total.astype(BF16)

    grads = [dq_ref[...], summed(dk_refs), summed(dv_refs)]
    dk_out[...] = grads[1]
    dv_out[...] = grads[2]
    weight_ref[...] = dot(jnp.concatenate(grads, axis=0), h_ref[...], 1, 0).T.astype(BF16)
    for i, grad in enumerate(grads):
        bias_ref[:, i : i + 1] = jnp.sum(grad.astype(F32), axis=1, keepdims=True)


def weight_grads(h_one, d_query, dk_parts, dv_parts):
    rows, width = h_one.shape
    tall = d_query.shape[0]
    block = pick_block(tall, 128)
    spec = pl.BlockSpec((block, rows), lambda i: (i, 0))
    kinds = jax.ShapeDtypeStruct
    parts = len(dk_parts)
    return pl.pallas_call(
        functools.partial(weight_grads_kernel, parts),
        grid=(tall // block,),
        in_specs=[whole_spec((rows, width))] + [spec] * (1 + 2 * parts),
        out_specs=[
            spec,
            spec,
            pl.BlockSpec((width, 3 * block), lambda i: (0, i)),
            pl.BlockSpec((block, 128), lambda i: (i, 0)),
        ],
        out_shape=[
            kinds((tall, rows), BF16),
            kinds((tall, rows), BF16),
            kinds((width, 3 * tall), BF16),
            kinds((tall, 128), F32),
        ],
        compiler_params=pltpu.CompilerParams(vmem_limit_bytes=VMEM_LIMIT),
        cost_estimate=pl.CostEstimate(flops=0, bytes_accessed=0, transcendentals=0),
        name="weight_grads",
    )(h_one, d_query, *dk_parts, *dv_parts)


def input_grads_kernel(counts, slot_ref, x_ref, d_res_ref, vectors_ref, w_ref, *refs):
    grad_refs, (out_ref, sums_ref) = refs[:-2], refs[-2:]
    width = x_ref.shape[1]

    @pl.when(pl.program_id(0) == 0)
    def _():
        sums_ref[...] = jnp.zeros_like(sums_ref)

    turned = None
    used = 0
    for kind in range(3):
        first = (2, 0, 1)[kind] * width
        grad = jnp.concatenate([ref[...] for ref in grad_refs[used : used + counts[kind]]], axis=0)
        used += counts[kind]
        update = dot(w_ref[:, first : first + width], grad, 1, 0)
        turned = update if turned is None else turned + update
    d_h_one = turned.T
    normed, inverse = norm_parts(x_ref[...].astype(F32))
    sums_ref[0:1, :] += add_rows(d_h_one)
    sums_ref[1:2, :] += add_rows(d_h_one * normed)
    grad = (d_res_ref[...] + norm_back(normed, inverse, d_h_one * (1.0 + vectors_ref[1:2, :]))).astype(BF16)
    out_ref[...] = grad.reshape(out_ref.shape)


def input_grads(slot, slots, inputs, half, d_residual, vectors, packed, grads):
    rows, width = inputs.shape
    block = pick_block(rows, 256)
    first = half * (rows // block)
    row_spec = pl.BlockSpec((block, width), lambda i, *_: (i, 0))
    flat = [grad for kind in grads for grad in kind]
    out_spec, out_shape = row_spec, (rows, width)
    if slots:
        out_spec = pl.BlockSpec((1, block, width), lambda i, at: (at[0], i, 0))
        out_shape = (slots, rows, width)
    return pl.pallas_call(
        functools.partial(input_grads_kernel, [len(kind) for kind in grads]),
        grid_spec=pltpu.PrefetchScalarGridSpec(
            num_scalar_prefetch=1,
            grid=(rows // block,),
            in_specs=[
                row_spec,
                pl.BlockSpec((block, width), lambda i, *_: (i + first, 0)),
                whole_spec(vectors.shape),
                whole_spec((width, 3 * width)),
            ]
            + [pl.BlockSpec((grad.shape[0], block), lambda i, *_: (0, i + first)) for grad in flat],
            out_specs=[out_spec, whole_spec((8, width))],
        ),
        out_shape=[jax.ShapeDtypeStruct(out_shape, BF16), jax.ShapeDtypeStruct((8, width), F32)],
        compiler_params=pltpu.CompilerParams(vmem_limit_bytes=VMEM_LIMIT),
        cost_estimate=pl.CostEstimate(
            flops=16 * rows * width * width, bytes_accessed=14 * rows * width + 6 * width * width, transcendentals=0
        ),
        name="input_grads",
    )(slot, inputs, d_residual, vectors, packed, *flat)


def time_features(t_index, model_width):
    half_width = model_width // 2
    indices = jnp.arange(half_width).astype(F32)
    frequency = jnp.exp(indices * (-math.log(10000.0) / (half_width - 1)))
    angles = t_index.astype(F32)[:, None] * frequency[None, :]
    return jnp.concatenate([jnp.sin(angles), jnp.cos(angles)], axis=1)


def rotary_tables(places):
    inverse = jnp.exp(jnp.arange(HALF).astype(F32) * (-2.0 * math.log(10000.0) / HDIM))
    angles = inverse[:, None] * places.astype(F32)[None, :]
    return jnp.cos(angles), jnp.sin(angles)


def after(values, *others):
    return lax.optimization_barrier((values,) + others)[0]


def make_body(mesh):
    n_dp, n_fsdp = mesh.shape["dp"], mesh.shape["fsdp"]
    n_pairs = n_fsdp // 2

    def shift(values, axis, size, by):
        return lax.ppermute(values, axis, [(i, (i + by) % size) for i in range(size)])

    def pick(values, index, axis=0):
        return lax.dynamic_index_in_dim(values, index, axis, keepdims=False)

    def body(
        frames,
        lengths,
        t_index,
        w_ada,
        b_ada,
        w_query,
        b_query,
        w_key,
        b_key,
        w_value,
        b_value,
        w_out,
        b_out,
        w_up,
        b_up,
        w_down,
        b_down,
        grad_out,
    ):
        slots, local, width = frames.shape
        group = n_fsdp // slots
        hidden_width = w_up.shape[1]
        shard = w_query.shape[0]
        ada_width = w_ada.shape[1]
        dp, fsdp = lax.axis_index("dp"), lax.axis_index("fsdp")
        me = dp * n_fsdp + fsdp
        slot, place = fsdp // group, fsdp % group
        other = 1 - slot
        core, pair = fsdp % 2, fsdp // 2
        side, deep, far = dp % 2, dp // 2, n_dp // 2
        length = pick(lengths, slot)

        def picked(values):
            return pick(values, slot), pick(values, other)

        split = local % 128 == 0

        def swap_in(own, away):
            parts = own, shift(away, "fsdp", n_fsdp, group)
            return parts if split else (jnp.concatenate(parts),) * 2

        def swap_out(whole, away, pieces=1):
            arrived = []
            for first in range(0, local, local // pieces):
                piece = shift(away[first : first + local // pieces], "fsdp", n_fsdp, group)
                arrived.append(piece)
                whole = lax.dynamic_update_slice(whole, piece[None], (other, first, 0))
            return whole, arrived

        def placed_own(own):
            return lax.dynamic_update_index_in_dim(jnp.zeros((slots, local, width), own.dtype), own, slot, 0)

        def places_of(member):
            at = slot * group + member
            blocks = [((at - by * group) + n_fsdp) % n_fsdp for by in range(slots)]
            return jnp.concatenate([b * local + jnp.arange(local, dtype=jnp.int32) for b in blocks])

        ring = lambda by: [(i, (i // group) * group + (i % group + by) % group) for i in range(n_fsdp)]

        def swap(values, axis, size):
            return lax.ppermute(values, axis, [(i, i ^ 1) for i in range(size)])

        def sum_core(values):
            values = values.reshape(n_dp, n_pairs, 2, shard, values.shape[1])
            arrived = swap(pick(values, 1 - core, 2), "fsdp", n_fsdp)
            return pick(values, core, 2).astype(F32) + arrived.astype(F32)

        def sum_pairs(values):
            axis = values.ndim - 3
            total = pick(values, pair, axis).astype(F32)
            for by in range(1, n_pairs):
                arrived = shift(pick(values, (pair + by) % n_pairs, axis), "fsdp", n_fsdp, 2 * by)
                total = total + arrived.astype(F32)
            return total

        def sum_side(values):
            values = values.reshape((far, 2) + values.shape[1:])
            arrived = swap(pick(values, 1 - side, 1), "dp", n_dp)
            return pick(values, side, 1).astype(F32) + arrived.astype(F32)

        def sum_far(values):
            total = pick(values, deep).astype(F32)
            for by in range(1, far):
                arrived = shift(pick(values, (deep + by) % far), "dp", n_dp, 2 * by)
                total = total + arrived.astype(F32)
            return total

        def gather_dp(values):
            values = jnp.stack([values] + [shift(values, "dp", n_dp, 2 * by) for by in range(1, far)])
            return jnp.stack([values, swap(values, "dp", n_dp)])

        packed = lax.all_gather(jnp.concatenate([w_key, w_value, w_query], axis=1), AXES, axis=0, tiled=True)
        ups = hidden_width // width
        w_up_turned = w_up.reshape(shard, n_dp * n_fsdp, ups, shard).swapaxes(1, 2).reshape(w_up.shape)
        downs = [w_down[i * shard : (i + 1) * shard] for i in range(ups)]
        packed_two = lax.all_gather(jnp.concatenate([w_out, w_up_turned, *downs], axis=1), AXES, axis=0, tiled=True)

        inputs = swap_in(*picked(frames))
        rows = slots * local
        own_grad, away_grad = picked(grad_out)

        t_all = gather_dp(t_index).reshape(-1)
        active = jax.nn.silu(time_features(t_all, width)).astype(BF16)
        active_mine = lax.dynamic_slice_in_dim(active, me * shard, shard, axis=1)
        partial = [dot(active_mine, w_ada, 1, 0)]
        for bias in (b_query, b_key, b_value, b_out, b_down, *jnp.split(b_up, ups)):
            size = bias.shape[0]
            zeros = jnp.zeros((1, size * n_dp * n_fsdp), F32)
            placed = lax.dynamic_update_slice_in_dim(zeros, bias.astype(F32)[None], me * size, axis=1)
            partial.append(jnp.broadcast_to(placed, (n_dp * slots, placed.shape[1])))
        placed = lax.dynamic_update_slice_in_dim(
            jnp.zeros((1, ada_width), F32), b_ada.astype(F32)[None], me * b_ada.shape[0], axis=1
        )
        partial[0] = partial[0] + placed
        partial = jnp.concatenate(partial, axis=1).reshape(2, far, slots, -1)
        partial = partial[0] + swap(partial[1], "dp", n_dp)
        summed = partial[0]
        for by in range(1, far):
            summed = summed + shift(partial[by], "dp", n_dp, -2 * by)
        one = pick(summed, slot) + shift(pick(summed, other), "fsdp", n_fsdp, group)
        vectors = one
        for by in range(1, group):
            vectors = vectors + lax.ppermute(one, "fsdp", ring(by))
        vectors = vectors.reshape(-1, width)
        vectors = jnp.pad(vectors, ((0, -vectors.shape[0] % 8), (0, 0)))

        key_places = jnp.concatenate([places_of((place - by + group) % group) for by in range(group)])
        cosine, sine = rotary_tables(key_places)
        key_bias = jnp.where(key_places < length, 0.0, -1e30)
        bias_columns = jnp.pad(key_bias.astype(BF16)[:, None], ((0, 0), (0, HDIM - 1)))
        keep = (key_places[:rows] < length).astype(F32)[:, None]

        wide = 2
        vectors, cosine, sine, key_bias, bias_columns, keep, own_grad, away_grad = lax.optimization_barrier(
            (vectors, cosine, sine, key_bias, bias_columns, keep, own_grad, away_grad)
        )
        h_one, q_rot, keys, values = project(inputs, vectors, packed, cosine[:, :rows], sine[:, :rows], wide)
        cotangent = swap_in(own_grad, after(away_grad, keys[0]))
        heads = width // HDIM
        tall = heads // wide
        with_ring = lambda own: [own] + [lax.ppermute(own, "fsdp", ring(by)) for by in range(1, group)]
        k_parts, v_parts = [with_ring(own) for own in keys], [with_ring(own) for own in values]
        heads_out, lses = [], []
        for at in range(wide):
            out, lse = attend(q_rot, k_parts[at], v_parts[at], bias_columns, at * tall)
            heads_out.append(out)
            lses.append(lse)
        at_slot = slot.reshape(1).astype(jnp.int32)
        mixed, away_mixed, d_residual, d_heads, g_rows, sums_two = feed_forward(
            at_slot, inputs, heads_out, cotangent, keep, packed_two, vectors, slots
        )
        if not split:
            mixed, away_mixed = placed_own(mixed[:local]), mixed[local:]
        mixed, _ = swap_out(mixed, away_mixed)

        sum_rows = lax.psum_scatter(g_rows, AXES, scatter_dimension=0, tiled=True).astype(F32)
        g_out = sum_rows[:, :width]
        g_up = sum_rows[:, width : width + hidden_width].reshape(shard, ups, n_dp * n_fsdp, shard)
        g_up = g_up.swapaxes(1, 2).reshape(w_up.shape)
        g_down = jnp.concatenate([sum_rows[:, (1 + ups + i) * width : (2 + ups + i) * width] for i in range(ups)])

        grads, d_biases, weight_sums = ([], [], []), [], []

        def sum_parts(pieces):
            sums = [weight_grads(h_one, *piece) for piece in pieces]
            for piece, (dk, dv, _, bias_grad) in zip(pieces, sums):
                for kind, grad in zip(grads, (piece[0], dk, dv)):
                    kind.append(grad)
                d_biases.append(bias_grad[:, :3])
            return jnp.concatenate([values[2] for values in sums], axis=1)

        counts = (tall, tall // 4, tall // 4, tall // 2)
        first, ready, arrived, moving = 0, d_heads, [], None
        for step, each in enumerate(counts):
            part, within = first // tall, first % tall
            dq, dk_parts, dv_parts = attend_back(
                q_rot,
                k_parts[part],
                v_parts[part],
                ready,
                heads_out[part],
                lses[part],
                key_bias[None],
                cosine,
                sine,
                first,
                within,
                each,
            )
            first += each
            dk_parts = [dk_parts[0]] + [lax.ppermute(dk_parts[by], "fsdp", ring(-by)) for by in range(1, group)]
            dv_parts = [dv_parts[0]] + [lax.ppermute(dv_parts[by], "fsdp", ring(-by)) for by in range(1, group)]
            arrived.append((dq, dk_parts, dv_parts))
            if step == 1:
                arrived[0][1][0] = after(arrived[0][1][0], dq)
                weight_sums.append(sum_parts([arrived[0]]))
                moving = sum_core(weight_sums[0]).astype(BF16)
                ready = after(d_heads, dq, weight_sums[0])
            if step == 2:
                moving = after(moving, dq)
                ready = after(d_heads, dq, moving)
        early_pairs = sum_pairs(moving).astype(BF16)
        arrived[2][1][0] = after(arrived[2][1][0], dq)
        weight_sums.append(sum_parts(arrived[1:3]))
        halves = [sum_core(weight_sums[1])]
        arrived[3][1][0] = after(arrived[3][1][0], weight_sums[1], sum_rows)
        weight_sums.append(sum_parts(arrived[3:]))
        halves.append(sum_core(weight_sums[2]))
        early_sum = sum_far(sum_side(early_pairs).astype(BF16))
        if split:
            rest = after(d_residual, weight_sums[2])
            away_frames, sums_away = input_grads(at_slot, 0, inputs[1], 1, rest, vectors, packed, grads)
            core_sums = jnp.concatenate(halves, axis=-1).astype(BF16)
            rest, away_frames, core_sums = lax.optimization_barrier((d_residual, away_frames, core_sums))
            own_frames, sums_own = input_grads(at_slot, slots, inputs[0], 0, rest, vectors, packed, grads)
            sums_one = sums_own + sums_away
        else:
            core_sums = jnp.concatenate(halves, axis=-1).astype(BF16)
            both, sums_one = input_grads(at_slot, 0, inputs[0], 0, d_residual, vectors, packed, grads)
            own_frames, away_frames = placed_own(both[:local]), both[local:]
        grad_frames, frames_arrived = swap_out(own_frames, away_frames, 3)
        side_sums = sum_side(core_sums).astype(BF16)
        late_sum = sum_pairs(sum_far(side_sums).astype(BF16))
        sums = [early_sum, late_sum]

        vector = jnp.concatenate(
            [sums_one[:2], sums_two[: 6 + ups], jnp.concatenate(d_biases).T]
        )
        for_slot = 6
        vector = after(vector, *frames_arrived[:2])
        total = vector
        for by in range(1, group):
            total = total + lax.ppermute(vector, "fsdp", ring(by))
        packs = gather_dp(total).reshape(n_dp, -1, width)
        pack = jnp.concatenate([packs[:, :for_slot].reshape(-1, width), jnp.sum(packs[:, for_slot:], axis=0)])
        pack, g_out, g_up, g_down, _ = lax.optimization_barrier((pack, g_out, g_up, g_down, frames_arrived[2]))
        across = shift(pack, "fsdp", n_fsdp, group)
        count = n_dp * for_slot
        d_mod = jnp.stack([jnp.where(slot == s, pack[:count], across[:count]).reshape(n_dp, -1) for s in range(slots)], axis=1)
        d_mod = d_mod.reshape(n_dp * slots, for_slot * width)
        d_vectors = pack[count:] + across[count:]

        g_w_ada = lax.dot_general(
            active_mine.astype(F32),
            d_mod,
            (((0,), (0,)), ((), ())),
            precision=lax.Precision.HIGHEST,
            preferred_element_type=F32,
        )

        def mine(vector):
            vector = vector.reshape(-1)
            size = vector.shape[0] // (n_dp * n_fsdp)
            return lax.dynamic_slice_in_dim(vector, me * size, size)

        columns = jnp.concatenate(sums, axis=1).reshape(shard, -1, 3, pick_block(tall // 2 * HDIM, 128))
        g_qkv = [columns[:, :, i].reshape(shard, width) for i in range(3)]
        return (
            mixed,
            grad_frames,
            g_w_ada,
            mine(jnp.sum(d_mod, axis=0)),
            g_qkv[0],
            mine(d_vectors[2 + ups]),
            g_qkv[1],
            mine(d_vectors[3 + ups]),
            g_qkv[2],
            mine(d_vectors[4 + ups]),
            g_out,
            mine(d_vectors[0]),
            g_up,
            jnp.concatenate([mine(d_vectors[2 + i]) for i in range(ups)]),
            g_down,
            mine(d_vectors[1]),
        )

    return body


def solution(mesh):
    rows, vector, matrix = P("dp", "fsdp", None), P(AXES), P(AXES, None)
    return jax.shard_map(
        make_body(mesh),
        mesh=mesh,
        in_specs=(rows, P("dp"), P("dp")) + (matrix, vector) * 7 + (rows,),
        out_specs=(rows, rows) + (matrix, vector) * 7,
        check_vma=False,
    )
```

```python
import functools
import math

import jax
import jax.numpy as jnp
from jax import lax
from jax.experimental import pallas as pl
from jax.experimental.pallas import tpu as pltpu
from jax.sharding import PartitionSpec as P

HDIM = 64
HALF = HDIM // 2
SCALE = HDIM ** (-0.5)
SCALE2 = SCALE * math.log2(math.e)
AXES = ("dp", "fsdp")
VMEM_LIMIT = 62 << 20
F32 = jnp.float32
BF16 = jnp.bfloat16


def dot(left_side, right_side, left_dim, right_dim):
    return lax.dot_general(
        left_side,
        right_side,
        (((left_dim,), (right_dim,)), ((), ())),
        preferred_element_type=F32,
    )


def pick_block(total, wanted):
    block = min(total, wanted)
    while total % block:
        block -= 128
    return block


def attend_kernel(parts, chunk, *refs):
    q_ref, bias_ref = refs[0], refs[1]
    k_refs, v_refs = refs[2 : 2 + parts], refs[2 + parts : 2 + 2 * parts]
    o_ref, lse_ref, k_aug, v_aug, q_aug = refs[2 + 2 * parts :]
    head, block = pl.program_id(0), pl.program_id(1)
    span = k_aug.shape[0]
    part = span // parts
    q_rows = q_ref.shape[1]

    @pl.when((head == 0) & (block == 0))
    def _():
        k_aug[:, HDIM:] = bias_ref[...]
        v_aug[HDIM:, :] = jnp.ones((16, span), BF16)
        q_aug[HDIM:, :] = jnp.ones((HDIM, q_rows), BF16)

    @pl.when(block == 0)
    def _():
        for i in range(parts):
            k_aug[i * part : (i + 1) * part, :HDIM] = k_refs[i][...].T
            v_aug[:HDIM, i * part : (i + 1) * part] = v_refs[i][...]

    q_aug[:HDIM, :] = q_ref[...]
    queries = q_aug[...]
    count = span // chunk

    def scores(i):
        return dot(k_aug[i * chunk : (i + 1) * chunk, :], queries, 1, 0)

    upcoming = scores(0)
    row_max = total = None
    for i in range(count):
        current = upcoming
        if i + 1 < count:
            upcoming = scores(i + 1)
        chunk_max = jnp.max(current, axis=0, keepdims=True) * SCALE2
        new_max = chunk_max if i == 0 else jnp.maximum(row_max, chunk_max)
        weights = jnp.exp2(current * SCALE2 - new_max).astype(BF16)
        update = dot(v_aug[:, i * chunk : (i + 1) * chunk], weights, 1, 0)
        total = update if i == 0 else total * jnp.exp2(row_max - new_max) + update
        row_max = new_max
    denominator = total[HDIM : HDIM + 1, :]
    o_ref[...] = (total[:HDIM, :] / denominator).astype(BF16)
    lse_ref[...] = (row_max + jnp.log2(denominator))[None]


def attend(q_rot, k_parts, v_parts, bias_columns, first):
    width, rows = k_parts[0].shape
    parts = len(k_parts)
    span = parts * rows
    heads = width // HDIM
    q_rows = pick_block(rows, 768)
    chunk = pick_block(span, 512)
    q_spec = pl.BlockSpec((HDIM, q_rows), lambda h, j: (h + first, j))
    k_spec = pl.BlockSpec((HDIM, rows), lambda h, j: (h, 0))
    return pl.pallas_call(
        functools.partial(attend_kernel, parts, chunk),
        grid=(heads, rows // q_rows),
        in_specs=[q_spec, pl.BlockSpec((span, HDIM), lambda h, j: (0, 0))] + [k_spec] * (2 * parts),
        out_specs=[
            pl.BlockSpec((HDIM, q_rows), lambda h, j: (h, j)),
            pl.BlockSpec((1, 1, q_rows), lambda h, j: (h, 0, j)),
        ],
        out_shape=[
            jax.ShapeDtypeStruct((width, rows), BF16),
            jax.ShapeDtypeStruct((heads, 1, rows), F32),
        ],
        scratch_shapes=[
            pltpu.VMEM((span, 2 * HDIM), BF16),
            pltpu.VMEM((HDIM + 16, span), BF16),
            pltpu.VMEM((2 * HDIM, q_rows), BF16),
        ],
        compiler_params=pltpu.CompilerParams(vmem_limit_bytes=VMEM_LIMIT),
        cost_estimate=pl.CostEstimate(
            flops=16 * heads * rows * span * HDIM,
            bytes_accessed=2 * width * (2 * rows + 2 * span),
            transcendentals=heads * rows * span,
        ),
        name="attend",
    )(q_rot, bias_columns, *k_parts, *v_parts)


def in_three(values):
    first = values.astype(BF16)
    rest = values - first.astype(F32)
    second = rest.astype(BF16)
    return first.astype(F32), second.astype(F32), rest - second.astype(F32)


def unrotate(values, cosine, sine):
    low, high = values[:HALF], values[HALF:]
    return low * cosine + high * sine, high * cosine - low * sine


def attend_back_kernel(parts, chunk, *refs):
    q_ref, do_ref, o_ref, lse_ref, bias_ref, cos_ref, sin_ref = refs[:7]
    k_refs, v_refs = refs[7 : 7 + parts], refs[7 + parts : 7 + 2 * parts]
    dq_ref = refs[7 + 2 * parts]
    dk_refs = refs[8 + 2 * parts : 8 + 3 * parts]
    dv_refs = refs[8 + 3 * parts : 8 + 4 * parts]
    k_aug, v_aug, k_rows, q_aug, do_aug, dk_acc, dv_acc = refs[8 + 4 * parts :]
    head, block = pl.program_id(0), pl.program_id(1)
    span = k_aug.shape[1]
    part = span // parts
    q_rows = q_ref.shape[1]

    @pl.when((head == 0) & (block == 0))
    def _():
        row = lax.broadcasted_iota(jnp.int32, (HDIM, span), 0)
        ones = jnp.where(row < 4, 1.0, 0.0)
        k_aug[HDIM:, :] = jnp.where(row == 0, bias_ref[...], ones).astype(BF16)
        v_aug[HDIM:, :] = jnp.where(row < 3, 1.0, 0.0).astype(BF16)
        k_rows[:, HDIM:] = jnp.zeros((span, HDIM), BF16)

    @pl.when(block == 0)
    def _():
        for i in range(parts):
            at = slice(i * part, (i + 1) * part)
            keys = k_refs[i][...]
            k_aug[:HDIM, at] = keys
            v_aug[:HDIM, at] = v_refs[i][...]
            k_rows[at, :HDIM] = keys.T
        dk_acc[...] = jnp.zeros_like(dk_acc)
        dv_acc[...] = jnp.zeros_like(dv_acc)

    queries, d_heads = q_ref[...], do_ref[...]
    delta = jnp.sum(d_heads.astype(F32) * o_ref[...].astype(F32), axis=0, keepdims=True)
    row = lax.broadcasted_iota(jnp.int32, (HDIM, q_rows), 0)
    lse_a, lse_b, lse_c = in_three(lse_ref[0] * (-1.0 / SCALE2))
    del_a, del_b, del_c = in_three(-delta)
    q_extra = jnp.where(row == 2, lse_b, jnp.where(row == 3, lse_c, 0.0))
    q_extra = jnp.where(row == 0, 1.0, jnp.where(row == 1, lse_a, q_extra))
    do_extra = jnp.where(row == 1, del_b, jnp.where(row == 2, del_c, 0.0))
    do_extra = jnp.where(row == 0, del_a, do_extra)
    q_aug[:HDIM, :] = queries
    q_aug[HDIM:, :] = q_extra.astype(BF16)
    do_aug[:HDIM, :] = d_heads
    do_aug[HDIM:, :] = do_extra.astype(BF16)
    q_side, do_side = q_aug[...].T, do_aug[...].T
    count = span // chunk

    def products(i):
        at = slice(i * chunk, (i + 1) * chunk)
        return dot(q_side, k_aug[:, at], 1, 0), dot(do_side, v_aug[:, at], 1, 0)

    upcoming = products(0)
    d_query = None
    for i in range(count):
        at = slice(i * chunk, (i + 1) * chunk)
        scores, d_probs = upcoming
        if i + 1 < count:
            upcoming = products(i + 1)
        probs = jnp.exp2(scores * SCALE2)
        d_scores = (probs * d_probs).astype(BF16)
        dv_acc[:, at] += dot(d_heads, probs.astype(BF16), 1, 0)
        dk_acc[:, at] += dot(queries, d_scores, 1, 0)
        update = dot(d_scores, k_rows[at, :], 1, 0)
        d_query = update if i == 0 else d_query + update
    first = pl.multiple_of(block * q_rows, q_rows)
    low, high = unrotate(
        d_query.T[:HDIM, :] * SCALE, cos_ref[:, pl.ds(first, q_rows)], sin_ref[:, pl.ds(first, q_rows)]
    )
    dq_ref[:HALF, :] = low.astype(BF16)
    dq_ref[HALF:, :] = high.astype(BF16)

    @pl.when(block == pl.num_programs(1) - 1)
    def _():
        for i in range(parts):
            at = slice(i * part, (i + 1) * part)
            low, high = unrotate(dk_acc[:, at] * SCALE, cos_ref[:, at], sin_ref[:, at])
            dk_refs[i][:HALF, :] = low.astype(dk_refs[i].dtype)
            dk_refs[i][HALF:, :] = high.astype(dk_refs[i].dtype)
            dv_refs[i][...] = dv_acc[:, at].astype(dv_refs[i].dtype)


def attend_back(q_rot, k_parts, v_parts, d_heads, heads_out, lse, bias_row, cosine, sine, first, within, count):
    rows = q_rot.shape[1]
    parts = len(k_parts)
    span = parts * rows
    q_rows = pick_block(rows, 1536)
    chunk = pick_block(span, 256)
    q_spec = pl.BlockSpec((HDIM, q_rows), lambda h, j: (h + first, j))
    k_spec = pl.BlockSpec((HDIM, rows), lambda h, j: (h + within, 0))
    whole = lambda array: pl.BlockSpec(array.shape, lambda h, j: (0, 0))
    part_out = pl.BlockSpec((HDIM, rows), lambda h, j: (h, 0))
    shape = lambda kind: jax.ShapeDtypeStruct((count * HDIM, rows), kind)
    part_kinds = [F32] + [BF16] * (parts - 1)
    out = pl.pallas_call(
        functools.partial(attend_back_kernel, parts, chunk),
        grid=(count, rows // q_rows),
        in_specs=[
            q_spec,
            q_spec,
            pl.BlockSpec((HDIM, q_rows), lambda h, j: (h + within, j)),
            pl.BlockSpec((1, 1, q_rows), lambda h, j: (h + within, 0, j)),
            whole(bias_row),
            whole(cosine),
            whole(sine),
        ]
        + [k_spec] * (2 * parts),
        out_specs=[pl.BlockSpec((HDIM, q_rows), lambda h, j: (h, j))] + [part_out] * (2 * parts),
        out_shape=[shape(BF16)] + [shape(kind) for kind in part_kinds * 2],
        scratch_shapes=[
            pltpu.VMEM((2 * HDIM, span), BF16),
            pltpu.VMEM((2 * HDIM, span), BF16),
            pltpu.VMEM((span, 2 * HDIM), BF16),
            pltpu.VMEM((2 * HDIM, q_rows), BF16),
            pltpu.VMEM((2 * HDIM, q_rows), BF16),
            pltpu.VMEM((HDIM, span), F32),
            pltpu.VMEM((HDIM, span), F32),
        ],
        compiler_params=pltpu.CompilerParams(vmem_limit_bytes=VMEM_LIMIT),
        cost_estimate=pl.CostEstimate(
            flops=5 * count * rows * span * HDIM,
            bytes_accessed=0,
            transcendentals=0,
        ),
        name="attend_back",
    )(q_rot, d_heads, heads_out, lse, bias_row, cosine, sine, *k_parts, *v_parts)
    return out[0], out[1 : 1 + parts], out[1 + parts :]


def norm_parts(values):
    centered = values - jnp.mean(values, axis=-1, keepdims=True)
    scale = lax.rsqrt(jnp.mean(centered * centered, axis=-1, keepdims=True) + 1e-06)
    return centered * scale, scale


def norm_back(normed, scale, d_normed):
    return (
        d_normed
        - jnp.mean(d_normed, axis=-1, keepdims=True)
        - normed * jnp.mean(d_normed * normed, axis=-1, keepdims=True)
    ) * scale


def gelu_both(values):
    square = values * values
    bend = jnp.tanh(0.7978845608028654 * (values + 0.044715 * values * square))
    half = 0.5 * (1.0 + bend)
    slope = 0.7978845608028654 * (1.0 + 3 * 0.044715 * square)
    return values * half, half + 0.5 * values * (1.0 - bend * bend) * slope


def add_rows(values):
    return jnp.sum(values, axis=0, keepdims=True)


def store_rotated(out_ref, values, cosine, sine):
    for at in range(0, out_ref.shape[0], HDIM):
        low, high = values[at : at + HALF], values[at + HALF : at + HDIM]
        out_ref[at : at + HALF, :] = (low * cosine - high * sine).astype(BF16)
        out_ref[at + HALF : at + HDIM, :] = (high * cosine + low * sine).astype(BF16)


def either(first_ref, second_ref):
    half = pl.num_programs(0) // 2
    return jnp.where(pl.program_id(0) < half, first_ref[...], second_ref[...])


def halves_spec(inputs, rows, block, width):
    if inputs[0].shape[0] == rows:
        return [pl.BlockSpec((block, width), lambda i, *_: (i, 0))] * 2
    half = rows // 2 // block
    return [
        pl.BlockSpec((block, width), lambda i, *_: (jnp.minimum(i, half - 1), 0)),
        pl.BlockSpec((block, width), lambda i, *_: (jnp.maximum(i - half, 0), 0)),
    ]


def project_kv_kernel(groups, x_ref, y_ref, vectors_ref, w_ref, cos_ref, sin_ref, h_ref, *refs):
    k_refs, v_refs = refs[:groups], refs[groups:]
    width = x_ref.shape[1]
    tall = width // groups
    normed, _ = norm_parts(either(x_ref, y_ref).astype(F32))
    h_one = (normed * (1.0 + vectors_ref[1:2, :]) + vectors_ref[0:1, :]).astype(BF16)
    h_ref[...] = h_one
    keys = (dot(h_one, w_ref[:, :width], 1, 0) + vectors_ref[7:8, :]).T
    values = (dot(h_one, w_ref[:, width:], 1, 0) + vectors_ref[8:9, :]).astype(BF16).T
    for i in range(groups):
        store_rotated(k_refs[i], keys[i * tall : (i + 1) * tall], cos_ref[...], sin_ref[...])
        v_refs[i][...] = values[i * tall : (i + 1) * tall]


def project_q_kernel(h_ref, vectors_ref, w_ref, cos_ref, sin_ref, q_ref):
    queries = dot(h_ref[...], w_ref[...], 1, 0) + vectors_ref[6:7, :]
    store_rotated(q_ref, queries.T, cos_ref[...], sin_ref[...])


def whole_spec(shape, column=0):
    return pl.BlockSpec(shape, lambda i, *_: (0, column), pipeline_mode=pl.Buffered(1))


def project(inputs, vectors, packed, cosine, sine, groups):
    width, rows = inputs[0].shape[1], cosine.shape[1]
    block = pick_block(inputs[0].shape[0], 256)
    tall = width // groups
    row_spec = pl.BlockSpec((block, width), lambda i: (i, 0))
    turned_spec = lambda height: pl.BlockSpec((height, block), lambda i: (0, i))
    turned = lambda height: jax.ShapeDtypeStruct((height, rows), BF16)
    table_spec = turned_spec(HALF)
    params = pltpu.CompilerParams(vmem_limit_bytes=VMEM_LIMIT)
    out = pl.pallas_call(
        functools.partial(project_kv_kernel, groups),
        grid=(rows // block,),
        in_specs=halves_spec(inputs, rows, block, width)
        + [whole_spec(vectors.shape), whole_spec((width, 2 * width)), table_spec, table_spec],
        out_specs=[row_spec] + [turned_spec(tall)] * (2 * groups),
        out_shape=[jax.ShapeDtypeStruct((rows, width), BF16)] + [turned(tall)] * (2 * groups),
        compiler_params=params,
        cost_estimate=pl.CostEstimate(
            flops=8 * rows * width * width, bytes_accessed=8 * rows * width + 4 * width * width, transcendentals=0
        ),
        name="project_kv",
    )(*inputs, vectors, packed, cosine, sine)
    h_one, keys, values = out[0], out[1 : 1 + groups], out[1 + groups :]
    queries = pl.pallas_call(
        project_q_kernel,
        grid=(rows // block,),
        in_specs=[row_spec, whole_spec(vectors.shape), whole_spec((width, width), 2), table_spec, table_spec],
        out_specs=turned_spec(width),
        out_shape=turned(width),
        compiler_params=params,
        cost_estimate=pl.CostEstimate(
            flops=4 * rows * width * width, bytes_accessed=4 * rows * width + 2 * width * width, transcendentals=0
        ),
        name="project_q",
    )(h_one, vectors, packed, cosine, sine)
    return h_one, queries, keys, values


def feed_forward_kernel(parts, pieces, split, slot_ref, *refs):
    o_refs = refs[:parts]
    x_ref, y_ref, cot_ref, cot_y_ref, keep_ref, w_ref, vectors_ref = refs[parts : parts + 7]
    own_ref, away_ref, d_res_ref, d_heads_ref, g_rows_ref, sums_ref = refs[parts + 7 : parts + 13]
    acc, acc_rows, slope_ref, hidden_ref, staged, sems = refs[parts + 13 :]
    step, count = pl.program_id(0), pl.num_programs(0)
    width = x_ref.shape[1]

    @pl.when(step == 0)
    def _():
        acc[...] = jnp.zeros_like(acc)
        acc_rows[...] = jnp.zeros_like(acc_rows)

    gate_one, shift_two, scale_two, gate_two, b_out, b_down = [vectors_ref[i : i + 1, :] for i in (2, 3, 4, 5, 9, 10)]
    out_at = slice(0, width)
    up_at = [slice((1 + i) * width, (2 + i) * width) for i in range(pieces)]
    down_at = [slice((1 + pieces + i) * width, (2 + pieces + i) * width) for i in range(pieces)]
    keep = keep_ref[...]
    heads_out = jnp.concatenate([ref[...] for ref in o_refs], axis=0)
    branch = (dot(heads_out, w_ref[:, out_at], 0, 0) + b_out) * keep
    residual = either(x_ref, y_ref).astype(F32) + gate_one * branch
    normed, inverse = norm_parts(residual)
    h_two = (normed * (1.0 + scale_two) + shift_two).astype(BF16)
    ff_out = b_down
    for i in range(pieces):
        value, slope = gelu_both(dot(h_two, w_ref[:, up_at[i]], 1, 0) + vectors_ref[11 + i : 12 + i, :])
        slope_ref[i] = slope
        hidden = value.astype(BF16)
        hidden_ref[i] = hidden
        ff_out = ff_out + dot(hidden, w_ref[:, down_at[i]], 1, 0)
    mixed = (residual + gate_two * ff_out).astype(BF16)
    if split:

        @pl.when(step < count // 2)
        def _():
            own_ref[0] = mixed

        @pl.when(step >= count // 2)
        def _():
            away_ref[...] = mixed
    else:
        own_ref[...] = mixed
    d_mixed = either(cot_ref, cot_y_ref).astype(F32)
    acc_rows[3:4, :] += add_rows(d_mixed * ff_out)
    d_ff = (d_mixed * gate_two).astype(BF16)
    acc_rows[5:6, :] += add_rows(d_ff.astype(F32))
    d_h_two = None
    for i in range(pieces):
        acc[:, down_at[i]] += dot(hidden_ref[i], d_ff, 0, 0)
        d_up = (dot(d_ff, w_ref[:, down_at[i]], 1, 1) * slope_ref[i]).astype(BF16)
        acc_rows[6 + i : 7 + i, :] += add_rows(d_up.astype(F32))
        acc[:, up_at[i]] += dot(h_two, d_up, 0, 0)
        update = dot(d_up, w_ref[:, up_at[i]], 1, 1)
        d_h_two = update if i == 0 else d_h_two + update
    acc_rows[1:2, :] += add_rows(d_h_two)
    acc_rows[2:3, :] += add_rows(d_h_two * normed)
    d_residual = d_mixed + norm_back(normed, inverse, d_h_two * (1.0 + scale_two))
    d_res_ref[...] = d_residual
    acc_rows[0:1, :] += add_rows(d_residual * branch)
    d_branch = (d_residual * gate_one * keep).astype(BF16)
    acc_rows[4:5, :] += add_rows(d_branch.astype(F32))
    acc[:, out_at] += dot(heads_out, d_branch, 1, 0)
    d_heads_ref[...] = dot(w_ref[:, out_at], d_branch, 1, 1).astype(BF16)

    @pl.when(step == count - 1)
    def _():
        sums_ref[...] = acc_rows[...]
        tall = staged.shape[1]
        copies = []
        for i in range(width // tall):
            slot = i % 2
            if i >= 2:
                copies[i - 2].wait()
            staged[slot] = acc[i * tall : (i + 1) * tall, :].astype(BF16)
            copies.append(pltpu.make_async_copy(staged.at[slot], g_rows_ref.at[pl.ds(i * tall, tall), :], sems.at[slot]))
            copies[i].start()
        for copy in copies[-2:]:
            copy.wait()


def feed_forward(slot, inputs, heads_out, cotangent, keep, packed, vectors, slots):
    rows, width = heads_out[0].shape[1], inputs[0].shape[1]
    pieces = (packed.shape[1] // width - 1) // 2
    block = pick_block(inputs[0].shape[0], 256)
    local = rows // slots
    split = inputs[0].shape[0] == local
    half = local // block
    row_spec = pl.BlockSpec((block, width), lambda i, *_: (i, 0))
    turned_spec = lambda height: pl.BlockSpec((height, block), lambda i, *_: (0, i))
    kinds = jax.ShapeDtypeStruct
    if split:
        mixed_specs = [
            pl.BlockSpec((1, block, width), lambda i, at: (at[0], jnp.minimum(i, half - 1), 0)),
            pl.BlockSpec((block, width), lambda i, *_: (jnp.maximum(i - half, 0), 0)),
        ]
        mixed_shapes = [kinds((slots, local, width), BF16), kinds((local, width), BF16)]
    else:
        mixed_specs = [row_spec, whole_spec((8, 128))]
        mixed_shapes = [kinds((rows, width), BF16), kinds((8, 128), BF16)]
    return pl.pallas_call(
        functools.partial(feed_forward_kernel, len(heads_out), pieces, split),
        grid_spec=pltpu.PrefetchScalarGridSpec(
            num_scalar_prefetch=1,
            grid=(rows // block,),
            in_specs=[turned_spec(part.shape[0]) for part in heads_out]
            + halves_spec(inputs, rows, block, width) * 2
            + [
                pl.BlockSpec((block, 1), lambda i, *_: (i, 0)),
                whole_spec(packed.shape),
                whole_spec(vectors.shape),
            ],
            out_specs=mixed_specs
            + [
                row_spec,
                turned_spec(width),
                pl.BlockSpec(memory_space=pl.ANY),
                whole_spec((8, width)),
            ],
            scratch_shapes=[
                pltpu.VMEM(packed.shape, F32),
                pltpu.VMEM((8, width), F32),
                pltpu.VMEM((pieces, block, width), F32),
                pltpu.VMEM((pieces, block, width), BF16),
                pltpu.VMEM((2, pick_block(width, 256), packed.shape[1]), BF16),
                pltpu.SemaphoreType.DMA((2,)),
            ],
        ),
        out_shape=mixed_shapes
        + [
            kinds((rows, width), F32),
            kinds((width, rows), BF16),
            kinds(packed.shape, BF16),
            kinds((8, width), F32),
        ],
        compiler_params=pltpu.CompilerParams(vmem_limit_bytes=VMEM_LIMIT),
        cost_estimate=pl.CostEstimate(
            flops=6 * rows * width * packed.shape[1],
            bytes_accessed=8 * rows * width + 4 * width * packed.shape[1],
            transcendentals=0,
        ),
        name="feed_forward",
    )(slot, *heads_out, *inputs, *cotangent, keep, packed, vectors)


def weight_grads_kernel(parts, h_ref, dq_ref, *refs):
    dk_refs, dv_refs = refs[:parts], refs[parts : 2 * parts]
    dk_out, dv_out, weight_ref, bias_ref = refs[2 * parts :]

    def summed(pieces):
        total = pieces[0][...]
        for ref in pieces[1:]:
            total = total + ref[...].astype(F32)
        return total.astype(BF16)

    grads = [dq_ref[...], summed(dk_refs), summed(dv_refs)]
    dk_out[...] = grads[1]
    dv_out[...] = grads[2]
    weight_ref[...] = dot(jnp.concatenate(grads, axis=0), h_ref[...], 1, 0).T.astype(BF16)
    for i, grad in enumerate(grads):
        bias_ref[:, i : i + 1] = jnp.sum(grad.astype(F32), axis=1, keepdims=True)


def weight_grads(h_one, d_query, dk_parts, dv_parts):
    rows, width = h_one.shape
    tall = d_query.shape[0]
    block = pick_block(tall, 128)
    spec = pl.BlockSpec((block, rows), lambda i: (i, 0))
    kinds = jax.ShapeDtypeStruct
    parts = len(dk_parts)
    return pl.pallas_call(
        functools.partial(weight_grads_kernel, parts),
        grid=(tall // block,),
        in_specs=[whole_spec((rows, width))] + [spec] * (1 + 2 * parts),
        out_specs=[
            spec,
            spec,
            pl.BlockSpec((width, 3 * block), lambda i: (0, i)),
            pl.BlockSpec((block, 128), lambda i: (i, 0)),
        ],
        out_shape=[
            kinds((tall, rows), BF16),
            kinds((tall, rows), BF16),
            kinds((width, 3 * tall), BF16),
            kinds((tall, 128), F32),
        ],
        compiler_params=pltpu.CompilerParams(vmem_limit_bytes=VMEM_LIMIT),
        cost_estimate=pl.CostEstimate(flops=0, bytes_accessed=0, transcendentals=0),
        name="weight_grads",
    )(h_one, d_query, *dk_parts, *dv_parts)


def input_grads_kernel(counts, slot_ref, x_ref, d_res_ref, vectors_ref, w_ref, *refs):
    grad_refs, (out_ref, sums_ref) = refs[:-2], refs[-2:]
    width = x_ref.shape[1]

    @pl.when(pl.program_id(0) == 0)
    def _():
        sums_ref[...] = jnp.zeros_like(sums_ref)

    turned = None
    used = 0
    for kind in range(3):
        first = (2, 0, 1)[kind] * width
        grad = jnp.concatenate([ref[...] for ref in grad_refs[used : used + counts[kind]]], axis=0)
        used += counts[kind]
        update = dot(w_ref[:, first : first + width], grad, 1, 0)
        turned = update if turned is None else turned + update
    d_h_one = turned.T
    normed, inverse = norm_parts(x_ref[...].astype(F32))
    sums_ref[0:1, :] += add_rows(d_h_one)
    sums_ref[1:2, :] += add_rows(d_h_one * normed)
    grad = (d_res_ref[...] + norm_back(normed, inverse, d_h_one * (1.0 + vectors_ref[1:2, :]))).astype(BF16)
    out_ref[...] = grad.reshape(out_ref.shape)


def input_grads(slot, slots, inputs, half, d_residual, vectors, packed, grads):
    rows, width = inputs.shape
    block = pick_block(rows, 256)
    first = half * (rows // block)
    row_spec = pl.BlockSpec((block, width), lambda i, *_: (i, 0))
    flat = [grad for kind in grads for grad in kind]
    out_spec, out_shape = row_spec, (rows, width)
    if slots:
        out_spec = pl.BlockSpec((1, block, width), lambda i, at: (at[0], i, 0))
        out_shape = (slots, rows, width)
    return pl.pallas_call(
        functools.partial(input_grads_kernel, [len(kind) for kind in grads]),
        grid_spec=pltpu.PrefetchScalarGridSpec(
            num_scalar_prefetch=1,
            grid=(rows // block,),
            in_specs=[
                row_spec,
                pl.BlockSpec((block, width), lambda i, *_: (i + first, 0)),
                whole_spec(vectors.shape),
                whole_spec((width, 3 * width)),
            ]
            + [pl.BlockSpec((grad.shape[0], block), lambda i, *_: (0, i + first)) for grad in flat],
            out_specs=[out_spec, whole_spec((8, width))],
        ),
        out_shape=[jax.ShapeDtypeStruct(out_shape, BF16), jax.ShapeDtypeStruct((8, width), F32)],
        compiler_params=pltpu.CompilerParams(vmem_limit_bytes=VMEM_LIMIT),
        cost_estimate=pl.CostEstimate(
            flops=16 * rows * width * width, bytes_accessed=14 * rows * width + 6 * width * width, transcendentals=0
        ),
        name="input_grads",
    )(slot, inputs, d_residual, vectors, packed, *flat)


def time_features(t_index, model_width):
    half_width = model_width // 2
    indices = jnp.arange(half_width).astype(F32)
    frequency = jnp.exp(indices * (-math.log(10000.0) / (half_width - 1)))
    angles = t_index.astype(F32)[:, None] * frequency[None, :]
    return jnp.concatenate([jnp.sin(angles), jnp.cos(angles)], axis=1)


def rotary_tables(places):
    inverse = jnp.exp(jnp.arange(HALF).astype(F32) * (-2.0 * math.log(10000.0) / HDIM))
    angles = inverse[:, None] * places.astype(F32)[None, :]
    return jnp.cos(angles), jnp.sin(angles)


def after(values, *others):
    return lax.optimization_barrier((values,) + others)[0] if others else values


def make_body(mesh):
    n_dp, n_fsdp = mesh.shape["dp"], mesh.shape["fsdp"]
    n_pairs = n_fsdp // 2

    def shift(values, axis, size, by):
        return lax.ppermute(values, axis, [(i, (i + by) % size) for i in range(size)])

    def pick(values, index, axis=0):
        return lax.dynamic_index_in_dim(values, index, axis, keepdims=False)

    def body(
        frames,
        lengths,
        t_index,
        w_ada,
        b_ada,
        w_query,
        b_query,
        w_key,
        b_key,
        w_value,
        b_value,
        w_out,
        b_out,
        w_up,
        b_up,
        w_down,
        b_down,
        grad_out,
    ):
        slots, local, width = frames.shape
        group = n_fsdp // slots
        hidden_width = w_up.shape[1]
        shard = w_query.shape[0]
        ada_width = w_ada.shape[1]
        dp, fsdp = lax.axis_index("dp"), lax.axis_index("fsdp")
        me = dp * n_fsdp + fsdp
        slot, place = fsdp // group, fsdp % group
        other = 1 - slot
        core, pair = fsdp % 2, fsdp // 2
        side, deep, far = dp % 2, dp // 2, n_dp // 2
        length = pick(lengths, slot)

        def picked(values):
            return pick(values, slot), pick(values, other)

        split = local % 128 == 0

        def swap_in(own, away):
            parts = own, shift(away, "fsdp", n_fsdp, group)
            return parts if split else (jnp.concatenate(parts),) * 2

        def swap_out(away, pieces=1):
            arrived = []
            for first in range(0, local, local // pieces):
                arrived.append(shift(away[first : first + local // pieces], "fsdp", n_fsdp, group))
            return arrived

        def placed_away(whole, arrived):
            first = 0
            for piece in arrived:
                whole = lax.dynamic_update_slice(whole, piece[None], (other, first, 0))
                first += piece.shape[0]
            return whole

        def placed_own(own):
            return lax.dynamic_update_index_in_dim(jnp.zeros((slots, local, width), own.dtype), own, slot, 0)

        def places_of(member):
            at = slot * group + member
            blocks = [((at - by * group) + n_fsdp) % n_fsdp for by in range(slots)]
            return jnp.concatenate([b * local + jnp.arange(local, dtype=jnp.int32) for b in blocks])

        ring = lambda by: [(i, (i // group) * group + (i % group + by) % group) for i in range(n_fsdp)]

        def swap(values, axis, size):
            return lax.ppermute(values, axis, [(i, i ^ 1) for i in range(size)])

        def sum_core(values, *others):
            values = values.reshape(n_dp, n_pairs, 2, shard, values.shape[1])
            arrived = after(swap(pick(values, 1 - core, 2), "fsdp", n_fsdp), *others)
            return pick(values, core, 2).astype(F32) + arrived.astype(F32)

        def sum_pairs(values, *others):
            axis = values.ndim - 3
            total = pick(values, pair, axis).astype(F32)
            for by in range(1, n_pairs):
                arrived = after(shift(pick(values, (pair + by) % n_pairs, axis), "fsdp", n_fsdp, 2 * by), *others)
                total = total + arrived.astype(F32)
            return total

        def sum_side(values, *others):
            values = values.reshape((far, 2) + values.shape[1:])
            arrived = after(swap(pick(values, 1 - side, 1), "dp", n_dp), *others)
            return pick(values, side, 1).astype(F32) + arrived.astype(F32)

        def sum_far(values, *others):
            total = pick(values, deep).astype(F32)
            for by in range(1, far):
                arrived = after(shift(pick(values, (deep + by) % far), "dp", n_dp, 2 * by), *others)
                total = total + arrived.astype(F32)
            return total

        def gather_dp(values):
            values = jnp.stack([values] + [shift(values, "dp", n_dp, 2 * by) for by in range(1, far)])
            return jnp.stack([values, swap(values, "dp", n_dp)])

        packed = lax.all_gather(jnp.concatenate([w_key, w_value, w_query], axis=1), AXES, axis=0, tiled=True)
        ups = hidden_width // width
        w_up_turned = w_up.reshape(shard, n_dp * n_fsdp, ups, shard).swapaxes(1, 2).reshape(w_up.shape)
        downs = [w_down[i * shard : (i + 1) * shard] for i in range(ups)]
        packed_two = lax.all_gather(jnp.concatenate([w_out, w_up_turned, *downs], axis=1), AXES, axis=0, tiled=True)

        inputs = swap_in(*picked(frames))
        rows = slots * local
        own_grad, away_grad = picked(grad_out)

        t_all = gather_dp(t_index).reshape(-1)
        active = jax.nn.silu(time_features(t_all, width)).astype(BF16)
        active_mine = lax.dynamic_slice_in_dim(active, me * shard, shard, axis=1)
        partial = [dot(active_mine, w_ada, 1, 0)]
        for bias in (b_query, b_key, b_value, b_out, b_down, *jnp.split(b_up, ups)):
            size = bias.shape[0]
            zeros = jnp.zeros((1, size * n_dp * n_fsdp), F32)
            placed = lax.dynamic_update_slice_in_dim(zeros, bias.astype(F32)[None], me * size, axis=1)
            partial.append(jnp.broadcast_to(placed, (n_dp * slots, placed.shape[1])))
        placed = lax.dynamic_update_slice_in_dim(
            jnp.zeros((1, ada_width), F32), b_ada.astype(F32)[None], me * b_ada.shape[0], axis=1
        )
        partial[0] = partial[0] + placed
        partial = jnp.concatenate(partial, axis=1).reshape(2, far, slots, -1)
        partial = partial[0] + swap(partial[1], "dp", n_dp)
        summed = partial[0]
        for by in range(1, far):
            summed = summed + shift(partial[by], "dp", n_dp, -2 * by)
        one = pick(summed, slot) + shift(pick(summed, other), "fsdp", n_fsdp, group)
        vectors = one
        for by in range(1, group):
            vectors = vectors + lax.ppermute(one, "fsdp", ring(by))
        vectors = vectors.reshape(-1, width)
        vectors = jnp.pad(vectors, ((0, -vectors.shape[0] % 8), (0, 0)))

        key_places = jnp.concatenate([places_of((place - by + group) % group) for by in range(group)])
        cosine, sine = rotary_tables(key_places)
        key_bias = jnp.where(key_places < length, 0.0, -1e30)
        bias_columns = jnp.pad(key_bias.astype(BF16)[:, None], ((0, 0), (0, HDIM - 1)))
        keep = (key_places[:rows] < length).astype(F32)[:, None]

        wide = 2
        vectors, cosine, sine, key_bias, bias_columns, keep, own_grad, away_grad = lax.optimization_barrier(
            (vectors, cosine, sine, key_bias, bias_columns, keep, own_grad, away_grad)
        )
        h_one, q_rot, keys, values = project(inputs, vectors, packed, cosine[:, :rows], sine[:, :rows], wide)
        cotangent = swap_in(own_grad, after(away_grad, keys[0]))
        heads = width // HDIM
        tall = heads // wide
        with_ring = lambda own: [own] + [lax.ppermute(own, "fsdp", ring(by)) for by in range(1, group)]
        k_parts, v_parts = [with_ring(own) for own in keys], [with_ring(own) for own in values]
        heads_out, lses = [], []
        for at in range(wide):
            out, lse = attend(q_rot, k_parts[at], v_parts[at], bias_columns, at * tall)
            heads_out.append(out)
            lses.append(lse)
        at_slot = slot.reshape(1).astype(jnp.int32)
        mixed, away_mixed, d_residual, d_heads, g_rows, sums_two = feed_forward(
            at_slot, inputs, heads_out, cotangent, keep, packed_two, vectors, slots
        )
        if not split:
            mixed, away_mixed = placed_own(mixed[:local]), mixed[local:]
        mixed_arrived = swap_out(away_mixed)

        sum_rows = lax.psum_scatter(g_rows, AXES, scatter_dimension=0, tiled=True).astype(F32)

        grads, d_biases, weight_sums = ([], [], []), [], []

        def sum_parts(pieces):
            sums = [weight_grads(h_one, *piece) for piece in pieces]
            for piece, (dk, dv, _, bias_grad) in zip(pieces, sums):
                for kind, grad in zip(grads, (piece[0], dk, dv)):
                    kind.append(grad)
                d_biases.append(bias_grad[:, :3])
            return [values[2] for values in sums]

        counts = (tall, tall // 4, tall // 4, tall // 2)
        first, ready, arrived, moving = 0, d_heads, [], None
        for step, each in enumerate(counts):
            part, within = first // tall, first % tall
            dq, dk_parts, dv_parts = attend_back(
                q_rot,
                k_parts[part],
                v_parts[part],
                ready,
                heads_out[part],
                lses[part],
                key_bias[None],
                cosine,
                sine,
                first,
                within,
                each,
            )
            first += each
            dk_parts = [dk_parts[0]] + [lax.ppermute(dk_parts[by], "fsdp", ring(-by)) for by in range(1, group)]
            dv_parts = [dv_parts[0]] + [lax.ppermute(dv_parts[by], "fsdp", ring(-by)) for by in range(1, group)]
            arrived.append((dq, dk_parts, dv_parts))
            if step == 1:
                arrived[0][1][0] = after(arrived[0][1][0], dq)
                weight_sums += sum_parts([arrived[0]])
                moving = sum_core(weight_sums[0]).astype(BF16)
                ready = after(d_heads, dq, weight_sums[0], *mixed_arrived)
            if step == 2:
                arrived[1][1][0] = after(arrived[1][1][0], dq)
                moving = after(moving, dq)
                ready = after(d_heads, dq, moving)
        early_sum = sum_pairs(moving, dq).astype(BF16)
        arrived[2][1][0] = after(arrived[2][1][0], dq)
        weight_sums += sum_parts(arrived[1:3])
        arrived[3][1][0] = after(arrived[3][1][0], weight_sums[2], sum_rows)
        weight_sums += sum_parts(arrived[3:])
        early_sum = sum_side(early_sum, weight_sums[3]).astype(BF16)
        if split:
            rest = after(d_residual, weight_sums[3], early_sum)
            away_frames, sums_away = input_grads(at_slot, 0, inputs[1], 1, rest, vectors, packed, grads)
            core_sums = [sum_core(values, away_frames) for values in weight_sums[1:]]
            core_sums = jnp.concatenate(core_sums, axis=-1).astype(BF16)
            rest, away_frames, core_sums = lax.optimization_barrier((d_residual, away_frames, core_sums))
            own_frames, sums_own = input_grads(at_slot, slots, inputs[0], 0, rest, vectors, packed, grads)
            sums_one = sums_own + sums_away
        else:
            core_sums = jnp.concatenate([sum_core(values) for values in weight_sums[1:]], axis=-1).astype(BF16)
            both, sums_one = input_grads(at_slot, 0, inputs[0], 0, d_residual, vectors, packed, grads)
            own_frames, away_frames = placed_own(both[:local]), both[local:]
        frames_arrived = swap_out(away_frames, 3)
        side_sums = sum_side(core_sums).astype(BF16)

        vector = jnp.concatenate(
            [sums_one[:2], sums_two[: 6 + ups], jnp.concatenate(d_biases).T]
        )
        for_slot = 6
        vector = after(vector, *frames_arrived[:2])
        total = vector
        for by in range(1, group):
            total = total + lax.ppermute(vector, "fsdp", ring(by))
        total, side_sums = lax.optimization_barrier((total, side_sums))
        all_sums = sum_far(jnp.concatenate([early_sum[:, None], side_sums], axis=1))
        sums = [all_sums[0], sum_pairs(all_sums[1:].astype(BF16))]
        sum_rows, mixed = after(sum_rows, total), after(mixed, total)
        g_out = sum_rows[:, :width]
        g_up = sum_rows[:, width : width + hidden_width].reshape(shard, ups, n_dp * n_fsdp, shard)
        g_up = g_up.swapaxes(1, 2).reshape(w_up.shape)
        g_down = jnp.concatenate([sum_rows[:, (1 + ups + i) * width : (2 + ups + i) * width] for i in range(ups)])
        mixed = placed_away(mixed, mixed_arrived)
        packs = gather_dp(total).reshape(n_dp, -1, width)
        pack = jnp.concatenate([packs[:, :for_slot].reshape(-1, width), jnp.sum(packs[:, for_slot:], axis=0)])
        pack, g_out, g_up, g_down, mixed, _ = lax.optimization_barrier(
            (pack, g_out, g_up, g_down, mixed, frames_arrived[2])
        )
        grad_frames = placed_away(own_frames, frames_arrived)
        across = shift(pack, "fsdp", n_fsdp, group)
        count = n_dp * for_slot
        d_mod = jnp.stack([jnp.where(slot == s, pack[:count], across[:count]).reshape(n_dp, -1) for s in range(slots)], axis=1)
        d_mod = d_mod.reshape(n_dp * slots, for_slot * width)
        d_vectors = pack[count:] + across[count:]

        g_w_ada = lax.dot_general(
            active_mine.astype(F32),
            d_mod,
            (((0,), (0,)), ((), ())),
            precision=lax.Precision.HIGHEST,
            preferred_element_type=F32,
        )

        def mine(vector):
            vector = vector.reshape(-1)
            size = vector.shape[0] // (n_dp * n_fsdp)
            return lax.dynamic_slice_in_dim(vector, me * size, size)

        columns = jnp.concatenate(sums, axis=1).reshape(shard, -1, 3, pick_block(tall // 2 * HDIM, 128))
        g_qkv = [columns[:, :, i].reshape(shard, width) for i in range(3)]
        return (
            mixed,
            grad_frames,
            g_w_ada,
            mine(jnp.sum(d_mod, axis=0)),
            g_qkv[0],
            mine(d_vectors[2 + ups]),
            g_qkv[1],
            mine(d_vectors[3 + ups]),
            g_qkv[2],
            mine(d_vectors[4 + ups]),
            g_out,
            mine(d_vectors[0]),
            g_up,
            jnp.concatenate([mine(d_vectors[2 + i]) for i in range(ups)]),
            g_down,
            mine(d_vectors[1]),
        )

    return body


def solution(mesh):
    rows, vector, matrix = P("dp", "fsdp", None), P(AXES), P(AXES, None)
    return jax.shard_map(
        make_body(mesh),
        mesh=mesh,
        in_specs=(rows, P("dp"), P("dp")) + (matrix, vector) * 7 + (rows,),
        out_specs=(rows, rows) + (matrix, vector) * 7,
        check_vma=False,
    )
```

```python
import functools
import math

import jax
import jax.numpy as jnp
from jax import lax
from jax.experimental import pallas as pl
from jax.experimental.pallas import tpu as pltpu
from jax.sharding import PartitionSpec as P

HDIM = 64
HALF = HDIM // 2
SCALE = HDIM ** (-0.5)
SCALE2 = SCALE * math.log2(math.e)
AXES = ("dp", "fsdp")
VMEM_LIMIT = 62 << 20
F32 = jnp.float32
BF16 = jnp.bfloat16


def dot(left_side, right_side, left_dim, right_dim):
    return lax.dot_general(
        left_side,
        right_side,
        (((left_dim,), (right_dim,)), ((), ())),
        preferred_element_type=F32,
    )


def pick_block(total, wanted):
    block = min(total, wanted)
    while total % block:
        block -= 128
    return block


def attend_kernel(parts, chunk, *refs):
    q_ref, bias_ref = refs[0], refs[1]
    k_refs, v_refs = refs[2 : 2 + parts], refs[2 + parts : 2 + 2 * parts]
    o_ref, lse_ref, k_aug, v_aug, q_aug = refs[2 + 2 * parts :]
    head, block = pl.program_id(0), pl.program_id(1)
    span = k_aug.shape[0]
    part = span // parts
    q_rows = q_ref.shape[1]

    @pl.when((head == 0) & (block == 0))
    def _():
        k_aug[:, HDIM:] = bias_ref[...]
        v_aug[HDIM:, :] = jnp.ones((16, span), BF16)
        q_aug[HDIM:, :] = jnp.ones((HDIM, q_rows), BF16)

    @pl.when(block == 0)
    def _():
        for i in range(parts):
            k_aug[i * part : (i + 1) * part, :HDIM] = k_refs[i][...].T
            v_aug[:HDIM, i * part : (i + 1) * part] = v_refs[i][...]

    q_aug[:HDIM, :] = q_ref[...]
    queries = q_aug[...]
    count = span // chunk

    def scores(i):
        return dot(k_aug[i * chunk : (i + 1) * chunk, :], queries, 1, 0)

    upcoming = scores(0)
    row_max = total = None
    for i in range(count):
        current = upcoming
        if i + 1 < count:
            upcoming = scores(i + 1)
        chunk_max = jnp.max(current, axis=0, keepdims=True) * SCALE2
        new_max = chunk_max if i == 0 else jnp.maximum(row_max, chunk_max)
        weights = jnp.exp2(current * SCALE2 - new_max).astype(BF16)
        update = dot(v_aug[:, i * chunk : (i + 1) * chunk], weights, 1, 0)
        total = update if i == 0 else total * jnp.exp2(row_max - new_max) + update
        row_max = new_max
    denominator = total[HDIM : HDIM + 1, :]
    o_ref[...] = (total[:HDIM, :] / denominator).astype(BF16)
    lse_ref[...] = (row_max + jnp.log2(denominator))[None]


def attend(q_rot, k_parts, v_parts, bias_columns, first):
    width, rows = k_parts[0].shape
    parts = len(k_parts)
    span = parts * rows
    heads = width // HDIM
    q_rows = pick_block(rows, 768)
    chunk = pick_block(span, 512)
    q_spec = pl.BlockSpec((HDIM, q_rows), lambda h, j: (h + first, j))
    k_spec = pl.BlockSpec((HDIM, rows), lambda h, j: (h, 0))
    return pl.pallas_call(
        functools.partial(attend_kernel, parts, chunk),
        grid=(heads, rows // q_rows),
        in_specs=[q_spec, pl.BlockSpec((span, HDIM), lambda h, j: (0, 0))] + [k_spec] * (2 * parts),
        out_specs=[
            pl.BlockSpec((HDIM, q_rows), lambda h, j: (h, j)),
            pl.BlockSpec((1, 1, q_rows), lambda h, j: (h, 0, j)),
        ],
        out_shape=[
            jax.ShapeDtypeStruct((width, rows), BF16),
            jax.ShapeDtypeStruct((heads, 1, rows), F32),
        ],
        scratch_shapes=[
            pltpu.VMEM((span, 2 * HDIM), BF16),
            pltpu.VMEM((HDIM + 16, span), BF16),
            pltpu.VMEM((2 * HDIM, q_rows), BF16),
        ],
        compiler_params=pltpu.CompilerParams(vmem_limit_bytes=VMEM_LIMIT),
        cost_estimate=pl.CostEstimate(
            flops=16 * heads * rows * span * HDIM,
            bytes_accessed=2 * width * (2 * rows + 2 * span),
            transcendentals=heads * rows * span,
        ),
        name="attend",
    )(q_rot, bias_columns, *k_parts, *v_parts)


def in_three(values):
    first = values.astype(BF16)
    rest = values - first.astype(F32)
    second = rest.astype(BF16)
    return first.astype(F32), second.astype(F32), rest - second.astype(F32)


def unrotate(values, cosine, sine):
    low, high = values[:HALF], values[HALF:]
    return low * cosine + high * sine, high * cosine - low * sine


def attend_back_kernel(parts, chunk, *refs):
    q_ref, do_ref, o_ref, lse_ref, bias_ref, cos_ref, sin_ref = refs[:7]
    k_refs, v_refs = refs[7 : 7 + parts], refs[7 + parts : 7 + 2 * parts]
    dq_ref = refs[7 + 2 * parts]
    dk_refs = refs[8 + 2 * parts : 8 + 3 * parts]
    dv_refs = refs[8 + 3 * parts : 8 + 4 * parts]
    k_aug, v_aug, k_rows, q_aug, do_aug, dk_acc, dv_acc = refs[8 + 4 * parts :]
    head, block = pl.program_id(0), pl.program_id(1)
    span = k_aug.shape[1]
    part = span // parts
    q_rows = q_ref.shape[1]

    @pl.when((head == 0) & (block == 0))
    def _():
        row = lax.broadcasted_iota(jnp.int32, (HDIM, span), 0)
        ones = jnp.where(row < 4, 1.0, 0.0)
        k_aug[HDIM:, :] = jnp.where(row == 0, bias_ref[...], ones).astype(BF16)
        v_aug[HDIM:, :] = jnp.where(row < 3, 1.0, 0.0).astype(BF16)
        k_rows[:, HDIM:] = jnp.zeros((span, HDIM), BF16)

    @pl.when(block == 0)
    def _():
        for i in range(parts):
            at = slice(i * part, (i + 1) * part)
            keys = k_refs[i][...]
            k_aug[:HDIM, at] = keys
            v_aug[:HDIM, at] = v_refs[i][...]
            k_rows[at, :HDIM] = keys.T
        dk_acc[...] = jnp.zeros_like(dk_acc)
        dv_acc[...] = jnp.zeros_like(dv_acc)

    queries, d_heads = q_ref[...], do_ref[...]
    delta = jnp.sum(d_heads.astype(F32) * o_ref[...].astype(F32), axis=0, keepdims=True)
    row = lax.broadcasted_iota(jnp.int32, (HDIM, q_rows), 0)
    lse_a, lse_b, lse_c = in_three(lse_ref[0] * (-1.0 / SCALE2))
    del_a, del_b, del_c = in_three(-delta)
    q_extra = jnp.where(row == 2, lse_b, jnp.where(row == 3, lse_c, 0.0))
    q_extra = jnp.where(row == 0, 1.0, jnp.where(row == 1, lse_a, q_extra))
    do_extra = jnp.where(row == 1, del_b, jnp.where(row == 2, del_c, 0.0))
    do_extra = jnp.where(row == 0, del_a, do_extra)
    q_aug[:HDIM, :] = queries
    q_aug[HDIM:, :] = q_extra.astype(BF16)
    do_aug[:HDIM, :] = d_heads
    do_aug[HDIM:, :] = do_extra.astype(BF16)
    q_side, do_side = q_aug[...].T, do_aug[...].T
    count = span // chunk

    def products(i):
        at = slice(i * chunk, (i + 1) * chunk)
        return dot(q_side, k_aug[:, at], 1, 0), dot(do_side, v_aug[:, at], 1, 0)

    upcoming = products(0)
    d_query = None
    for i in range(count):
        at = slice(i * chunk, (i + 1) * chunk)
        scores, d_probs = upcoming
        if i + 1 < count:
            upcoming = products(i + 1)
        probs = jnp.exp2(scores * SCALE2)
        d_scores = (probs * d_probs).astype(BF16)
        dv_acc[:, at] += dot(d_heads, probs.astype(BF16), 1, 0)
        dk_acc[:, at] += dot(queries, d_scores, 1, 0)
        update = dot(d_scores, k_rows[at, :], 1, 0)
        d_query = update if i == 0 else d_query + update
    first = pl.multiple_of(block * q_rows, q_rows)
    low, high = unrotate(
        d_query.T[:HDIM, :] * SCALE, cos_ref[:, pl.ds(first, q_rows)], sin_ref[:, pl.ds(first, q_rows)]
    )
    dq_ref[:HALF, :] = low.astype(BF16)
    dq_ref[HALF:, :] = high.astype(BF16)

    @pl.when(block == pl.num_programs(1) - 1)
    def _():
        for i in range(parts):
            at = slice(i * part, (i + 1) * part)
            low, high = unrotate(dk_acc[:, at] * SCALE, cos_ref[:, at], sin_ref[:, at])
            dk_refs[i][:HALF, :] = low.astype(dk_refs[i].dtype)
            dk_refs[i][HALF:, :] = high.astype(dk_refs[i].dtype)
            dv_refs[i][...] = dv_acc[:, at].astype(dv_refs[i].dtype)


def attend_back(q_rot, k_parts, v_parts, d_heads, heads_out, lse, bias_row, cosine, sine, first, within, count):
    rows = q_rot.shape[1]
    parts = len(k_parts)
    span = parts * rows
    q_rows = pick_block(rows, 1536)
    chunk = pick_block(span, 256)
    q_spec = pl.BlockSpec((HDIM, q_rows), lambda h, j: (h + first, j))
    k_spec = pl.BlockSpec((HDIM, rows), lambda h, j: (h + within, 0))
    whole = lambda array: pl.BlockSpec(array.shape, lambda h, j: (0, 0))
    part_out = pl.BlockSpec((HDIM, rows), lambda h, j: (h, 0))
    shape = lambda kind: jax.ShapeDtypeStruct((count * HDIM, rows), kind)
    part_kinds = [F32] + [BF16] * (parts - 1)
    out = pl.pallas_call(
        functools.partial(attend_back_kernel, parts, chunk),
        grid=(count, rows // q_rows),
        in_specs=[
            q_spec,
            q_spec,
            pl.BlockSpec((HDIM, q_rows), lambda h, j: (h + within, j)),
            pl.BlockSpec((1, 1, q_rows), lambda h, j: (h + within, 0, j)),
            whole(bias_row),
            whole(cosine),
            whole(sine),
        ]
        + [k_spec] * (2 * parts),
        out_specs=[pl.BlockSpec((HDIM, q_rows), lambda h, j: (h, j))] + [part_out] * (2 * parts),
        out_shape=[shape(BF16)] + [shape(kind) for kind in part_kinds * 2],
        scratch_shapes=[
            pltpu.VMEM((2 * HDIM, span), BF16),
            pltpu.VMEM((2 * HDIM, span), BF16),
            pltpu.VMEM((span, 2 * HDIM), BF16),
            pltpu.VMEM((2 * HDIM, q_rows), BF16),
            pltpu.VMEM((2 * HDIM, q_rows), BF16),
            pltpu.VMEM((HDIM, span), F32),
            pltpu.VMEM((HDIM, span), F32),
        ],
        compiler_params=pltpu.CompilerParams(vmem_limit_bytes=VMEM_LIMIT),
        cost_estimate=pl.CostEstimate(
            flops=5 * count * rows * span * HDIM,
            bytes_accessed=0,
            transcendentals=0,
        ),
        name="attend_back",
    )(q_rot, d_heads, heads_out, lse, bias_row, cosine, sine, *k_parts, *v_parts)
    return out[0], out[1 : 1 + parts], out[1 + parts :]


def norm_parts(values):
    centered = values - jnp.mean(values, axis=-1, keepdims=True)
    scale = lax.rsqrt(jnp.mean(centered * centered, axis=-1, keepdims=True) + 1e-06)
    return centered * scale, scale


def norm_back(normed, scale, d_normed):
    return (
        d_normed
        - jnp.mean(d_normed, axis=-1, keepdims=True)
        - normed * jnp.mean(d_normed * normed, axis=-1, keepdims=True)
    ) * scale


def gelu_both(values):
    square = values * values
    bend = jnp.tanh(0.7978845608028654 * (values + 0.044715 * values * square))
    half = 0.5 * (1.0 + bend)
    slope = 0.7978845608028654 * (1.0 + 3 * 0.044715 * square)
    return values * half, half + 0.5 * values * (1.0 - bend * bend) * slope


def add_rows(values):
    return jnp.sum(values, axis=0, keepdims=True)


def store_rotated(out_ref, values, cosine, sine):
    for at in range(0, out_ref.shape[0], HDIM):
        low, high = values[at : at + HALF], values[at + HALF : at + HDIM]
        out_ref[at : at + HALF, :] = (low * cosine - high * sine).astype(BF16)
        out_ref[at + HALF : at + HDIM, :] = (high * cosine + low * sine).astype(BF16)


def either(first_ref, second_ref):
    half = pl.num_programs(0) // 2
    return jnp.where(pl.program_id(0) < half, first_ref[...], second_ref[...])


def halves_spec(inputs, rows, block, width):
    if inputs[0].shape[0] == rows:
        return [pl.BlockSpec((block, width), lambda i, *_: (i, 0))] * 2
    half = rows // 2 // block
    return [
        pl.BlockSpec((block, width), lambda i, *_: (jnp.minimum(i, half - 1), 0)),
        pl.BlockSpec((block, width), lambda i, *_: (jnp.maximum(i - half, 0), 0)),
    ]


def project_kv_kernel(groups, x_ref, y_ref, vectors_ref, w_ref, cos_ref, sin_ref, h_ref, *refs):
    k_refs, v_refs = refs[:groups], refs[groups:]
    width = x_ref.shape[1]
    tall = width // groups
    normed, _ = norm_parts(either(x_ref, y_ref).astype(F32))
    h_one = (normed * (1.0 + vectors_ref[1:2, :]) + vectors_ref[0:1, :]).astype(BF16)
    h_ref[...] = h_one
    keys = (dot(h_one, w_ref[:, :width], 1, 0) + vectors_ref[7:8, :]).T
    values = (dot(h_one, w_ref[:, width:], 1, 0) + vectors_ref[8:9, :]).astype(BF16).T
    for i in range(groups):
        store_rotated(k_refs[i], keys[i * tall : (i + 1) * tall], cos_ref[...], sin_ref[...])
        v_refs[i][...] = values[i * tall : (i + 1) * tall]


def project_q_kernel(h_ref, vectors_ref, w_ref, cos_ref, sin_ref, q_ref):
    queries = dot(h_ref[...], w_ref[...], 1, 0) + vectors_ref[6:7, :]
    store_rotated(q_ref, queries.T, cos_ref[...], sin_ref[...])


def whole_spec(shape, column=0):
    return pl.BlockSpec(shape, lambda i, *_: (0, column), pipeline_mode=pl.Buffered(1))


def project(inputs, vectors, packed, cosine, sine, groups):
    width, rows = inputs[0].shape[1], cosine.shape[1]
    block = pick_block(inputs[0].shape[0], 256)
    tall = width // groups
    row_spec = pl.BlockSpec((block, width), lambda i: (i, 0))
    turned_spec = lambda height: pl.BlockSpec((height, block), lambda i: (0, i))
    turned = lambda height: jax.ShapeDtypeStruct((height, rows), BF16)
    table_spec = turned_spec(HALF)
    params = pltpu.CompilerParams(vmem_limit_bytes=VMEM_LIMIT)
    out = pl.pallas_call(
        functools.partial(project_kv_kernel, groups),
        grid=(rows // block,),
        in_specs=halves_spec(inputs, rows, block, width)
        + [whole_spec(vectors.shape), whole_spec((width, 2 * width)), table_spec, table_spec],
        out_specs=[row_spec] + [turned_spec(tall)] * (2 * groups),
        out_shape=[jax.ShapeDtypeStruct((rows, width), BF16)] + [turned(tall)] * (2 * groups),
        compiler_params=params,
        cost_estimate=pl.CostEstimate(
            flops=8 * rows * width * width, bytes_accessed=8 * rows * width + 4 * width * width, transcendentals=0
        ),
        name="project_kv",
    )(*inputs, vectors, packed, cosine, sine)
    h_one, keys, values = out[0], out[1 : 1 + groups], out[1 + groups :]
    queries = pl.pallas_call(
        project_q_kernel,
        grid=(rows // block,),
        in_specs=[row_spec, whole_spec(vectors.shape), whole_spec((width, width), 2), table_spec, table_spec],
        out_specs=turned_spec(width),
        out_shape=turned(width),
        compiler_params=params,
        cost_estimate=pl.CostEstimate(
            flops=4 * rows * width * width, bytes_accessed=4 * rows * width + 2 * width * width, transcendentals=0
        ),
        name="project_q",
    )(h_one, vectors, packed, cosine, sine)
    return h_one, queries, keys, values


def feed_forward_kernel(parts, pieces, split, slot_ref, *refs):
    o_refs = refs[:parts]
    x_ref, y_ref, cot_ref, cot_y_ref, keep_ref, w_ref, vectors_ref = refs[parts : parts + 7]
    own_ref, away_ref, d_res_ref, d_heads_ref, g_rows_ref, sums_ref = refs[parts + 7 : parts + 13]
    acc, acc_rows, slope_ref, hidden_ref, staged, sems = refs[parts + 13 :]
    step, count = pl.program_id(0), pl.num_programs(0)
    width = x_ref.shape[1]

    @pl.when(step == 0)
    def _():
        acc[...] = jnp.zeros_like(acc)
        acc_rows[...] = jnp.zeros_like(acc_rows)

    gate_one, shift_two, scale_two, gate_two, b_out, b_down = [vectors_ref[i : i + 1, :] for i in (2, 3, 4, 5, 9, 10)]
    out_at = slice(0, width)
    up_at = [slice((1 + i) * width, (2 + i) * width) for i in range(pieces)]
    down_at = [slice((1 + pieces + i) * width, (2 + pieces + i) * width) for i in range(pieces)]
    keep = keep_ref[...]
    heads_out = jnp.concatenate([ref[...] for ref in o_refs], axis=0)
    branch = (dot(heads_out, w_ref[:, out_at], 0, 0) + b_out) * keep
    residual = either(x_ref, y_ref).astype(F32) + gate_one * branch
    normed, inverse = norm_parts(residual)
    h_two = (normed * (1.0 + scale_two) + shift_two).astype(BF16)
    ff_out = b_down
    for i in range(pieces):
        value, slope = gelu_both(dot(h_two, w_ref[:, up_at[i]], 1, 0) + vectors_ref[11 + i : 12 + i, :])
        slope_ref[i] = slope
        hidden = value.astype(BF16)
        hidden_ref[i] = hidden
        ff_out = ff_out + dot(hidden, w_ref[:, down_at[i]], 1, 0)
    mixed = (residual + gate_two * ff_out).astype(BF16)
    if split:

        @pl.when(step < count // 2)
        def _():
            own_ref[0] = mixed

        @pl.when(step >= count // 2)
        def _():
            away_ref[...] = mixed
    else:
        own_ref[...] = mixed
    d_mixed = either(cot_ref, cot_y_ref).astype(F32)
    acc_rows[3:4, :] += add_rows(d_mixed * ff_out)
    d_ff = (d_mixed * gate_two).astype(BF16)
    acc_rows[5:6, :] += add_rows(d_ff.astype(F32))
    d_h_two = None
    for i in range(pieces):
        acc[:, down_at[i]] += dot(hidden_ref[i], d_ff, 0, 0)
        d_up = (dot(d_ff, w_ref[:, down_at[i]], 1, 1) * slope_ref[i]).astype(BF16)
        acc_rows[6 + i : 7 + i, :] += add_rows(d_up.astype(F32))
        acc[:, up_at[i]] += dot(h_two, d_up, 0, 0)
        update = dot(d_up, w_ref[:, up_at[i]], 1, 1)
        d_h_two = update if i == 0 else d_h_two + update
    acc_rows[1:2, :] += add_rows(d_h_two)
    acc_rows[2:3, :] += add_rows(d_h_two * normed)
    d_residual = d_mixed + norm_back(normed, inverse, d_h_two * (1.0 + scale_two))
    d_res_ref[...] = d_residual
    acc_rows[0:1, :] += add_rows(d_residual * branch)
    d_branch = (d_residual * gate_one * keep).astype(BF16)
    acc_rows[4:5, :] += add_rows(d_branch.astype(F32))
    acc[:, out_at] += dot(heads_out, d_branch, 1, 0)
    d_heads_ref[...] = dot(w_ref[:, out_at], d_branch, 1, 1).astype(BF16)

    @pl.when(step == count - 1)
    def _():
        sums_ref[...] = acc_rows[...]
        tall = staged.shape[1]
        copies = []
        for i in range(width // tall):
            slot = i % 2
            if i >= 2:
                copies[i - 2].wait()
            staged[slot] = acc[i * tall : (i + 1) * tall, :].astype(BF16)
            copies.append(pltpu.make_async_copy(staged.at[slot], g_rows_ref.at[pl.ds(i * tall, tall), :], sems.at[slot]))
            copies[i].start()
        for copy in copies[-2:]:
            copy.wait()


def feed_forward(slot, inputs, heads_out, cotangent, keep, packed, vectors, slots):
    rows, width = heads_out[0].shape[1], inputs[0].shape[1]
    pieces = (packed.shape[1] // width - 1) // 2
    block = pick_block(inputs[0].shape[0], 256)
    local = rows // slots
    split = inputs[0].shape[0] == local
    half = local // block
    row_spec = pl.BlockSpec((block, width), lambda i, *_: (i, 0))
    turned_spec = lambda height: pl.BlockSpec((height, block), lambda i, *_: (0, i))
    kinds = jax.ShapeDtypeStruct
    if split:
        mixed_specs = [
            pl.BlockSpec((1, block, width), lambda i, at: (at[0], jnp.minimum(i, half - 1), 0)),
            pl.BlockSpec((block, width), lambda i, *_: (jnp.maximum(i - half, 0), 0)),
        ]
        mixed_shapes = [kinds((slots, local, width), BF16), kinds((local, width), BF16)]
    else:
        mixed_specs = [row_spec, whole_spec((8, 128))]
        mixed_shapes = [kinds((rows, width), BF16), kinds((8, 128), BF16)]
    return pl.pallas_call(
        functools.partial(feed_forward_kernel, len(heads_out), pieces, split),
        grid_spec=pltpu.PrefetchScalarGridSpec(
            num_scalar_prefetch=1,
            grid=(rows // block,),
            in_specs=[turned_spec(part.shape[0]) for part in heads_out]
            + halves_spec(inputs, rows, block, width) * 2
            + [
                pl.BlockSpec((block, 1), lambda i, *_: (i, 0)),
                whole_spec(packed.shape),
                whole_spec(vectors.shape),
            ],
            out_specs=mixed_specs
            + [
                row_spec,
                turned_spec(width),
                pl.BlockSpec(memory_space=pl.ANY),
                whole_spec((8, width)),
            ],
            scratch_shapes=[
                pltpu.VMEM(packed.shape, F32),
                pltpu.VMEM((8, width), F32),
                pltpu.VMEM((pieces, block, width), F32),
                pltpu.VMEM((pieces, block, width), BF16),
                pltpu.VMEM((2, pick_block(width, 256), packed.shape[1]), BF16),
                pltpu.SemaphoreType.DMA((2,)),
            ],
        ),
        out_shape=mixed_shapes
        + [
            kinds((rows, width), F32),
            kinds((width, rows), BF16),
            kinds(packed.shape, BF16),
            kinds((8, width), F32),
        ],
        compiler_params=pltpu.CompilerParams(vmem_limit_bytes=VMEM_LIMIT),
        cost_estimate=pl.CostEstimate(
            flops=6 * rows * width * packed.shape[1],
            bytes_accessed=8 * rows * width + 4 * width * packed.shape[1],
            transcendentals=0,
        ),
        name="feed_forward",
    )(slot, *heads_out, *inputs, *cotangent, keep, packed, vectors)


def weight_grads_kernel(parts, shard, core_ref, h_ref, dq_ref, *refs):
    dk_refs, dv_refs = refs[:parts], refs[parts : 2 * parts]
    dk_out, dv_out, keep_ref, send_ref, bias_ref = refs[2 * parts :]

    def summed(pieces):
        total = pieces[0][...]
        for ref in pieces[1:]:
            total = total + ref[...].astype(F32)
        return total.astype(BF16)

    grads = [dq_ref[...], summed(dk_refs), summed(dv_refs)]
    dk_out[...] = grads[1]
    dv_out[...] = grads[2]
    weight_grad = dot(jnp.concatenate(grads, axis=0), h_ref[...], 1, 0).T.astype(BF16)
    for i, grad in enumerate(grads):
        bias_ref[:, i : i + 1] = jnp.sum(grad.astype(F32), axis=1, keepdims=True)
    if not shard:
        keep_ref[...] = weight_grad
        return

    def store(even_ref, odd_ref):
        for i in range(0, weight_grad.shape[0] // 2, shard):
            even_ref[i : i + shard, :] = weight_grad[2 * i : 2 * i + shard]
            odd_ref[i : i + shard, :] = weight_grad[2 * i + shard : 2 * (i + shard)]

    @pl.when(core_ref[0] == 0)
    def _():
        store(keep_ref, send_ref)

    @pl.when(core_ref[0] != 0)
    def _():
        store(send_ref, keep_ref)


def weight_grads(core, shard, h_one, d_query, dk_parts, dv_parts):
    rows, width = h_one.shape
    tall = d_query.shape[0]
    block = pick_block(tall, 128)
    spec = pl.BlockSpec((block, rows), lambda i, *_: (i, 0))
    kinds = jax.ShapeDtypeStruct
    parts = len(dk_parts)
    in_kernel = shard % 16 == 0
    height = width // 2 if in_kernel else width
    columns = lambda height: pl.BlockSpec((height, 3 * block), lambda i, *_: (0, i))
    dk, dv, keep, send, bias = pl.pallas_call(
        functools.partial(weight_grads_kernel, parts, shard if in_kernel else 0),
        grid_spec=pltpu.PrefetchScalarGridSpec(
            num_scalar_prefetch=1,
            grid=(tall // block,),
            in_specs=[whole_spec((rows, width))] + [spec] * (1 + 2 * parts),
            out_specs=[
                spec,
                spec,
                columns(height),
                columns(height if in_kernel else 16),
                pl.BlockSpec((block, 128), lambda i, *_: (i, 0)),
            ],
        ),
        out_shape=[
            kinds((tall, rows), BF16),
            kinds((tall, rows), BF16),
            kinds((height, 3 * tall), BF16),
            kinds((height if in_kernel else 16, 3 * tall), BF16),
            kinds((tall, 128), F32),
        ],
        compiler_params=pltpu.CompilerParams(vmem_limit_bytes=VMEM_LIMIT),
        cost_estimate=pl.CostEstimate(flops=0, bytes_accessed=0, transcendentals=0),
        name="weight_grads",
    )(core, h_one, d_query, *dk_parts, *dv_parts)
    if not in_kernel:
        both = keep.reshape(-1, 2, shard, 3 * tall)
        keep, send = [
            lax.dynamic_index_in_dim(both, at, 1, keepdims=False).reshape(-1, 3 * tall) for at in (core[0], 1 - core[0])
        ]
    return dk, dv, keep, send, bias


def input_grads_kernel(counts, slot_ref, x_ref, d_res_ref, vectors_ref, w_ref, *refs):
    grad_refs, (out_ref, sums_ref) = refs[:-2], refs[-2:]
    width = x_ref.shape[1]

    @pl.when(pl.program_id(0) == 0)
    def _():
        sums_ref[...] = jnp.zeros_like(sums_ref)

    turned = None
    used = 0
    for kind in range(3):
        first = (2, 0, 1)[kind] * width
        grad = jnp.concatenate([ref[...] for ref in grad_refs[used : used + counts[kind]]], axis=0)
        used += counts[kind]
        update = dot(w_ref[:, first : first + width], grad, 1, 0)
        turned = update if turned is None else turned + update
    d_h_one = turned.T
    normed, inverse = norm_parts(x_ref[...].astype(F32))
    sums_ref[0:1, :] += add_rows(d_h_one)
    sums_ref[1:2, :] += add_rows(d_h_one * normed)
    grad = (d_res_ref[...] + norm_back(normed, inverse, d_h_one * (1.0 + vectors_ref[1:2, :]))).astype(BF16)
    out_ref[...] = grad.reshape(out_ref.shape)


def input_grads(slot, slots, inputs, half, d_residual, vectors, packed, grads):
    rows, width = inputs.shape
    block = pick_block(rows, 256)
    first = half * (rows // block)
    row_spec = pl.BlockSpec((block, width), lambda i, *_: (i, 0))
    flat = [grad for kind in grads for grad in kind]
    out_spec, out_shape = row_spec, (rows, width)
    if slots:
        out_spec = pl.BlockSpec((1, block, width), lambda i, at: (at[0], i, 0))
        out_shape = (slots, rows, width)
    return pl.pallas_call(
        functools.partial(input_grads_kernel, [len(kind) for kind in grads]),
        grid_spec=pltpu.PrefetchScalarGridSpec(
            num_scalar_prefetch=1,
            grid=(rows // block,),
            in_specs=[
                row_spec,
                pl.BlockSpec((block, width), lambda i, *_: (i + first, 0)),
                whole_spec(vectors.shape),
                whole_spec((width, 3 * width)),
            ]
            + [pl.BlockSpec((grad.shape[0], block), lambda i, *_: (0, i + first)) for grad in flat],
            out_specs=[out_spec, whole_spec((8, width))],
        ),
        out_shape=[jax.ShapeDtypeStruct(out_shape, BF16), jax.ShapeDtypeStruct((8, width), F32)],
        compiler_params=pltpu.CompilerParams(vmem_limit_bytes=VMEM_LIMIT),
        cost_estimate=pl.CostEstimate(
            flops=16 * rows * width * width, bytes_accessed=14 * rows * width + 6 * width * width, transcendentals=0
        ),
        name="input_grads",
    )(slot, inputs, d_residual, vectors, packed, *flat)


def time_features(t_index, model_width):
    half_width = model_width // 2
    indices = jnp.arange(half_width).astype(F32)
    frequency = jnp.exp(indices * (-math.log(10000.0) / (half_width - 1)))
    angles = t_index.astype(F32)[:, None] * frequency[None, :]
    return jnp.concatenate([jnp.sin(angles), jnp.cos(angles)], axis=1)


def rotary_tables(places):
    inverse = jnp.exp(jnp.arange(HALF).astype(F32) * (-2.0 * math.log(10000.0) / HDIM))
    angles = inverse[:, None] * places.astype(F32)[None, :]
    return jnp.cos(angles), jnp.sin(angles)


def after(values, *others):
    return lax.optimization_barrier((values,) + others)[0] if others else values


def make_body(mesh):
    n_dp, n_fsdp = mesh.shape["dp"], mesh.shape["fsdp"]
    n_pairs = n_fsdp // 2

    def shift(values, axis, size, by):
        return lax.ppermute(values, axis, [(i, (i + by) % size) for i in range(size)])

    def pick(values, index, axis=0):
        return lax.dynamic_index_in_dim(values, index, axis, keepdims=False)

    def body(
        frames,
        lengths,
        t_index,
        w_ada,
        b_ada,
        w_query,
        b_query,
        w_key,
        b_key,
        w_value,
        b_value,
        w_out,
        b_out,
        w_up,
        b_up,
        w_down,
        b_down,
        grad_out,
    ):
        slots, local, width = frames.shape
        group = n_fsdp // slots
        hidden_width = w_up.shape[1]
        shard = w_query.shape[0]
        ada_width = w_ada.shape[1]
        dp, fsdp = lax.axis_index("dp"), lax.axis_index("fsdp")
        me = dp * n_fsdp + fsdp
        slot, place = fsdp // group, fsdp % group
        other = 1 - slot
        core, pair = fsdp % 2, fsdp // 2
        side, deep, far = dp % 2, dp // 2, n_dp // 2
        length = pick(lengths, slot)

        def picked(values):
            return pick(values, slot), pick(values, other)

        split = local % 128 == 0

        def swap_in(own, away):
            parts = own, shift(away, "fsdp", n_fsdp, group)
            return parts if split else (jnp.concatenate(parts),) * 2

        def swap_out(*pieces):
            return [shift(piece, "fsdp", n_fsdp, group) for piece in pieces]

        def placed_away(whole, arrived):
            first = 0
            for piece in arrived:
                whole = lax.dynamic_update_slice(whole, piece[None], (other, first, 0))
                first += piece.shape[0]
            return whole

        def placed_own(own):
            return lax.dynamic_update_index_in_dim(jnp.zeros((slots, local, width), own.dtype), own, slot, 0)

        def places_of(member):
            at = slot * group + member
            blocks = [((at - by * group) + n_fsdp) % n_fsdp for by in range(slots)]
            return jnp.concatenate([b * local + jnp.arange(local, dtype=jnp.int32) for b in blocks])

        ring = lambda by: [(i, (i // group) * group + (i % group + by) % group) for i in range(n_fsdp)]

        def swap(values, axis, size):
            return lax.ppermute(values, axis, [(i, i ^ 1) for i in range(size)])

        def sum_core(keep, send, *others):
            arrived = after(swap(send, "fsdp", n_fsdp), *others)
            total = keep.astype(F32) + arrived.astype(F32)
            return total.astype(BF16).reshape(n_dp, n_pairs, shard, keep.shape[1])

        def sum_pairs(values, *others):
            axis = values.ndim - 3
            total = pick(values, pair, axis).astype(F32)
            for by in range(1, n_pairs):
                arrived = after(shift(pick(values, (pair + by) % n_pairs, axis), "fsdp", n_fsdp, 2 * by), *others)
                total = total + arrived.astype(F32)
            return total

        def sum_side(values, *others):
            values = values.reshape((far, 2) + values.shape[1:])
            arrived = after(swap(pick(values, 1 - side, 1), "dp", n_dp), *others)
            return pick(values, side, 1).astype(F32) + arrived.astype(F32)

        def sum_far(values, *others):
            total = pick(values, deep).astype(F32)
            for by in range(1, far):
                arrived = after(shift(pick(values, (deep + by) % far), "dp", n_dp, 2 * by), *others)
                total = total + arrived.astype(F32)
            return total

        def gather_dp(values):
            values = jnp.stack([values] + [shift(values, "dp", n_dp, 2 * by) for by in range(1, far)])
            return jnp.stack([values, swap(values, "dp", n_dp)])

        packed = lax.all_gather(jnp.concatenate([w_key, w_value, w_query], axis=1), AXES, axis=0, tiled=True)
        ups = hidden_width // width
        w_up_turned = w_up.reshape(shard, n_dp * n_fsdp, ups, shard).swapaxes(1, 2).reshape(w_up.shape)
        downs = [w_down[i * shard : (i + 1) * shard] for i in range(ups)]
        packed_two = lax.all_gather(jnp.concatenate([w_out, w_up_turned, *downs], axis=1), AXES, axis=0, tiled=True)

        inputs = swap_in(*picked(frames))
        rows = slots * local
        own_grad, away_grad = picked(grad_out)

        t_all = gather_dp(t_index).reshape(-1)
        active = jax.nn.silu(time_features(t_all, width)).astype(BF16)
        active_mine = lax.dynamic_slice_in_dim(active, me * shard, shard, axis=1)
        partial = [dot(active_mine, w_ada, 1, 0)]
        for bias in (b_query, b_key, b_value, b_out, b_down, *jnp.split(b_up, ups)):
            size = bias.shape[0]
            zeros = jnp.zeros((1, size * n_dp * n_fsdp), F32)
            placed = lax.dynamic_update_slice_in_dim(zeros, bias.astype(F32)[None], me * size, axis=1)
            partial.append(jnp.broadcast_to(placed, (n_dp * slots, placed.shape[1])))
        placed = lax.dynamic_update_slice_in_dim(
            jnp.zeros((1, ada_width), F32), b_ada.astype(F32)[None], me * b_ada.shape[0], axis=1
        )
        partial[0] = partial[0] + placed
        partial = jnp.concatenate(partial, axis=1).reshape(2, far, slots, -1)
        partial = partial[0] + swap(partial[1], "dp", n_dp)
        summed = partial[0]
        for by in range(1, far):
            summed = summed + shift(partial[by], "dp", n_dp, -2 * by)
        one = pick(summed, slot) + shift(pick(summed, other), "fsdp", n_fsdp, group)
        vectors = one
        for by in range(1, group):
            vectors = vectors + lax.ppermute(one, "fsdp", ring(by))
        vectors = vectors.reshape(-1, width)
        vectors = jnp.pad(vectors, ((0, -vectors.shape[0] % 8), (0, 0)))

        key_places = jnp.concatenate([places_of((place - by + group) % group) for by in range(group)])
        cosine, sine = rotary_tables(key_places)
        key_bias = jnp.where(key_places < length, 0.0, -1e30)
        bias_columns = jnp.pad(key_bias.astype(BF16)[:, None], ((0, 0), (0, HDIM - 1)))
        keep = (key_places[:rows] < length).astype(F32)[:, None]

        wide = 2
        vectors, cosine, sine, key_bias, bias_columns, keep, own_grad, away_grad = lax.optimization_barrier(
            (vectors, cosine, sine, key_bias, bias_columns, keep, own_grad, away_grad)
        )
        h_one, q_rot, keys, values = project(inputs, vectors, packed, cosine[:, :rows], sine[:, :rows], wide)
        cotangent = swap_in(own_grad, after(away_grad, keys[0]))
        heads = width // HDIM
        tall = heads // wide
        with_ring = lambda own: [own] + [lax.ppermute(own, "fsdp", ring(by)) for by in range(1, group)]
        k_parts, v_parts = [with_ring(own) for own in keys], [with_ring(own) for own in values]
        heads_out, lses = [], []
        for at in range(wide):
            out, lse = attend(q_rot, k_parts[at], v_parts[at], bias_columns, at * tall)
            heads_out.append(out)
            lses.append(lse)
        at_slot = slot.reshape(1).astype(jnp.int32)
        mixed, away_mixed, d_residual, d_heads, g_rows, sums_two = feed_forward(
            at_slot, inputs, heads_out, cotangent, keep, packed_two, vectors, slots
        )
        if not split:
            mixed, away_mixed = placed_own(mixed[:local]), mixed[local:]
        mixed_arrived = swap_out(away_mixed)

        sum_rows = lax.psum_scatter(g_rows, AXES, scatter_dimension=0, tiled=True)

        grads, d_biases = ([], [], []), []
        at_core = core.reshape(1).astype(jnp.int32)

        def sum_parts(dq, dk_parts, dv_parts, *others):
            dk_parts = [after(dk_parts[0], *others)] + dk_parts[1:]
            dk, dv, keep, send, bias_grad = weight_grads(at_core, shard, h_one, dq, dk_parts, dv_parts)
            for kind, grad in zip(grads, (dq, dk, dv)):
                kind.append(grad)
            d_biases.append(bias_grad[:, :3])
            return keep, send

        counts = (tall, tall // 2, tall // 2)
        first, ready, arrived = 0, d_heads, []
        for step, each in enumerate(counts):
            part, within = first // tall, first % tall
            dq, dk_parts, dv_parts = attend_back(
                q_rot,
                k_parts[part],
                v_parts[part],
                ready,
                heads_out[part],
                lses[part],
                key_bias[None],
                cosine,
                sine,
                first,
                within,
                each,
            )
            first += each
            dk_parts = [dk_parts[0]] + [lax.ppermute(dk_parts[by], "fsdp", ring(-by)) for by in range(1, group)]
            dv_parts = [dv_parts[0]] + [lax.ppermute(dv_parts[by], "fsdp", ring(-by)) for by in range(1, group)]
            arrived.append((dq, dk_parts, dv_parts))
            if step == 1:
                early = sum_parts(*arrived[0], dq)
                ready = after(d_heads, dq, early[0])
        early_sum = sum_core(*early, dq)
        middle = sum_parts(*arrived[1], dq)
        last = sum_parts(*arrived[2], middle[0], sum_rows, *mixed_arrived)
        early_sum = sum_pairs(early_sum, last[0]).astype(BF16)
        if split:
            rest = after(d_residual, last[0], early_sum)
            away_frames, sums_away = input_grads(at_slot, 0, inputs[1], 1, rest, vectors, packed, grads)
            core_sums = jnp.concatenate([sum_core(*sums, away_frames) for sums in (middle, last)], axis=-1)
            rest, core_sums, _ = lax.optimization_barrier((d_residual, core_sums, away_frames))
            own_frames, sums_own = input_grads(at_slot, slots, inputs[0], 0, rest, vectors, packed, grads)
            sums_one = sums_own + sums_away
        else:
            core_sums = jnp.concatenate([sum_core(*sums) for sums in (middle, last)], axis=-1)
            both, sums_one = input_grads(at_slot, 0, inputs[0], 0, d_residual, vectors, packed, grads)
            own_frames, away_frames = placed_own(both[:local]), both[local:]
        cut = local * 2 // 3 // 16 * 16
        frames_arrived = swap_out(away_frames[:cut], after(away_frames[cut:], core_sums))
        side_sums = sum_side(core_sums).astype(BF16)
        early_sum = sum_side(early_sum, side_sums).astype(BF16)

        vector = jnp.concatenate(
            [sums_one[:2], sums_two[: 6 + ups], jnp.concatenate(d_biases).T]
        )
        for_slot = 6
        vector = after(vector, frames_arrived[0])
        total = vector
        for by in range(1, group):
            total = total + lax.ppermute(vector, "fsdp", ring(by))
        total, side_sums = lax.optimization_barrier((total, side_sums))
        all_sums = sum_far(jnp.concatenate([early_sum[:, None], side_sums], axis=1))
        sums = [all_sums[0], sum_pairs(all_sums[1:].astype(BF16))]
        sum_rows, mixed = after(sum_rows, total).astype(F32), after(mixed, total)
        g_out = sum_rows[:, :width]
        g_up = sum_rows[:, width : width + hidden_width].reshape(shard, ups, n_dp * n_fsdp, shard)
        g_up = g_up.swapaxes(1, 2).reshape(w_up.shape)
        g_down = jnp.concatenate([sum_rows[:, (1 + ups + i) * width : (2 + ups + i) * width] for i in range(ups)])
        mixed = placed_away(mixed, mixed_arrived)
        packs = gather_dp(total).reshape(n_dp, -1, width)
        pack = jnp.concatenate([packs[:, :for_slot].reshape(-1, width), jnp.sum(packs[:, for_slot:], axis=0)])
        pack, g_out, g_up, g_down, mixed, _ = lax.optimization_barrier(
            (pack, g_out, g_up, g_down, mixed, frames_arrived[1])
        )
        grad_frames = placed_away(own_frames, frames_arrived)
        across = shift(pack, "fsdp", n_fsdp, group)
        count = n_dp * for_slot
        d_mod = jnp.stack([jnp.where(slot == s, pack[:count], across[:count]).reshape(n_dp, -1) for s in range(slots)], axis=1)
        d_mod = d_mod.reshape(n_dp * slots, for_slot * width)
        d_vectors = pack[count:] + across[count:]

        g_w_ada = lax.dot_general(
            active_mine.astype(F32),
            d_mod,
            (((0,), (0,)), ((), ())),
            precision=lax.Precision.HIGHEST,
            preferred_element_type=F32,
        )

        def mine(vector):
            vector = vector.reshape(-1)
            size = vector.shape[0] // (n_dp * n_fsdp)
            return lax.dynamic_slice_in_dim(vector, me * size, size)

        columns = jnp.concatenate(sums, axis=1).reshape(shard, -1, 3, pick_block(tall // 2 * HDIM, 128))
        g_qkv = [columns[:, :, i].reshape(shard, width) for i in range(3)]
        return (
            mixed,
            grad_frames,
            g_w_ada,
            mine(jnp.sum(d_mod, axis=0)),
            g_qkv[0],
            mine(d_vectors[2 + ups]),
            g_qkv[1],
            mine(d_vectors[3 + ups]),
            g_qkv[2],
            mine(d_vectors[4 + ups]),
            g_out,
            mine(d_vectors[0]),
            g_up,
            jnp.concatenate([mine(d_vectors[2 + i]) for i in range(ups)]),
            g_down,
            mine(d_vectors[1]),
        )

    return body


def solution(mesh):
    rows, vector, matrix = P("dp", "fsdp", None), P(AXES), P(AXES, None)
    return jax.shard_map(
        make_body(mesh),
        mesh=mesh,
        in_specs=(rows, P("dp"), P("dp")) + (matrix, vector) * 7 + (rows,),
        out_specs=(rows, rows) + (matrix, vector) * 7,
        check_vma=False,
    )
```

```python
import functools
import math

import jax
import jax.numpy as jnp
from jax import lax
from jax.experimental import pallas as pl
from jax.experimental.pallas import tpu as pltpu
from jax.sharding import PartitionSpec as P

HDIM = 64
HALF = HDIM // 2
SCALE = HDIM ** (-0.5)
SCALE2 = SCALE * math.log2(math.e)
AXES = ("dp", "fsdp")
VMEM_LIMIT = 62 << 20
F32 = jnp.float32
BF16 = jnp.bfloat16


def dot(left_side, right_side, left_dim, right_dim):
    return lax.dot_general(
        left_side,
        right_side,
        (((left_dim,), (right_dim,)), ((), ())),
        preferred_element_type=F32,
    )


def pick_block(total, wanted):
    block = min(total, wanted)
    while total % block:
        block -= 128
    return block


def attend_kernel(parts, chunk, *refs):
    q_ref, bias_ref = refs[0], refs[1]
    k_refs, v_refs = refs[2 : 2 + parts], refs[2 + parts : 2 + 2 * parts]
    o_ref, lse_ref, k_aug, v_aug, q_aug = refs[2 + 2 * parts :]
    head, block = pl.program_id(0), pl.program_id(1)
    span = k_aug.shape[0]
    part = span // parts
    q_rows = q_ref.shape[1]

    @pl.when((head == 0) & (block == 0))
    def _():
        k_aug[:, HDIM:] = bias_ref[...]
        v_aug[HDIM:, :] = jnp.ones((16, span), BF16)
        q_aug[HDIM:, :] = jnp.ones((HDIM, q_rows), BF16)

    @pl.when(block == 0)
    def _():
        for i in range(parts):
            k_aug[i * part : (i + 1) * part, :HDIM] = k_refs[i][...].T
            v_aug[:HDIM, i * part : (i + 1) * part] = v_refs[i][...]

    q_aug[:HDIM, :] = q_ref[...]
    queries = q_aug[...]
    count = span // chunk

    def scores(i):
        return dot(k_aug[i * chunk : (i + 1) * chunk, :], queries, 1, 0)

    upcoming = scores(0)
    row_max = total = None
    for i in range(count):
        current = upcoming
        if i + 1 < count:
            upcoming = scores(i + 1)
        chunk_max = jnp.max(current, axis=0, keepdims=True) * SCALE2
        new_max = chunk_max if i == 0 else jnp.maximum(row_max, chunk_max)
        weights = jnp.exp2(current * SCALE2 - new_max).astype(BF16)
        update = dot(v_aug[:, i * chunk : (i + 1) * chunk], weights, 1, 0)
        total = update if i == 0 else total * jnp.exp2(row_max - new_max) + update
        row_max = new_max
    denominator = total[HDIM : HDIM + 1, :]
    o_ref[...] = (total[:HDIM, :] / denominator).astype(BF16)
    lse_ref[...] = (row_max + jnp.log2(denominator))[None]


def attend(q_rot, k_parts, v_parts, bias_columns, first):
    width, rows = k_parts[0].shape
    parts = len(k_parts)
    span = parts * rows
    heads = width // HDIM
    q_rows = pick_block(rows, 768)
    chunk = pick_block(span, 512)
    q_spec = pl.BlockSpec((HDIM, q_rows), lambda h, j: (h + first, j))
    k_spec = pl.BlockSpec((HDIM, rows), lambda h, j: (h, 0))
    return pl.pallas_call(
        functools.partial(attend_kernel, parts, chunk),
        grid=(heads, rows // q_rows),
        in_specs=[q_spec, pl.BlockSpec((span, HDIM), lambda h, j: (0, 0))] + [k_spec] * (2 * parts),
        out_specs=[
            pl.BlockSpec((HDIM, q_rows), lambda h, j: (h, j)),
            pl.BlockSpec((1, 1, q_rows), lambda h, j: (h, 0, j)),
        ],
        out_shape=[
            jax.ShapeDtypeStruct((width, rows), BF16),
            jax.ShapeDtypeStruct((heads, 1, rows), F32),
        ],
        scratch_shapes=[
            pltpu.VMEM((span, 2 * HDIM), BF16),
            pltpu.VMEM((HDIM + 16, span), BF16),
            pltpu.VMEM((2 * HDIM, q_rows), BF16),
        ],
        compiler_params=pltpu.CompilerParams(vmem_limit_bytes=VMEM_LIMIT),
        cost_estimate=pl.CostEstimate(
            flops=16 * heads * rows * span * HDIM,
            bytes_accessed=2 * width * (2 * rows + 2 * span),
            transcendentals=heads * rows * span,
        ),
        name="attend",
    )(q_rot, bias_columns, *k_parts, *v_parts)


def in_three(values):
    first = values.astype(BF16)
    rest = values - first.astype(F32)
    second = rest.astype(BF16)
    return first.astype(F32), second.astype(F32), rest - second.astype(F32)


def unrotate(values, cosine, sine):
    low, high = values[:HALF], values[HALF:]
    return low * cosine + high * sine, high * cosine - low * sine


def attend_back_kernel(parts, chunk, *refs):
    q_ref, do_ref, o_ref, lse_ref, bias_ref, cos_ref, sin_ref = refs[:7]
    k_refs, v_refs = refs[7 : 7 + parts], refs[7 + parts : 7 + 2 * parts]
    dq_ref = refs[7 + 2 * parts]
    dk_refs = refs[8 + 2 * parts : 8 + 3 * parts]
    dv_refs = refs[8 + 3 * parts : 8 + 4 * parts]
    k_aug, v_aug, k_rows, q_aug, do_aug, dk_acc, dv_acc = refs[8 + 4 * parts :]
    head, block = pl.program_id(0), pl.program_id(1)
    span = k_aug.shape[1]
    part = span // parts
    q_rows = q_ref.shape[1]

    @pl.when((head == 0) & (block == 0))
    def _():
        row = lax.broadcasted_iota(jnp.int32, (HDIM, span), 0)
        ones = jnp.where(row < 4, 1.0, 0.0)
        k_aug[HDIM:, :] = jnp.where(row == 0, bias_ref[...], ones).astype(BF16)
        v_aug[HDIM:, :] = jnp.where(row < 3, 1.0, 0.0).astype(BF16)
        k_rows[:, HDIM:] = jnp.zeros((span, HDIM), BF16)

    @pl.when(block == 0)
    def _():
        for i in range(parts):
            at = slice(i * part, (i + 1) * part)
            keys = k_refs[i][...]
            k_aug[:HDIM, at] = keys
            v_aug[:HDIM, at] = v_refs[i][...]
            k_rows[at, :HDIM] = keys.T
        dk_acc[...] = jnp.zeros_like(dk_acc)
        dv_acc[...] = jnp.zeros_like(dv_acc)

    queries, d_heads = q_ref[...], do_ref[...]
    delta = jnp.sum(d_heads.astype(F32) * o_ref[...].astype(F32), axis=0, keepdims=True)
    row = lax.broadcasted_iota(jnp.int32, (HDIM, q_rows), 0)
    lse_a, lse_b, lse_c = in_three(lse_ref[0] * (-1.0 / SCALE2))
    del_a, del_b, del_c = in_three(-delta)
    q_extra = jnp.where(row == 2, lse_b, jnp.where(row == 3, lse_c, 0.0))
    q_extra = jnp.where(row == 0, 1.0, jnp.where(row == 1, lse_a, q_extra))
    do_extra = jnp.where(row == 1, del_b, jnp.where(row == 2, del_c, 0.0))
    do_extra = jnp.where(row == 0, del_a, do_extra)
    q_aug[:HDIM, :] = queries
    q_aug[HDIM:, :] = q_extra.astype(BF16)
    do_aug[:HDIM, :] = d_heads
    do_aug[HDIM:, :] = do_extra.astype(BF16)
    q_side, do_side = q_aug[...].T, do_aug[...].T
    count = span // chunk

    def products(i):
        at = slice(i * chunk, (i + 1) * chunk)
        return dot(q_side, k_aug[:, at], 1, 0), dot(do_side, v_aug[:, at], 1, 0)

    upcoming = products(0)
    d_query = None
    for i in range(count):
        at = slice(i * chunk, (i + 1) * chunk)
        scores, d_probs = upcoming
        if i + 1 < count:
            upcoming = products(i + 1)
        probs = jnp.exp2(scores * SCALE2)
        d_scores = (probs * d_probs).astype(BF16)
        dv_acc[:, at] += dot(d_heads, probs.astype(BF16), 1, 0)
        dk_acc[:, at] += dot(queries, d_scores, 1, 0)
        update = dot(d_scores, k_rows[at, :], 1, 0)
        d_query = update if i == 0 else d_query + update
    first = pl.multiple_of(block * q_rows, q_rows)
    low, high = unrotate(
        d_query.T[:HDIM, :] * SCALE, cos_ref[:, pl.ds(first, q_rows)], sin_ref[:, pl.ds(first, q_rows)]
    )
    dq_ref[:HALF, :] = low.astype(BF16)
    dq_ref[HALF:, :] = high.astype(BF16)

    @pl.when(block == pl.num_programs(1) - 1)
    def _():
        for i in range(parts):
            at = slice(i * part, (i + 1) * part)
            low, high = unrotate(dk_acc[:, at] * SCALE, cos_ref[:, at], sin_ref[:, at])
            dk_refs[i][:HALF, :] = low.astype(dk_refs[i].dtype)
            dk_refs[i][HALF:, :] = high.astype(dk_refs[i].dtype)
            dv_refs[i][...] = dv_acc[:, at].astype(dv_refs[i].dtype)


def attend_back(q_rot, k_parts, v_parts, d_heads, heads_out, lse, bias_row, cosine, sine, first, within, count):
    rows = q_rot.shape[1]
    parts = len(k_parts)
    span = parts * rows
    q_rows = pick_block(rows, 1536)
    chunk = pick_block(span, 256)
    q_spec = pl.BlockSpec((HDIM, q_rows), lambda h, j: (h + first, j))
    k_spec = pl.BlockSpec((HDIM, rows), lambda h, j: (h + within, 0))
    whole = lambda array: pl.BlockSpec(array.shape, lambda h, j: (0, 0))
    part_out = pl.BlockSpec((HDIM, rows), lambda h, j: (h, 0))
    shape = lambda kind: jax.ShapeDtypeStruct((count * HDIM, rows), kind)
    part_kinds = [F32] + [BF16] * (parts - 1)
    out = pl.pallas_call(
        functools.partial(attend_back_kernel, parts, chunk),
        grid=(count, rows // q_rows),
        in_specs=[
            q_spec,
            q_spec,
            pl.BlockSpec((HDIM, q_rows), lambda h, j: (h + within, j)),
            pl.BlockSpec((1, 1, q_rows), lambda h, j: (h + within, 0, j)),
            whole(bias_row),
            whole(cosine),
            whole(sine),
        ]
        + [k_spec] * (2 * parts),
        out_specs=[pl.BlockSpec((HDIM, q_rows), lambda h, j: (h, j))] + [part_out] * (2 * parts),
        out_shape=[shape(BF16)] + [shape(kind) for kind in part_kinds * 2],
        scratch_shapes=[
            pltpu.VMEM((2 * HDIM, span), BF16),
            pltpu.VMEM((2 * HDIM, span), BF16),
            pltpu.VMEM((span, 2 * HDIM), BF16),
            pltpu.VMEM((2 * HDIM, q_rows), BF16),
            pltpu.VMEM((2 * HDIM, q_rows), BF16),
            pltpu.VMEM((HDIM, span), F32),
            pltpu.VMEM((HDIM, span), F32),
        ],
        compiler_params=pltpu.CompilerParams(vmem_limit_bytes=VMEM_LIMIT),
        cost_estimate=pl.CostEstimate(
            flops=5 * count * rows * span * HDIM,
            bytes_accessed=0,
            transcendentals=0,
        ),
        name="attend_back",
    )(q_rot, d_heads, heads_out, lse, bias_row, cosine, sine, *k_parts, *v_parts)
    return out[0], out[1 : 1 + parts], out[1 + parts :]


def norm_parts(values):
    centered = values - jnp.mean(values, axis=-1, keepdims=True)
    scale = lax.rsqrt(jnp.mean(centered * centered, axis=-1, keepdims=True) + 1e-06)
    return centered * scale, scale


def norm_back(normed, scale, d_normed):
    return (
        d_normed
        - jnp.mean(d_normed, axis=-1, keepdims=True)
        - normed * jnp.mean(d_normed * normed, axis=-1, keepdims=True)
    ) * scale


def gelu_both(values):
    square = values * values
    bend = jnp.tanh(0.7978845608028654 * (values + 0.044715 * values * square))
    half = 0.5 * (1.0 + bend)
    slope = 0.7978845608028654 * (1.0 + 3 * 0.044715 * square)
    return values * half, half + 0.5 * values * (1.0 - bend * bend) * slope


def add_rows(values):
    return jnp.sum(values, axis=0, keepdims=True)


def store_rotated(out_ref, values, cosine, sine):
    for at in range(0, out_ref.shape[0], HDIM):
        low, high = values[at : at + HALF], values[at + HALF : at + HDIM]
        out_ref[at : at + HALF, :] = (low * cosine - high * sine).astype(BF16)
        out_ref[at + HALF : at + HDIM, :] = (high * cosine + low * sine).astype(BF16)


def either(first_ref, second_ref):
    half = pl.num_programs(0) // 2
    return jnp.where(pl.program_id(0) < half, first_ref[...], second_ref[...])


def halves_spec(inputs, rows, block, width):
    if inputs[0].shape[0] == rows:
        return [pl.BlockSpec((block, width), lambda i, *_: (i, 0))] * 2
    half = rows // 2 // block
    return [
        pl.BlockSpec((block, width), lambda i, *_: (jnp.minimum(i, half - 1), 0)),
        pl.BlockSpec((block, width), lambda i, *_: (jnp.maximum(i - half, 0), 0)),
    ]


def project_kv_kernel(groups, x_ref, y_ref, vectors_ref, w_ref, cos_ref, sin_ref, h_ref, *refs):
    k_refs, v_refs = refs[:groups], refs[groups:]
    width = x_ref.shape[1]
    tall = width // groups
    normed, _ = norm_parts(either(x_ref, y_ref).astype(F32))
    h_one = (normed * (1.0 + vectors_ref[1:2, :]) + vectors_ref[0:1, :]).astype(BF16)
    h_ref[...] = h_one
    keys = (dot(h_one, w_ref[:, :width], 1, 0) + vectors_ref[7:8, :]).T
    values = (dot(h_one, w_ref[:, width:], 1, 0) + vectors_ref[8:9, :]).astype(BF16).T
    for i in range(groups):
        store_rotated(k_refs[i], keys[i * tall : (i + 1) * tall], cos_ref[...], sin_ref[...])
        v_refs[i][...] = values[i * tall : (i + 1) * tall]


def project_q_kernel(h_ref, vectors_ref, w_ref, cos_ref, sin_ref, q_ref):
    queries = dot(h_ref[...], w_ref[...], 1, 0) + vectors_ref[6:7, :]
    store_rotated(q_ref, queries.T, cos_ref[...], sin_ref[...])


def whole_spec(shape, column=0):
    return pl.BlockSpec(shape, lambda i, *_: (0, column), pipeline_mode=pl.Buffered(1))


def project(inputs, vectors, packed, cosine, sine, groups):
    width, rows = inputs[0].shape[1], cosine.shape[1]
    block = pick_block(inputs[0].shape[0], 256)
    tall = width // groups
    row_spec = pl.BlockSpec((block, width), lambda i: (i, 0))
    turned_spec = lambda height: pl.BlockSpec((height, block), lambda i: (0, i))
    turned = lambda height: jax.ShapeDtypeStruct((height, rows), BF16)
    table_spec = turned_spec(HALF)
    params = pltpu.CompilerParams(vmem_limit_bytes=VMEM_LIMIT)
    out = pl.pallas_call(
        functools.partial(project_kv_kernel, groups),
        grid=(rows // block,),
        in_specs=halves_spec(inputs, rows, block, width)
        + [whole_spec(vectors.shape), whole_spec((width, 2 * width)), table_spec, table_spec],
        out_specs=[row_spec] + [turned_spec(tall)] * (2 * groups),
        out_shape=[jax.ShapeDtypeStruct((rows, width), BF16)] + [turned(tall)] * (2 * groups),
        compiler_params=params,
        cost_estimate=pl.CostEstimate(
            flops=8 * rows * width * width, bytes_accessed=8 * rows * width + 4 * width * width, transcendentals=0
        ),
        name="project_kv",
    )(*inputs, vectors, packed, cosine, sine)
    h_one, keys, values = out[0], out[1 : 1 + groups], out[1 + groups :]
    queries = pl.pallas_call(
        project_q_kernel,
        grid=(rows // block,),
        in_specs=[row_spec, whole_spec(vectors.shape), whole_spec((width, width), 2), table_spec, table_spec],
        out_specs=turned_spec(width),
        out_shape=turned(width),
        compiler_params=params,
        cost_estimate=pl.CostEstimate(
            flops=4 * rows * width * width, bytes_accessed=4 * rows * width + 2 * width * width, transcendentals=0
        ),
        name="project_q",
    )(h_one, vectors, packed, cosine, sine)
    return h_one, queries, keys, values


def feed_forward_kernel(parts, pieces, split, slot_ref, *refs):
    o_refs = refs[:parts]
    x_ref, y_ref, cot_ref, cot_y_ref, keep_ref, w_ref, vectors_ref = refs[parts : parts + 7]
    own_ref, away_ref, d_res_ref, d_heads_ref, g_rows_ref, sums_ref = refs[parts + 7 : parts + 13]
    acc, acc_rows, slope_ref, hidden_ref, staged, sems = refs[parts + 13 :]
    step, count = pl.program_id(0), pl.num_programs(0)
    width = x_ref.shape[1]

    @pl.when(step == 0)
    def _():
        acc[...] = jnp.zeros_like(acc)
        acc_rows[...] = jnp.zeros_like(acc_rows)

    gate_one, shift_two, scale_two, gate_two, b_out, b_down = [vectors_ref[i : i + 1, :] for i in (2, 3, 4, 5, 9, 10)]
    out_at = slice(0, width)
    up_at = [slice((1 + i) * width, (2 + i) * width) for i in range(pieces)]
    down_at = [slice((1 + pieces + i) * width, (2 + pieces + i) * width) for i in range(pieces)]
    keep = keep_ref[...]
    heads_out = jnp.concatenate([ref[...] for ref in o_refs], axis=0)
    branch = (dot(heads_out, w_ref[:, out_at], 0, 0) + b_out) * keep
    residual = either(x_ref, y_ref).astype(F32) + gate_one * branch
    normed, inverse = norm_parts(residual)
    h_two = (normed * (1.0 + scale_two) + shift_two).astype(BF16)
    ff_out = b_down
    for i in range(pieces):
        value, slope = gelu_both(dot(h_two, w_ref[:, up_at[i]], 1, 0) + vectors_ref[11 + i : 12 + i, :])
        slope_ref[i] = slope
        hidden = value.astype(BF16)
        hidden_ref[i] = hidden
        ff_out = ff_out + dot(hidden, w_ref[:, down_at[i]], 1, 0)
    mixed = (residual + gate_two * ff_out).astype(BF16)
    if split:

        @pl.when(step < count // 2)
        def _():
            own_ref[0] = mixed

        @pl.when(step >= count // 2)
        def _():
            away_ref[...] = mixed
    else:
        own_ref[...] = mixed
    d_mixed = either(cot_ref, cot_y_ref).astype(F32)
    acc_rows[3:4, :] += add_rows(d_mixed * ff_out)
    d_ff = (d_mixed * gate_two).astype(BF16)
    acc_rows[5:6, :] += add_rows(d_ff.astype(F32))
    d_h_two = None
    for i in range(pieces):
        acc[:, down_at[i]] += dot(hidden_ref[i], d_ff, 0, 0)
        d_up = (dot(d_ff, w_ref[:, down_at[i]], 1, 1) * slope_ref[i]).astype(BF16)
        acc_rows[6 + i : 7 + i, :] += add_rows(d_up.astype(F32))
        acc[:, up_at[i]] += dot(h_two, d_up, 0, 0)
        update = dot(d_up, w_ref[:, up_at[i]], 1, 1)
        d_h_two = update if i == 0 else d_h_two + update
    acc_rows[1:2, :] += add_rows(d_h_two)
    acc_rows[2:3, :] += add_rows(d_h_two * normed)
    d_residual = d_mixed + norm_back(normed, inverse, d_h_two * (1.0 + scale_two))
    d_res_ref[...] = d_residual
    acc_rows[0:1, :] += add_rows(d_residual * branch)
    d_branch = (d_residual * gate_one * keep).astype(BF16)
    acc_rows[4:5, :] += add_rows(d_branch.astype(F32))
    acc[:, out_at] += dot(heads_out, d_branch, 1, 0)
    d_heads_ref[...] = dot(w_ref[:, out_at], d_branch, 1, 1).astype(BF16)

    @pl.when(step == count - 1)
    def _():
        sums_ref[...] = acc_rows[...]
        tall = staged.shape[1]
        copies = []
        for i in range(width // tall):
            slot = i % 2
            if i >= 2:
                copies[i - 2].wait()
            staged[slot] = acc[i * tall : (i + 1) * tall, :].astype(BF16)
            copies.append(pltpu.make_async_copy(staged.at[slot], g_rows_ref.at[pl.ds(i * tall, tall), :], sems.at[slot]))
            copies[i].start()
        for copy in copies[-2:]:
            copy.wait()


def feed_forward(slot, inputs, heads_out, cotangent, keep, packed, vectors, slots):
    rows, width = heads_out[0].shape[1], inputs[0].shape[1]
    pieces = (packed.shape[1] // width - 1) // 2
    block = pick_block(inputs[0].shape[0], 256)
    local = rows // slots
    split = inputs[0].shape[0] == local
    half = local // block
    row_spec = pl.BlockSpec((block, width), lambda i, *_: (i, 0))
    turned_spec = lambda height: pl.BlockSpec((height, block), lambda i, *_: (0, i))
    kinds = jax.ShapeDtypeStruct
    if split:
        mixed_specs = [
            pl.BlockSpec((1, block, width), lambda i, at: (at[0], jnp.minimum(i, half - 1), 0)),
            pl.BlockSpec((block, width), lambda i, *_: (jnp.maximum(i - half, 0), 0)),
        ]
        mixed_shapes = [kinds((slots, local, width), BF16), kinds((local, width), BF16)]
    else:
        mixed_specs = [row_spec, whole_spec((8, 128))]
        mixed_shapes = [kinds((rows, width), BF16), kinds((8, 128), BF16)]
    return pl.pallas_call(
        functools.partial(feed_forward_kernel, len(heads_out), pieces, split),
        grid_spec=pltpu.PrefetchScalarGridSpec(
            num_scalar_prefetch=1,
            grid=(rows // block,),
            in_specs=[turned_spec(part.shape[0]) for part in heads_out]
            + halves_spec(inputs, rows, block, width) * 2
            + [
                pl.BlockSpec((block, 1), lambda i, *_: (i, 0)),
                whole_spec(packed.shape),
                whole_spec(vectors.shape),
            ],
            out_specs=mixed_specs
            + [
                row_spec,
                turned_spec(width),
                pl.BlockSpec(memory_space=pl.ANY),
                whole_spec((8, width)),
            ],
            scratch_shapes=[
                pltpu.VMEM(packed.shape, F32),
                pltpu.VMEM((8, width), F32),
                pltpu.VMEM((pieces, block, width), F32),
                pltpu.VMEM((pieces, block, width), BF16),
                pltpu.VMEM((2, pick_block(width, 256), packed.shape[1]), BF16),
                pltpu.SemaphoreType.DMA((2,)),
            ],
        ),
        out_shape=mixed_shapes
        + [
            kinds((rows, width), F32),
            kinds((width, rows), BF16),
            kinds(packed.shape, BF16),
            kinds((8, width), F32),
        ],
        compiler_params=pltpu.CompilerParams(vmem_limit_bytes=VMEM_LIMIT),
        cost_estimate=pl.CostEstimate(
            flops=6 * rows * width * packed.shape[1],
            bytes_accessed=8 * rows * width + 4 * width * packed.shape[1],
            transcendentals=0,
        ),
        name="feed_forward",
    )(slot, *heads_out, *inputs, *cotangent, keep, packed, vectors)


def weight_grads_kernel(parts, shard, core_ref, h_ref, dq_ref, *refs):
    dk_refs, dv_refs = refs[:parts], refs[parts : 2 * parts]
    dk_out, dv_out, keep_ref, send_ref, bias_ref = refs[2 * parts :]

    def summed(pieces):
        total = pieces[0][...]
        for ref in pieces[1:]:
            total = total + ref[...].astype(F32)
        return total.astype(BF16)

    grads = [dq_ref[...], summed(dk_refs), summed(dv_refs)]
    dk_out[...] = grads[1]
    dv_out[...] = grads[2]
    weight_grad = dot(jnp.concatenate(grads, axis=0), h_ref[...], 1, 0).T.astype(BF16)
    for i, grad in enumerate(grads):
        bias_ref[:, i : i + 1] = jnp.sum(grad.astype(F32), axis=1, keepdims=True)
    if not shard:
        keep_ref[...] = weight_grad
        return

    def store(even_ref, odd_ref):
        for i in range(0, weight_grad.shape[0] // 2, shard):
            even_ref[i : i + shard, :] = weight_grad[2 * i : 2 * i + shard]
            odd_ref[i : i + shard, :] = weight_grad[2 * i + shard : 2 * (i + shard)]

    @pl.when(core_ref[0] == 0)
    def _():
        store(keep_ref, send_ref)

    @pl.when(core_ref[0] != 0)
    def _():
        store(send_ref, keep_ref)


def weight_grads(core, shard, h_one, d_query, dk_parts, dv_parts):
    rows, width = h_one.shape
    tall = d_query.shape[0]
    block = pick_block(tall, 128)
    spec = pl.BlockSpec((block, rows), lambda i, *_: (i, 0))
    kinds = jax.ShapeDtypeStruct
    parts = len(dk_parts)
    in_kernel = shard % 16 == 0
    height = width // 2 if in_kernel else width
    columns = lambda height: pl.BlockSpec((height, 3 * block), lambda i, *_: (0, i))
    dk, dv, keep, send, bias = pl.pallas_call(
        functools.partial(weight_grads_kernel, parts, shard if in_kernel else 0),
        grid_spec=pltpu.PrefetchScalarGridSpec(
            num_scalar_prefetch=1,
            grid=(tall // block,),
            in_specs=[whole_spec((rows, width))] + [spec] * (1 + 2 * parts),
            out_specs=[
                spec,
                spec,
                columns(height),
                columns(height if in_kernel else 16),
                pl.BlockSpec((block, 128), lambda i, *_: (i, 0)),
            ],
        ),
        out_shape=[
            kinds((tall, rows), BF16),
            kinds((tall, rows), BF16),
            kinds((height, 3 * tall), BF16),
            kinds((height if in_kernel else 16, 3 * tall), BF16),
            kinds((tall, 128), F32),
        ],
        compiler_params=pltpu.CompilerParams(vmem_limit_bytes=VMEM_LIMIT),
        cost_estimate=pl.CostEstimate(flops=0, bytes_accessed=0, transcendentals=0),
        name="weight_grads",
    )(core, h_one, d_query, *dk_parts, *dv_parts)
    if not in_kernel:
        both = keep.reshape(-1, 2, shard, 3 * tall)
        keep, send = [
            lax.dynamic_index_in_dim(both, at, 1, keepdims=False).reshape(-1, 3 * tall) for at in (core[0], 1 - core[0])
        ]
    return dk, dv, keep, send, bias


def input_grads_kernel(counts, cut, slot_ref, x_ref, d_res_ref, vectors_ref, w_ref, *refs):
    outs = 2 if cut else 1
    grad_refs, out_refs, sums_ref = refs[: -outs - 1], refs[-outs - 1 : -1], refs[-1]
    width = x_ref.shape[1]

    @pl.when(pl.program_id(0) == 0)
    def _():
        sums_ref[...] = jnp.zeros_like(sums_ref)

    turned = None
    used = 0
    for kind in range(3):
        first = (2, 0, 1)[kind] * width
        groups = []
        for parts in counts[kind]:
            total = grad_refs[used][...]
            for ref in grad_refs[used + 1 : used + parts]:
                total = total + ref[...].astype(F32)
            groups.append(total.astype(BF16))
            used += parts
        grad = jnp.concatenate(groups, axis=0)
        update = dot(w_ref[:, first : first + width], grad, 1, 0)
        turned = update if turned is None else turned + update
    d_h_one = turned.T
    normed, inverse = norm_parts(x_ref[...].astype(F32))
    sums_ref[0:1, :] += add_rows(d_h_one)
    sums_ref[1:2, :] += add_rows(d_h_one * normed)
    grad = (d_res_ref[...] + norm_back(normed, inverse, d_h_one * (1.0 + vectors_ref[1:2, :]))).astype(BF16)
    if not cut:
        out_refs[0][...] = grad.reshape(out_refs[0].shape)
        return

    @pl.when(pl.program_id(0) < cut)
    def _():
        out_refs[0][...] = grad

    @pl.when(pl.program_id(0) >= cut)
    def _():
        out_refs[1][...] = grad


def input_grads(slot, slots, inputs, half, d_residual, vectors, packed, grads, in_two=False):
    rows, width = inputs.shape
    block = pick_block(rows, 256)
    first = half * (rows // block)
    row_spec = pl.BlockSpec((block, width), lambda i, *_: (i, 0))
    flat = [part for kind in grads for group in kind for part in group]
    out_spec, out_shape = row_spec, (rows, width)
    if slots:
        out_spec = pl.BlockSpec((1, block, width), lambda i, at: (at[0], i, 0))
        out_shape = (slots, rows, width)
    out_specs, out_shapes = [out_spec], [out_shape]
    cut = rows // block // 3 if in_two else 0
    if cut:
        out_specs = [
            pl.BlockSpec((block, width), lambda i, *_: (jnp.minimum(i, cut - 1), 0)),
            pl.BlockSpec((block, width), lambda i, *_: (jnp.maximum(i - cut, 0), 0)),
        ]
        out_shapes = [(cut * block, width), (rows - cut * block, width)]
    return pl.pallas_call(
        functools.partial(input_grads_kernel, [[len(group) for group in kind] for kind in grads], cut),
        grid_spec=pltpu.PrefetchScalarGridSpec(
            num_scalar_prefetch=1,
            grid=(rows // block,),
            in_specs=[
                row_spec,
                pl.BlockSpec((block, width), lambda i, *_: (i + first, 0)),
                whole_spec(vectors.shape),
                whole_spec((width, 3 * width)),
            ]
            + [pl.BlockSpec((grad.shape[0], block), lambda i, *_: (0, i + first)) for grad in flat],
            out_specs=out_specs + [whole_spec((8, width))],
        ),
        out_shape=[jax.ShapeDtypeStruct(shape, BF16) for shape in out_shapes] + [jax.ShapeDtypeStruct((8, width), F32)],
        compiler_params=pltpu.CompilerParams(vmem_limit_bytes=VMEM_LIMIT),
        cost_estimate=pl.CostEstimate(
            flops=16 * rows * width * width, bytes_accessed=14 * rows * width + 6 * width * width, transcendentals=0
        ),
        name="input_grads",
    )(slot, inputs, d_residual, vectors, packed, *flat)


def time_features(t_index, model_width):
    half_width = model_width // 2
    indices = jnp.arange(half_width).astype(F32)
    frequency = jnp.exp(indices * (-math.log(10000.0) / (half_width - 1)))
    angles = t_index.astype(F32)[:, None] * frequency[None, :]
    return jnp.concatenate([jnp.sin(angles), jnp.cos(angles)], axis=1)


def rotary_tables(places):
    inverse = jnp.exp(jnp.arange(HALF).astype(F32) * (-2.0 * math.log(10000.0) / HDIM))
    angles = inverse[:, None] * places.astype(F32)[None, :]
    return jnp.cos(angles), jnp.sin(angles)


def after(values, *others):
    return lax.optimization_barrier((values,) + others)[0] if others else values


def make_body(mesh):
    n_dp, n_fsdp = mesh.shape["dp"], mesh.shape["fsdp"]
    n_pairs = n_fsdp // 2

    def shift(values, axis, size, by):
        return lax.ppermute(values, axis, [(i, (i + by) % size) for i in range(size)])

    def pick(values, index, axis=0):
        return lax.dynamic_index_in_dim(values, index, axis, keepdims=False)

    def body(
        frames,
        lengths,
        t_index,
        w_ada,
        b_ada,
        w_query,
        b_query,
        w_key,
        b_key,
        w_value,
        b_value,
        w_out,
        b_out,
        w_up,
        b_up,
        w_down,
        b_down,
        grad_out,
    ):
        slots, local, width = frames.shape
        group = n_fsdp // slots
        hidden_width = w_up.shape[1]
        shard = w_query.shape[0]
        ada_width = w_ada.shape[1]
        dp, fsdp = lax.axis_index("dp"), lax.axis_index("fsdp")
        me = dp * n_fsdp + fsdp
        slot, place = fsdp // group, fsdp % group
        other = 1 - slot
        core, pair = fsdp % 2, fsdp // 2
        side, deep, far = dp % 2, dp // 2, n_dp // 2
        length = pick(lengths, slot)

        def picked(values):
            return pick(values, slot), pick(values, other)

        split = local % 128 == 0

        def swap_in(own, away):
            parts = own, shift(away, "fsdp", n_fsdp, group)
            return parts if split else (jnp.concatenate(parts),) * 2

        def swap_out(*pieces):
            return [shift(piece, "fsdp", n_fsdp, group) for piece in pieces]

        def placed_away(whole, arrived):
            first = 0
            for piece in arrived:
                whole = lax.dynamic_update_slice(whole, piece[None], (other, first, 0))
                first += piece.shape[0]
            return whole

        def placed_own(own):
            return lax.dynamic_update_index_in_dim(jnp.zeros((slots, local, width), own.dtype), own, slot, 0)

        def places_of(member):
            at = slot * group + member
            blocks = [((at - by * group) + n_fsdp) % n_fsdp for by in range(slots)]
            return jnp.concatenate([b * local + jnp.arange(local, dtype=jnp.int32) for b in blocks])

        ring = lambda by: [(i, (i // group) * group + (i % group + by) % group) for i in range(n_fsdp)]

        def swap(values, axis, size):
            return lax.ppermute(values, axis, [(i, i ^ 1) for i in range(size)])

        def sum_core(keep, send, *others):
            arrived = after(swap(send, "fsdp", n_fsdp), *others)
            total = keep.astype(F32) + arrived.astype(F32)
            return total.astype(BF16).reshape(n_dp, n_pairs, shard, keep.shape[1])

        def sum_pairs(values, *others):
            axis = values.ndim - 3
            total = pick(values, pair, axis).astype(F32)
            for by in range(1, n_pairs):
                arrived = after(shift(pick(values, (pair + by) % n_pairs, axis), "fsdp", n_fsdp, 2 * by), *others)
                total = total + arrived.astype(F32)
            return total

        def sum_side(values, *others):
            values = values.reshape((far, 2) + values.shape[1:])
            arrived = after(swap(pick(values, 1 - side, 1), "dp", n_dp), *others)
            return pick(values, side, 1).astype(F32) + arrived.astype(F32)

        def sum_far(values, *others):
            total = pick(values, deep).astype(F32)
            for by in range(1, far):
                arrived = after(shift(pick(values, (deep + by) % far), "dp", n_dp, 2 * by), *others)
                total = total + arrived.astype(F32)
            return total

        def gather_dp(values):
            values = jnp.stack([values] + [shift(values, "dp", n_dp, 2 * by) for by in range(1, far)])
            return jnp.stack([values, swap(values, "dp", n_dp)])

        packed = lax.all_gather(jnp.concatenate([w_key, w_value, w_query], axis=1), AXES, axis=0, tiled=True)
        ups = hidden_width // width
        w_up_turned = w_up.reshape(shard, n_dp * n_fsdp, ups, shard).swapaxes(1, 2).reshape(w_up.shape)
        downs = [w_down[i * shard : (i + 1) * shard] for i in range(ups)]
        packed_two = lax.all_gather(jnp.concatenate([w_out, w_up_turned, *downs], axis=1), AXES, axis=0, tiled=True)

        inputs = swap_in(*picked(frames))
        rows = slots * local
        own_grad, away_grad = picked(grad_out)

        t_all = gather_dp(t_index).reshape(-1)
        active = jax.nn.silu(time_features(t_all, width)).astype(BF16)
        active_mine = lax.dynamic_slice_in_dim(active, me * shard, shard, axis=1)
        partial = [dot(active_mine, w_ada, 1, 0)]
        for bias in (b_query, b_key, b_value, b_out, b_down, *jnp.split(b_up, ups)):
            size = bias.shape[0]
            zeros = jnp.zeros((1, size * n_dp * n_fsdp), F32)
            placed = lax.dynamic_update_slice_in_dim(zeros, bias.astype(F32)[None], me * size, axis=1)
            partial.append(jnp.broadcast_to(placed, (n_dp * slots, placed.shape[1])))
        placed = lax.dynamic_update_slice_in_dim(
            jnp.zeros((1, ada_width), F32), b_ada.astype(F32)[None], me * b_ada.shape[0], axis=1
        )
        partial[0] = partial[0] + placed
        partial = jnp.concatenate(partial, axis=1).reshape(2, far, slots, -1)
        partial = partial[0] + swap(partial[1], "dp", n_dp)
        summed = partial[0]
        for by in range(1, far):
            summed = summed + shift(partial[by], "dp", n_dp, -2 * by)
        one = pick(summed, slot) + shift(pick(summed, other), "fsdp", n_fsdp, group)
        vectors = one
        for by in range(1, group):
            vectors = vectors + lax.ppermute(one, "fsdp", ring(by))
        vectors = vectors.reshape(-1, width)
        vectors = jnp.pad(vectors, ((0, -vectors.shape[0] % 8), (0, 0)))

        key_places = jnp.concatenate([places_of((place - by + group) % group) for by in range(group)])
        cosine, sine = rotary_tables(key_places)
        key_bias = jnp.where(key_places < length, 0.0, -1e30)
        bias_columns = jnp.pad(key_bias.astype(BF16)[:, None], ((0, 0), (0, HDIM - 1)))
        keep = (key_places[:rows] < length).astype(F32)[:, None]

        wide = 2
        vectors, cosine, sine, key_bias, bias_columns, keep, own_grad, away_grad = lax.optimization_barrier(
            (vectors, cosine, sine, key_bias, bias_columns, keep, own_grad, away_grad)
        )
        h_one, q_rot, keys, values = project(inputs, vectors, packed, cosine[:, :rows], sine[:, :rows], wide)
        cotangent = swap_in(own_grad, after(away_grad, keys[0]))
        heads = width // HDIM
        tall = heads // wide
        with_ring = lambda own: [own] + [lax.ppermute(own, "fsdp", ring(by)) for by in range(1, group)]
        k_parts, v_parts = [with_ring(own) for own in keys], [with_ring(own) for own in values]
        heads_out, lses = [], []
        for at in range(wide):
            out, lse = attend(q_rot, k_parts[at], v_parts[at], bias_columns, at * tall)
            heads_out.append(out)
            lses.append(lse)
        at_slot = slot.reshape(1).astype(jnp.int32)
        mixed, away_mixed, d_residual, d_heads, g_rows, sums_two = feed_forward(
            at_slot, inputs, heads_out, cotangent, keep, packed_two, vectors, slots
        )
        if not split:
            mixed, away_mixed = placed_own(mixed[:local]), mixed[local:]
        mixed_arrived = swap_out(away_mixed)

        sum_rows = lax.psum_scatter(g_rows, AXES, scatter_dimension=0, tiled=True)

        grads, d_biases = ([], [], []), []
        at_core = core.reshape(1).astype(jnp.int32)

        def sum_parts(dq, dk_parts, dv_parts, *others):
            dk_parts = [after(dk_parts[0], *others)] + dk_parts[1:]
            dk, dv, keep, send, bias_grad = weight_grads(at_core, shard, h_one, dq, dk_parts, dv_parts)
            for kind, grad in zip(grads, (dq, dk, dv)):
                kind.append([grad])
            d_biases.append(bias_grad[:, :3])
            return keep, send

        counts = (tall, tall // 2, tall // 2)
        first, ready, arrived = 0, d_heads, []
        for step, each in enumerate(counts):
            part, within = first // tall, first % tall
            dq, dk_parts, dv_parts = attend_back(
                q_rot,
                k_parts[part],
                v_parts[part],
                ready,
                heads_out[part],
                lses[part],
                key_bias[None],
                cosine,
                sine,
                first,
                within,
                each,
            )
            first += each
            dk_parts = [dk_parts[0]] + [lax.ppermute(dk_parts[by], "fsdp", ring(-by)) for by in range(1, group)]
            dv_parts = [dv_parts[0]] + [lax.ppermute(dv_parts[by], "fsdp", ring(-by)) for by in range(1, group)]
            arrived.append((dq, dk_parts, dv_parts))
            if step == 1:
                early = sum_parts(*arrived[0], dq)
                ready = after(d_heads, dq, early[0])
        early_sum = sum_core(*early, dq)
        if split:
            in_parts = [
                grads[0] + [[piece[0]] for piece in arrived[1:]],
                grads[1] + [piece[1] for piece in arrived[1:]],
                grads[2] + [piece[2] for piece in arrived[1:]],
            ]
            rest = after(d_residual, early_sum)
            *away_frames, sums_away = input_grads(at_slot, 0, inputs[1], 1, rest, vectors, packed, in_parts, True)
            frames_arrived = swap_out(*away_frames)
            early_sum = sum_pairs(early_sum, sums_away).astype(BF16)
            middle = sum_parts(*arrived[1], sums_away)
            last = sum_parts(*arrived[2], middle[0], sum_rows, *mixed_arrived, frames_arrived[0])
            core_sums = jnp.concatenate([sum_core(*sums, last[0]) for sums in (middle, last)], axis=-1)
            rest, core_sums = lax.optimization_barrier((d_residual, core_sums))
            own_frames, sums_own = input_grads(at_slot, slots, inputs[0], 0, rest, vectors, packed, grads)
            sums_one = sums_own + sums_away
        else:
            early_sum = sum_pairs(early_sum).astype(BF16)
            middle, last = sum_parts(*arrived[1]), sum_parts(*arrived[2])
            core_sums = jnp.concatenate([sum_core(*sums) for sums in (middle, last)], axis=-1)
            both, sums_one = input_grads(at_slot, 0, inputs[0], 0, d_residual, vectors, packed, grads)
            own_frames, frames_arrived = placed_own(both[:local]), swap_out(both[local:])
        side_sums = sum_side(core_sums).astype(BF16)
        early_sum = sum_side(early_sum, side_sums).astype(BF16)

        vector = jnp.concatenate(
            [sums_one[:2], sums_two[: 6 + ups], jnp.concatenate(d_biases).T]
        )
        for_slot = 6
        vector = after(vector, *frames_arrived)
        total = vector
        for by in range(1, group):
            total = total + lax.ppermute(vector, "fsdp", ring(by))
        total, side_sums = lax.optimization_barrier((total, side_sums))
        all_sums = sum_far(jnp.concatenate([early_sum[:, None], side_sums], axis=1))
        sums = [all_sums[0], sum_pairs(all_sums[1:].astype(BF16))]
        sum_rows, mixed = after(sum_rows, total).astype(F32), after(mixed, total)
        g_out = sum_rows[:, :width]
        g_up = sum_rows[:, width : width + hidden_width].reshape(shard, ups, n_dp * n_fsdp, shard)
        g_up = g_up.swapaxes(1, 2).reshape(w_up.shape)
        g_down = jnp.concatenate([sum_rows[:, (1 + ups + i) * width : (2 + ups + i) * width] for i in range(ups)])
        mixed = placed_away(mixed, mixed_arrived)
        packs = gather_dp(total).reshape(n_dp, -1, width)
        pack = jnp.concatenate([packs[:, :for_slot].reshape(-1, width), jnp.sum(packs[:, for_slot:], axis=0)])
        pack, g_out, g_up, g_down, mixed = lax.optimization_barrier((pack, g_out, g_up, g_down, mixed))
        grad_frames = placed_away(own_frames, frames_arrived)
        across = shift(pack, "fsdp", n_fsdp, group)
        count = n_dp * for_slot
        d_mod = jnp.stack([jnp.where(slot == s, pack[:count], across[:count]).reshape(n_dp, -1) for s in range(slots)], axis=1)
        d_mod = d_mod.reshape(n_dp * slots, for_slot * width)
        d_vectors = pack[count:] + across[count:]

        g_w_ada = lax.dot_general(
            active_mine.astype(F32),
            d_mod,
            (((0,), (0,)), ((), ())),
            precision=lax.Precision.HIGHEST,
            preferred_element_type=F32,
        )

        def mine(vector):
            vector = vector.reshape(-1)
            size = vector.shape[0] // (n_dp * n_fsdp)
            return lax.dynamic_slice_in_dim(vector, me * size, size)

        columns = jnp.concatenate(sums, axis=1).reshape(shard, -1, 3, pick_block(tall // 2 * HDIM, 128))
        g_qkv = [columns[:, :, i].reshape(shard, width) for i in range(3)]
        return (
            mixed,
            grad_frames,
            g_w_ada,
            mine(jnp.sum(d_mod, axis=0)),
            g_qkv[0],
            mine(d_vectors[2 + ups]),
            g_qkv[1],
            mine(d_vectors[3 + ups]),
            g_qkv[2],
            mine(d_vectors[4 + ups]),
            g_out,
            mine(d_vectors[0]),
            g_up,
            jnp.concatenate([mine(d_vectors[2 + i]) for i in range(ups)]),
            g_down,
            mine(d_vectors[1]),
        )

    return body


def solution(mesh):
    rows, vector, matrix = P("dp", "fsdp", None), P(AXES), P(AXES, None)
    return jax.shard_map(
        make_body(mesh),
        mesh=mesh,
        in_specs=(rows, P("dp"), P("dp")) + (matrix, vector) * 7 + (rows,),
        out_specs=(rows, rows) + (matrix, vector) * 7,
        check_vma=False,
    )
```

```python
import functools
import math

import jax
import jax.numpy as jnp
from jax import lax
from jax.experimental import pallas as pl
from jax.experimental.pallas import tpu as pltpu
from jax.sharding import PartitionSpec as P

HDIM = 64
HALF = HDIM // 2
SCALE = HDIM ** (-0.5)
SCALE2 = SCALE * math.log2(math.e)
AXES = ("dp", "fsdp")
VMEM_LIMIT = 62 << 20
F32 = jnp.float32
BF16 = jnp.bfloat16


def dot(left_side, right_side, left_dim, right_dim):
    return lax.dot_general(
        left_side,
        right_side,
        (((left_dim,), (right_dim,)), ((), ())),
        preferred_element_type=F32,
    )


def pick_block(total, wanted):
    block = min(total, wanted)
    while total % block:
        block -= 128
    return block


def attend_kernel(parts, chunk, *refs):
    q_ref, bias_ref = refs[0], refs[1]
    k_refs, v_refs = refs[2 : 2 + parts], refs[2 + parts : 2 + 2 * parts]
    o_ref, lse_ref, k_aug, v_aug, q_aug = refs[2 + 2 * parts :]
    head, block = pl.program_id(0), pl.program_id(1)
    span = k_aug.shape[0]
    part = span // parts
    q_rows = q_ref.shape[1]

    @pl.when((head == 0) & (block == 0))
    def _():
        k_aug[:, HDIM:] = bias_ref[...]
        v_aug[HDIM:, :] = jnp.ones((16, span), BF16)
        q_aug[HDIM:, :] = jnp.ones((HDIM, q_rows), BF16)

    @pl.when(block == 0)
    def _():
        for i in range(parts):
            k_aug[i * part : (i + 1) * part, :HDIM] = k_refs[i][...].T
            v_aug[:HDIM, i * part : (i + 1) * part] = v_refs[i][...]

    q_aug[:HDIM, :] = q_ref[...]
    queries = q_aug[...]
    count = span // chunk

    def scores(i):
        return dot(k_aug[i * chunk : (i + 1) * chunk, :], queries, 1, 0)

    upcoming = scores(0)
    row_max = total = None
    for i in range(count):
        current = upcoming
        if i + 1 < count:
            upcoming = scores(i + 1)
        chunk_max = jnp.max(current, axis=0, keepdims=True) * SCALE2
        new_max = chunk_max if i == 0 else jnp.maximum(row_max, chunk_max)
        weights = jnp.exp2(current * SCALE2 - new_max).astype(BF16)
        update = dot(v_aug[:, i * chunk : (i + 1) * chunk], weights, 1, 0)
        total = update if i == 0 else total * jnp.exp2(row_max - new_max) + update
        row_max = new_max
    denominator = total[HDIM : HDIM + 1, :]
    o_ref[...] = (total[:HDIM, :] / denominator).astype(BF16)
    lse_ref[...] = (row_max + jnp.log2(denominator))[None]


def attend(q_rot, k_parts, v_parts, bias_columns, first):
    width, rows = k_parts[0].shape
    parts = len(k_parts)
    span = parts * rows
    heads = width // HDIM
    q_rows = pick_block(rows, 768)
    chunk = pick_block(span, 256)
    q_spec = pl.BlockSpec((HDIM, q_rows), lambda h, j: (h + first, j))
    k_spec = pl.BlockSpec((HDIM, rows), lambda h, j: (h, 0))
    return pl.pallas_call(
        functools.partial(attend_kernel, parts, chunk),
        grid=(heads, rows // q_rows),
        in_specs=[q_spec, pl.BlockSpec((span, HDIM), lambda h, j: (0, 0))] + [k_spec] * (2 * parts),
        out_specs=[
            pl.BlockSpec((HDIM, q_rows), lambda h, j: (h, j)),
            pl.BlockSpec((1, 1, q_rows), lambda h, j: (h, 0, j)),
        ],
        out_shape=[
            jax.ShapeDtypeStruct((width, rows), BF16),
            jax.ShapeDtypeStruct((heads, 1, rows), F32),
        ],
        scratch_shapes=[
            pltpu.VMEM((span, 2 * HDIM), BF16),
            pltpu.VMEM((HDIM + 16, span), BF16),
            pltpu.VMEM((2 * HDIM, q_rows), BF16),
        ],
        compiler_params=pltpu.CompilerParams(vmem_limit_bytes=VMEM_LIMIT),
        cost_estimate=pl.CostEstimate(
            flops=16 * heads * rows * span * HDIM,
            bytes_accessed=2 * width * (2 * rows + 2 * span),
            transcendentals=heads * rows * span,
        ),
        name="attend",
    )(q_rot, bias_columns, *k_parts, *v_parts)


def in_three(values):
    first = values.astype(BF16)
    rest = values - first.astype(F32)
    second = rest.astype(BF16)
    return first.astype(F32), second.astype(F32), rest - second.astype(F32)


def unrotate(values, cosine, sine):
    low, high = values[:HALF], values[HALF:]
    return low * cosine + high * sine, high * cosine - low * sine


def attend_back_kernel(parts, chunk, *refs):
    q_ref, do_ref, o_ref, lse_ref, bias_ref, cos_ref, sin_ref = refs[:7]
    k_refs, v_refs = refs[7 : 7 + parts], refs[7 + parts : 7 + 2 * parts]
    dq_ref = refs[7 + 2 * parts]
    dk_refs = refs[8 + 2 * parts : 8 + 3 * parts]
    dv_refs = refs[8 + 3 * parts : 8 + 4 * parts]
    k_aug, v_aug, k_rows, q_aug, do_aug, dk_acc, dv_acc = refs[8 + 4 * parts :]
    head, block = pl.program_id(0), pl.program_id(1)
    span = k_aug.shape[1]
    part = span // parts
    q_rows = q_ref.shape[1]

    @pl.when((head == 0) & (block == 0))
    def _():
        row = lax.broadcasted_iota(jnp.int32, (HDIM, span), 0)
        ones = jnp.where(row < 4, 1.0, 0.0)
        k_aug[HDIM:, :] = jnp.where(row == 0, bias_ref[...], ones).astype(BF16)
        v_aug[HDIM:, :] = jnp.where(row < 3, 1.0, 0.0).astype(BF16)
        k_rows[:, HDIM:] = jnp.zeros((span, HDIM), BF16)

    @pl.when(block == 0)
    def _():
        for i in range(parts):
            at = slice(i * part, (i + 1) * part)
            keys = k_refs[i][...]
            k_aug[:HDIM, at] = keys
            v_aug[:HDIM, at] = v_refs[i][...]
            k_rows[at, :HDIM] = keys.T
        dk_acc[...] = jnp.zeros_like(dk_acc)
        dv_acc[...] = jnp.zeros_like(dv_acc)

    queries, d_heads = q_ref[...], do_ref[...]
    delta = jnp.sum(d_heads.astype(F32) * o_ref[...].astype(F32), axis=0, keepdims=True)
    row = lax.broadcasted_iota(jnp.int32, (HDIM, q_rows), 0)
    lse_a, lse_b, lse_c = in_three(lse_ref[0] * (-1.0 / SCALE2))
    del_a, del_b, del_c = in_three(-delta)
    q_extra = jnp.where(row == 2, lse_b, jnp.where(row == 3, lse_c, 0.0))
    q_extra = jnp.where(row == 0, 1.0, jnp.where(row == 1, lse_a, q_extra))
    do_extra = jnp.where(row == 1, del_b, jnp.where(row == 2, del_c, 0.0))
    do_extra = jnp.where(row == 0, del_a, do_extra)
    q_aug[:HDIM, :] = queries
    q_aug[HDIM:, :] = q_extra.astype(BF16)
    do_aug[:HDIM, :] = d_heads
    do_aug[HDIM:, :] = do_extra.astype(BF16)
    q_side, do_side = q_aug[...].T, do_aug[...].T
    count = span // chunk

    def products(i):
        at = slice(i * chunk, (i + 1) * chunk)
        return dot(q_side, k_aug[:, at], 1, 0), dot(do_side, v_aug[:, at], 1, 0)

    upcoming = products(0)
    d_query = None
    for i in range(count):
        at = slice(i * chunk, (i + 1) * chunk)
        scores, d_probs = upcoming
        if i + 1 < count:
            upcoming = products(i + 1)
        probs = jnp.exp2(scores * SCALE2)
        d_scores = (probs * d_probs).astype(BF16)
        dv_acc[:, at] += dot(d_heads, probs.astype(BF16), 1, 0)
        dk_acc[:, at] += dot(queries, d_scores, 1, 0)
        update = dot(d_scores, k_rows[at, :], 1, 0)
        d_query = update if i == 0 else d_query + update
    first = pl.multiple_of(block * q_rows, q_rows)
    low, high = unrotate(
        d_query.T[:HDIM, :] * SCALE, cos_ref[:, pl.ds(first, q_rows)], sin_ref[:, pl.ds(first, q_rows)]
    )
    dq_ref[:HALF, :] = low.astype(BF16)
    dq_ref[HALF:, :] = high.astype(BF16)

    @pl.when(block == pl.num_programs(1) - 1)
    def _():
        for i in range(parts):
            at = slice(i * part, (i + 1) * part)
            low, high = unrotate(dk_acc[:, at] * SCALE, cos_ref[:, at], sin_ref[:, at])
            dk_refs[i][:HALF, :] = low.astype(dk_refs[i].dtype)
            dk_refs[i][HALF:, :] = high.astype(dk_refs[i].dtype)
            dv_refs[i][...] = dv_acc[:, at].astype(dv_refs[i].dtype)


def attend_back(q_rot, k_parts, v_parts, d_heads, heads_out, lse, bias_row, cosine, sine, first, within, count):
    rows = q_rot.shape[1]
    parts = len(k_parts)
    span = parts * rows
    q_rows = pick_block(rows, 1536)
    chunk = pick_block(span, 128)
    q_spec = pl.BlockSpec((HDIM, q_rows), lambda h, j: (h + first, j))
    k_spec = pl.BlockSpec((HDIM, rows), lambda h, j: (h + within, 0))
    whole = lambda array: pl.BlockSpec(array.shape, lambda h, j: (0, 0))
    part_out = pl.BlockSpec((HDIM, rows), lambda h, j: (h, 0))
    shape = lambda kind: jax.ShapeDtypeStruct((count * HDIM, rows), kind)
    part_kinds = [F32] + [BF16] * (parts - 1)
    out = pl.pallas_call(
        functools.partial(attend_back_kernel, parts, chunk),
        grid=(count, rows // q_rows),
        in_specs=[
            q_spec,
            q_spec,
            pl.BlockSpec((HDIM, q_rows), lambda h, j: (h + within, j)),
            pl.BlockSpec((1, 1, q_rows), lambda h, j: (h + within, 0, j)),
            whole(bias_row),
            whole(cosine),
            whole(sine),
        ]
        + [k_spec] * (2 * parts),
        out_specs=[pl.BlockSpec((HDIM, q_rows), lambda h, j: (h, j))] + [part_out] * (2 * parts),
        out_shape=[shape(BF16)] + [shape(kind) for kind in part_kinds * 2],
        scratch_shapes=[
            pltpu.VMEM((2 * HDIM, span), BF16),
            pltpu.VMEM((2 * HDIM, span), BF16),
            pltpu.VMEM((span, 2 * HDIM), BF16),
            pltpu.VMEM((2 * HDIM, q_rows), BF16),
            pltpu.VMEM((2 * HDIM, q_rows), BF16),
            pltpu.VMEM((HDIM, span), F32),
            pltpu.VMEM((HDIM, span), F32),
        ],
        compiler_params=pltpu.CompilerParams(vmem_limit_bytes=VMEM_LIMIT),
        cost_estimate=pl.CostEstimate(
            flops=5 * count * rows * span * HDIM,
            bytes_accessed=0,
            transcendentals=0,
        ),
        name="attend_back",
    )(q_rot, d_heads, heads_out, lse, bias_row, cosine, sine, *k_parts, *v_parts)
    return out[0], out[1 : 1 + parts], out[1 + parts :]


def norm_parts(values):
    centered = values - jnp.mean(values, axis=-1, keepdims=True)
    scale = lax.rsqrt(jnp.mean(centered * centered, axis=-1, keepdims=True) + 1e-06)
    return centered * scale, scale


def norm_back(normed, scale, d_normed):
    return (
        d_normed
        - jnp.mean(d_normed, axis=-1, keepdims=True)
        - normed * jnp.mean(d_normed * normed, axis=-1, keepdims=True)
    ) * scale


def gelu_both(values):
    square = values * values
    bend = jnp.tanh(0.7978845608028654 * (values + 0.044715 * values * square))
    half = 0.5 * (1.0 + bend)
    slope = 0.7978845608028654 * (1.0 + 3 * 0.044715 * square)
    return values * half, half + 0.5 * values * (1.0 - bend * bend) * slope


def add_rows(values):
    return jnp.sum(values, axis=0, keepdims=True)


def store_rotated(out_ref, values, cosine, sine):
    for at in range(0, out_ref.shape[0], HDIM):
        low, high = values[at : at + HALF], values[at + HALF : at + HDIM]
        out_ref[at : at + HALF, :] = (low * cosine - high * sine).astype(BF16)
        out_ref[at + HALF : at + HDIM, :] = (high * cosine + low * sine).astype(BF16)


def either(first_ref, second_ref):
    half = pl.num_programs(0) // 2
    return jnp.where(pl.program_id(0) < half, first_ref[...], second_ref[...])


def halves_spec(inputs, rows, block, width):
    if inputs[0].shape[0] == rows:
        return [pl.BlockSpec((block, width), lambda i, *_: (i, 0))] * 2
    half = rows // 2 // block
    return [
        pl.BlockSpec((block, width), lambda i, *_: (jnp.minimum(i, half - 1), 0)),
        pl.BlockSpec((block, width), lambda i, *_: (jnp.maximum(i - half, 0), 0)),
    ]


def project_kv_kernel(groups, x_ref, y_ref, vectors_ref, w_ref, cos_ref, sin_ref, h_ref, *refs):
    k_refs, v_refs = refs[:groups], refs[groups:]
    width = x_ref.shape[1]
    tall = width // groups
    normed, _ = norm_parts(either(x_ref, y_ref).astype(F32))
    h_one = (normed * (1.0 + vectors_ref[1:2, :]) + vectors_ref[0:1, :]).astype(BF16)
    h_ref[...] = h_one
    keys = (dot(h_one, w_ref[:, :width], 1, 0) + vectors_ref[7:8, :]).T
    values = (dot(h_one, w_ref[:, width:], 1, 0) + vectors_ref[8:9, :]).astype(BF16).T
    for i in range(groups):
        store_rotated(k_refs[i], keys[i * tall : (i + 1) * tall], cos_ref[...], sin_ref[...])
        v_refs[i][...] = values[i * tall : (i + 1) * tall]


def project_q_kernel(h_ref, vectors_ref, w_ref, cos_ref, sin_ref, q_ref):
    queries = dot(h_ref[...], w_ref[...], 1, 0) + vectors_ref[6:7, :]
    store_rotated(q_ref, queries.T, cos_ref[...], sin_ref[...])


def whole_spec(shape, column=0):
    return pl.BlockSpec(shape, lambda i, *_: (0, column), pipeline_mode=pl.Buffered(1))


def project(inputs, vectors, packed, cosine, sine, groups):
    width, rows = inputs[0].shape[1], cosine.shape[1]
    block = pick_block(inputs[0].shape[0], 256)
    tall = width // groups
    row_spec = pl.BlockSpec((block, width), lambda i: (i, 0))
    turned_spec = lambda height: pl.BlockSpec((height, block), lambda i: (0, i))
    turned = lambda height: jax.ShapeDtypeStruct((height, rows), BF16)
    table_spec = turned_spec(HALF)
    params = pltpu.CompilerParams(vmem_limit_bytes=VMEM_LIMIT)
    out = pl.pallas_call(
        functools.partial(project_kv_kernel, groups),
        grid=(rows // block,),
        in_specs=halves_spec(inputs, rows, block, width)
        + [whole_spec(vectors.shape), whole_spec((width, 2 * width)), table_spec, table_spec],
        out_specs=[row_spec] + [turned_spec(tall)] * (2 * groups),
        out_shape=[jax.ShapeDtypeStruct((rows, width), BF16)] + [turned(tall)] * (2 * groups),
        compiler_params=params,
        cost_estimate=pl.CostEstimate(
            flops=8 * rows * width * width, bytes_accessed=8 * rows * width + 4 * width * width, transcendentals=0
        ),
        name="project_kv",
    )(*inputs, vectors, packed, cosine, sine)
    h_one, keys, values = out[0], out[1 : 1 + groups], out[1 + groups :]
    queries = pl.pallas_call(
        project_q_kernel,
        grid=(rows // block,),
        in_specs=[row_spec, whole_spec(vectors.shape), whole_spec((width, width), 2), table_spec, table_spec],
        out_specs=turned_spec(width),
        out_shape=turned(width),
        compiler_params=params,
        cost_estimate=pl.CostEstimate(
            flops=4 * rows * width * width, bytes_accessed=4 * rows * width + 2 * width * width, transcendentals=0
        ),
        name="project_q",
    )(h_one, vectors, packed, cosine, sine)
    return h_one, queries, keys, values


def feed_forward_kernel(parts, pieces, split, slot_ref, *refs):
    o_refs = refs[:parts]
    x_ref, y_ref, cot_ref, cot_y_ref, keep_ref, w_ref, vectors_ref = refs[parts : parts + 7]
    own_ref, away_ref, d_res_ref, d_heads_ref, g_rows_ref, sums_ref = refs[parts + 7 : parts + 13]
    acc, acc_rows, slope_ref, hidden_ref, staged, sems = refs[parts + 13 :]
    step, count = pl.program_id(0), pl.num_programs(0)
    width = x_ref.shape[1]

    @pl.when(step == 0)
    def _():
        acc[...] = jnp.zeros_like(acc)
        acc_rows[...] = jnp.zeros_like(acc_rows)

    gate_one, shift_two, scale_two, gate_two, b_out, b_down = [vectors_ref[i : i + 1, :] for i in (2, 3, 4, 5, 9, 10)]
    out_at = slice(0, width)
    up_at = [slice((1 + i) * width, (2 + i) * width) for i in range(pieces)]
    down_at = [slice((1 + pieces + i) * width, (2 + pieces + i) * width) for i in range(pieces)]
    keep = keep_ref[...]
    heads_out = jnp.concatenate([ref[...] for ref in o_refs], axis=0)
    branch = (dot(heads_out, w_ref[:, out_at], 0, 0) + b_out) * keep
    residual = either(x_ref, y_ref).astype(F32) + gate_one * branch
    normed, inverse = norm_parts(residual)
    h_two = (normed * (1.0 + scale_two) + shift_two).astype(BF16)
    ff_out = b_down
    for i in range(pieces):
        value, slope = gelu_both(dot(h_two, w_ref[:, up_at[i]], 1, 0) + vectors_ref[11 + i : 12 + i, :])
        slope_ref[i] = slope
        hidden = value.astype(BF16)
        hidden_ref[i] = hidden
        ff_out = ff_out + dot(hidden, w_ref[:, down_at[i]], 1, 0)
    mixed = (residual + gate_two * ff_out).astype(BF16)
    if split:

        @pl.when(step < count // 2)
        def _():
            own_ref[0] = mixed

        @pl.when(step >= count // 2)
        def _():
            away_ref[...] = mixed
    else:
        own_ref[...] = mixed
    d_mixed = either(cot_ref, cot_y_ref).astype(F32)
    acc_rows[3:4, :] += add_rows(d_mixed * ff_out)
    d_ff = (d_mixed * gate_two).astype(BF16)
    acc_rows[5:6, :] += add_rows(d_ff.astype(F32))
    d_h_two = None
    for i in range(pieces):
        acc[:, down_at[i]] += dot(hidden_ref[i], d_ff, 0, 0)
        d_up = (dot(d_ff, w_ref[:, down_at[i]], 1, 1) * slope_ref[i]).astype(BF16)
        acc_rows[6 + i : 7 + i, :] += add_rows(d_up.astype(F32))
        acc[:, up_at[i]] += dot(h_two, d_up, 0, 0)
        update = dot(d_up, w_ref[:, up_at[i]], 1, 1)
        d_h_two = update if i == 0 else d_h_two + update
    acc_rows[1:2, :] += add_rows(d_h_two)
    acc_rows[2:3, :] += add_rows(d_h_two * normed)
    d_residual = d_mixed + norm_back(normed, inverse, d_h_two * (1.0 + scale_two))
    d_res_ref[...] = d_residual
    acc_rows[0:1, :] += add_rows(d_residual * branch)
    d_branch = (d_residual * gate_one * keep).astype(BF16)
    acc_rows[4:5, :] += add_rows(d_branch.astype(F32))
    acc[:, out_at] += dot(heads_out, d_branch, 1, 0)
    d_heads_ref[...] = dot(w_ref[:, out_at], d_branch, 1, 1).astype(BF16)

    @pl.when(step == count - 1)
    def _():
        sums_ref[...] = acc_rows[...]
        tall = staged.shape[1]
        copies = []
        for i in range(width // tall):
            slot = i % 2
            if i >= 2:
                copies[i - 2].wait()
            staged[slot] = acc[i * tall : (i + 1) * tall, :].astype(BF16)
            copies.append(pltpu.make_async_copy(staged.at[slot], g_rows_ref.at[pl.ds(i * tall, tall), :], sems.at[slot]))
            copies[i].start()
        for copy in copies[-2:]:
            copy.wait()


def feed_forward(slot, inputs, heads_out, cotangent, keep, packed, vectors, slots):
    rows, width = heads_out[0].shape[1], inputs[0].shape[1]
    pieces = (packed.shape[1] // width - 1) // 2
    block = pick_block(inputs[0].shape[0], 256)
    local = rows // slots
    split = inputs[0].shape[0] == local
    half = local // block
    row_spec = pl.BlockSpec((block, width), lambda i, *_: (i, 0))
    turned_spec = lambda height: pl.BlockSpec((height, block), lambda i, *_: (0, i))
    kinds = jax.ShapeDtypeStruct
    if split:
        mixed_specs = [
            pl.BlockSpec((1, block, width), lambda i, at: (at[0], jnp.minimum(i, half - 1), 0)),
            pl.BlockSpec((block, width), lambda i, *_: (jnp.maximum(i - half, 0), 0)),
        ]
        mixed_shapes = [kinds((slots, local, width), BF16), kinds((local, width), BF16)]
    else:
        mixed_specs = [row_spec, whole_spec((8, 128))]
        mixed_shapes = [kinds((rows, width), BF16), kinds((8, 128), BF16)]
    return pl.pallas_call(
        functools.partial(feed_forward_kernel, len(heads_out), pieces, split),
        grid_spec=pltpu.PrefetchScalarGridSpec(
            num_scalar_prefetch=1,
            grid=(rows // block,),
            in_specs=[turned_spec(part.shape[0]) for part in heads_out]
            + halves_spec(inputs, rows, block, width) * 2
            + [
                pl.BlockSpec((block, 1), lambda i, *_: (i, 0)),
                whole_spec(packed.shape),
                whole_spec(vectors.shape),
            ],
            out_specs=mixed_specs
            + [
                row_spec,
                turned_spec(width),
                pl.BlockSpec(memory_space=pl.ANY),
                whole_spec((8, width)),
            ],
            scratch_shapes=[
                pltpu.VMEM(packed.shape, F32),
                pltpu.VMEM((8, width), F32),
                pltpu.VMEM((pieces, block, width), F32),
                pltpu.VMEM((pieces, block, width), BF16),
                pltpu.VMEM((2, pick_block(width, 256), packed.shape[1]), BF16),
                pltpu.SemaphoreType.DMA((2,)),
            ],
        ),
        out_shape=mixed_shapes
        + [
            kinds((rows, width), F32),
            kinds((width, rows), BF16),
            kinds(packed.shape, BF16),
            kinds((8, width), F32),
        ],
        compiler_params=pltpu.CompilerParams(vmem_limit_bytes=VMEM_LIMIT),
        cost_estimate=pl.CostEstimate(
            flops=6 * rows * width * packed.shape[1],
            bytes_accessed=8 * rows * width + 4 * width * packed.shape[1],
            transcendentals=0,
        ),
        name="feed_forward",
    )(slot, *heads_out, *inputs, *cotangent, keep, packed, vectors)


def weight_grads_kernel(parts, shard, core_ref, h_ref, dq_ref, *refs):
    dk_refs, dv_refs = refs[:parts], refs[parts : 2 * parts]
    dk_out, dv_out, keep_ref, send_ref, bias_ref = refs[2 * parts :]

    def summed(pieces):
        total = pieces[0][...]
        for ref in pieces[1:]:
            total = total + ref[...].astype(F32)
        return total.astype(BF16)

    grads = [dq_ref[...], summed(dk_refs), summed(dv_refs)]
    dk_out[...] = grads[1]
    dv_out[...] = grads[2]
    weight_grad = dot(jnp.concatenate(grads, axis=0), h_ref[...], 1, 0).T.astype(BF16)
    for i, grad in enumerate(grads):
        bias_ref[:, i : i + 1] = jnp.sum(grad.astype(F32), axis=1, keepdims=True)
    if not shard:
        keep_ref[...] = weight_grad
        return

    def store(even_ref, odd_ref):
        for i in range(0, weight_grad.shape[0] // 2, shard):
            even_ref[i : i + shard, :] = weight_grad[2 * i : 2 * i + shard]
            odd_ref[i : i + shard, :] = weight_grad[2 * i + shard : 2 * (i + shard)]

    @pl.when(core_ref[0] == 0)
    def _():
        store(keep_ref, send_ref)

    @pl.when(core_ref[0] != 0)
    def _():
        store(send_ref, keep_ref)


def weight_grads(core, shard, h_one, d_query, dk_parts, dv_parts):
    rows, width = h_one.shape
    tall = d_query.shape[0]
    block = pick_block(tall, 128)
    spec = pl.BlockSpec((block, rows), lambda i, *_: (i, 0))
    kinds = jax.ShapeDtypeStruct
    parts = len(dk_parts)
    in_kernel = shard % 16 == 0
    height = width // 2 if in_kernel else width
    columns = lambda height: pl.BlockSpec((height, 3 * block), lambda i, *_: (0, i))
    dk, dv, keep, send, bias = pl.pallas_call(
        functools.partial(weight_grads_kernel, parts, shard if in_kernel else 0),
        grid_spec=pltpu.PrefetchScalarGridSpec(
            num_scalar_prefetch=1,
            grid=(tall // block,),
            in_specs=[whole_spec((rows, width))] + [spec] * (1 + 2 * parts),
            out_specs=[
                spec,
                spec,
                columns(height),
                columns(height if in_kernel else 16),
                pl.BlockSpec((block, 128), lambda i, *_: (i, 0)),
            ],
        ),
        out_shape=[
            kinds((tall, rows), BF16),
            kinds((tall, rows), BF16),
            kinds((height, 3 * tall), BF16),
            kinds((height if in_kernel else 16, 3 * tall), BF16),
            kinds((tall, 128), F32),
        ],
        compiler_params=pltpu.CompilerParams(vmem_limit_bytes=VMEM_LIMIT),
        cost_estimate=pl.CostEstimate(flops=0, bytes_accessed=0, transcendentals=0),
        name="weight_grads",
    )(core, h_one, d_query, *dk_parts, *dv_parts)
    if not in_kernel:
        both = keep.reshape(-1, 2, shard, 3 * tall)
        keep, send = [
            lax.dynamic_index_in_dim(both, at, 1, keepdims=False).reshape(-1, 3 * tall) for at in (core[0], 1 - core[0])
        ]
    return dk, dv, keep, send, bias


def input_grads_kernel(counts, cut, slot_ref, x_ref, d_res_ref, vectors_ref, w_ref, *refs):
    outs = 2 if cut else 1
    grad_refs, out_refs, sums_ref = refs[: -outs - 1], refs[-outs - 1 : -1], refs[-1]
    width = x_ref.shape[1]

    @pl.when(pl.program_id(0) == 0)
    def _():
        sums_ref[...] = jnp.zeros_like(sums_ref)

    turned = None
    used = 0
    for kind in range(3):
        first = (2, 0, 1)[kind] * width
        groups = []
        for parts in counts[kind]:
            total = grad_refs[used][...]
            for ref in grad_refs[used + 1 : used + parts]:
                total = total + ref[...].astype(F32)
            groups.append(total.astype(BF16))
            used += parts
        grad = jnp.concatenate(groups, axis=0)
        update = dot(w_ref[:, first : first + width], grad, 1, 0)
        turned = update if turned is None else turned + update
    d_h_one = turned.T
    normed, inverse = norm_parts(x_ref[...].astype(F32))
    sums_ref[0:1, :] += add_rows(d_h_one)
    sums_ref[1:2, :] += add_rows(d_h_one * normed)
    grad = (d_res_ref[...] + norm_back(normed, inverse, d_h_one * (1.0 + vectors_ref[1:2, :]))).astype(BF16)
    if not cut:
        out_refs[0][...] = grad.reshape(out_refs[0].shape)
        return

    @pl.when(pl.program_id(0) < cut)
    def _():
        out_refs[0][...] = grad

    @pl.when(pl.program_id(0) >= cut)
    def _():
        out_refs[1][...] = grad


def input_grads(slot, slots, inputs, half, d_residual, vectors, packed, grads, in_two=False):
    rows, width = inputs.shape
    block = pick_block(rows, 256)
    first = half * (rows // block)
    row_spec = pl.BlockSpec((block, width), lambda i, *_: (i, 0))
    flat = [part for kind in grads for group in kind for part in group]
    out_spec, out_shape = row_spec, (rows, width)
    if slots:
        out_spec = pl.BlockSpec((1, block, width), lambda i, at: (at[0], i, 0))
        out_shape = (slots, rows, width)
    out_specs, out_shapes = [out_spec], [out_shape]
    cut = rows // block // 3 if in_two else 0
    if cut:
        out_specs = [
            pl.BlockSpec((block, width), lambda i, *_: (jnp.minimum(i, cut - 1), 0)),
            pl.BlockSpec((block, width), lambda i, *_: (jnp.maximum(i - cut, 0), 0)),
        ]
        out_shapes = [(cut * block, width), (rows - cut * block, width)]
    return pl.pallas_call(
        functools.partial(input_grads_kernel, [[len(group) for group in kind] for kind in grads], cut),
        grid_spec=pltpu.PrefetchScalarGridSpec(
            num_scalar_prefetch=1,
            grid=(rows // block,),
            in_specs=[
                row_spec,
                pl.BlockSpec((block, width), lambda i, *_: (i + first, 0)),
                whole_spec(vectors.shape),
                whole_spec((width, 3 * width)),
            ]
            + [pl.BlockSpec((grad.shape[0], block), lambda i, *_: (0, i + first)) for grad in flat],
            out_specs=out_specs + [whole_spec((8, width))],
        ),
        out_shape=[jax.ShapeDtypeStruct(shape, BF16) for shape in out_shapes] + [jax.ShapeDtypeStruct((8, width), F32)],
        compiler_params=pltpu.CompilerParams(vmem_limit_bytes=VMEM_LIMIT),
        cost_estimate=pl.CostEstimate(
            flops=16 * rows * width * width, bytes_accessed=14 * rows * width + 6 * width * width, transcendentals=0
        ),
        name="input_grads",
    )(slot, inputs, d_residual, vectors, packed, *flat)


def time_features(t_index, model_width):
    half_width = model_width // 2
    indices = jnp.arange(half_width).astype(F32)
    frequency = jnp.exp(indices * (-math.log(10000.0) / (half_width - 1)))
    angles = t_index.astype(F32)[:, None] * frequency[None, :]
    return jnp.concatenate([jnp.sin(angles), jnp.cos(angles)], axis=1)


def rotary_tables(places):
    inverse = jnp.exp(jnp.arange(HALF).astype(F32) * (-2.0 * math.log(10000.0) / HDIM))
    angles = inverse[:, None] * places.astype(F32)[None, :]
    return jnp.cos(angles), jnp.sin(angles)


def after(values, *others):
    return lax.optimization_barrier((values,) + others)[0] if others else values


def make_body(mesh):
    n_dp, n_fsdp = mesh.shape["dp"], mesh.shape["fsdp"]
    n_pairs = n_fsdp // 2

    def shift(values, axis, size, by):
        return lax.ppermute(values, axis, [(i, (i + by) % size) for i in range(size)])

    def pick(values, index, axis=0):
        return lax.dynamic_index_in_dim(values, index, axis, keepdims=False)

    def body(
        frames,
        lengths,
        t_index,
        w_ada,
        b_ada,
        w_query,
        b_query,
        w_key,
        b_key,
        w_value,
        b_value,
        w_out,
        b_out,
        w_up,
        b_up,
        w_down,
        b_down,
        grad_out,
    ):
        slots, local, width = frames.shape
        group = n_fsdp // slots
        hidden_width = w_up.shape[1]
        shard = w_query.shape[0]
        ada_width = w_ada.shape[1]
        dp, fsdp = lax.axis_index("dp"), lax.axis_index("fsdp")
        me = dp * n_fsdp + fsdp
        slot, place = fsdp // group, fsdp % group
        other = 1 - slot
        core, pair = fsdp % 2, fsdp // 2
        side, deep, far = dp % 2, dp // 2, n_dp // 2
        length = pick(lengths, slot)

        def picked(values):
            return pick(values, slot), pick(values, other)

        split = local % 128 == 0

        def swap_in(own, away):
            parts = own, shift(away, "fsdp", n_fsdp, group)
            return parts if split else (jnp.concatenate(parts),) * 2

        def swap_out(*pieces):
            return [shift(piece, "fsdp", n_fsdp, group) for piece in pieces]

        def placed_away(whole, arrived):
            first = 0
            for piece in arrived:
                whole = lax.dynamic_update_slice(whole, piece[None], (other, first, 0))
                first += piece.shape[0]
            return whole

        def placed_own(own):
            return lax.dynamic_update_index_in_dim(jnp.zeros((slots, local, width), own.dtype), own, slot, 0)

        def places_of(member):
            at = slot * group + member
            blocks = [((at - by * group) + n_fsdp) % n_fsdp for by in range(slots)]
            return jnp.concatenate([b * local + jnp.arange(local, dtype=jnp.int32) for b in blocks])

        ring = lambda by: [(i, (i // group) * group + (i % group + by) % group) for i in range(n_fsdp)]

        def swap(values, axis, size):
            return lax.ppermute(values, axis, [(i, i ^ 1) for i in range(size)])

        def sum_core(keep, send, *others):
            arrived = after(swap(send, "fsdp", n_fsdp), *others)
            total = keep.astype(F32) + arrived.astype(F32)
            return total.astype(BF16).reshape(n_dp, n_pairs, shard, keep.shape[1])

        def sum_pairs(values, *others):
            axis = values.ndim - 3
            total = pick(values, pair, axis).astype(F32)
            for by in range(1, n_pairs):
                arrived = after(shift(pick(values, (pair + by) % n_pairs, axis), "fsdp", n_fsdp, 2 * by), *others)
                total = total + arrived.astype(F32)
            return total

        def sum_side(values, *others):
            values = values.reshape((far, 2) + values.shape[1:])
            arrived = after(swap(pick(values, 1 - side, 1), "dp", n_dp), *others)
            return pick(values, side, 1).astype(F32) + arrived.astype(F32)

        def sum_far(values, *others):
            total = pick(values, deep).astype(F32)
            for by in range(1, far):
                arrived = after(shift(pick(values, (deep + by) % far), "dp", n_dp, 2 * by), *others)
                total = total + arrived.astype(F32)
            return total

        def gather_dp(values):
            values = jnp.stack([values] + [shift(values, "dp", n_dp, 2 * by) for by in range(1, far)])
            return jnp.stack([values, swap(values, "dp", n_dp)])

        packed = lax.all_gather(jnp.concatenate([w_key, w_value, w_query], axis=1), AXES, axis=0, tiled=True)
        ups = hidden_width // width
        w_up_turned = w_up.reshape(shard, n_dp * n_fsdp, ups, shard).swapaxes(1, 2).reshape(w_up.shape)
        downs = [w_down[i * shard : (i + 1) * shard] for i in range(ups)]
        packed_two = lax.all_gather(jnp.concatenate([w_out, w_up_turned, *downs], axis=1), AXES, axis=0, tiled=True)

        inputs = swap_in(*picked(frames))
        rows = slots * local
        own_grad, away_grad = picked(grad_out)

        t_all = gather_dp(t_index).reshape(-1)
        active = jax.nn.silu(time_features(t_all, width)).astype(BF16)
        active_mine = lax.dynamic_slice_in_dim(active, me * shard, shard, axis=1)
        partial = [dot(active_mine, w_ada, 1, 0)]
        for bias in (b_query, b_key, b_value, b_out, b_down, *jnp.split(b_up, ups)):
            size = bias.shape[0]
            zeros = jnp.zeros((1, size * n_dp * n_fsdp), F32)
            placed = lax.dynamic_update_slice_in_dim(zeros, bias.astype(F32)[None], me * size, axis=1)
            partial.append(jnp.broadcast_to(placed, (n_dp * slots, placed.shape[1])))
        placed = lax.dynamic_update_slice_in_dim(
            jnp.zeros((1, ada_width), F32), b_ada.astype(F32)[None], me * b_ada.shape[0], axis=1
        )
        partial[0] = partial[0] + placed
        partial = jnp.concatenate(partial, axis=1).reshape(2, far, slots, -1)
        partial = partial[0] + swap(partial[1], "dp", n_dp)
        summed = partial[0]
        for by in range(1, far):
            summed = summed + shift(partial[by], "dp", n_dp, -2 * by)
        one = pick(summed, slot) + shift(pick(summed, other), "fsdp", n_fsdp, group)
        vectors = one
        for by in range(1, group):
            vectors = vectors + lax.ppermute(one, "fsdp", ring(by))
        vectors = vectors.reshape(-1, width)
        vectors = jnp.pad(vectors, ((0, -vectors.shape[0] % 8), (0, 0)))

        key_places = jnp.concatenate([places_of((place - by + group) % group) for by in range(group)])
        cosine, sine = rotary_tables(key_places)
        key_bias = jnp.where(key_places < length, 0.0, -1e30)
        bias_columns = jnp.pad(key_bias.astype(BF16)[:, None], ((0, 0), (0, HDIM - 1)))
        keep = (key_places[:rows] < length).astype(F32)[:, None]

        wide = 2
        vectors, cosine, sine, key_bias, bias_columns, keep, own_grad, away_grad = lax.optimization_barrier(
            (vectors, cosine, sine, key_bias, bias_columns, keep, own_grad, away_grad)
        )
        h_one, q_rot, keys, values = project(inputs, vectors, packed, cosine[:, :rows], sine[:, :rows], wide)
        cotangent = swap_in(own_grad, after(away_grad, keys[0]))
        heads = width // HDIM
        tall = heads // wide
        with_ring = lambda own: [own] + [lax.ppermute(own, "fsdp", ring(by)) for by in range(1, group)]
        k_parts, v_parts = [with_ring(own) for own in keys], [with_ring(own) for own in values]
        heads_out, lses = [], []
        for at in range(wide):
            out, lse = attend(q_rot, k_parts[at], v_parts[at], bias_columns, at * tall)
            heads_out.append(out)
            lses.append(lse)
        at_slot = slot.reshape(1).astype(jnp.int32)
        mixed, away_mixed, d_residual, d_heads, g_rows, sums_two = feed_forward(
            at_slot, inputs, heads_out, cotangent, keep, packed_two, vectors, slots
        )
        if not split:
            mixed, away_mixed = placed_own(mixed[:local]), mixed[local:]
        mixed_arrived = swap_out(away_mixed)

        sum_rows = lax.psum_scatter(g_rows, AXES, scatter_dimension=0, tiled=True)

        grads, d_biases = ([], [], []), []
        at_core = core.reshape(1).astype(jnp.int32)

        def sum_parts(dq, dk_parts, dv_parts, *others):
            dk_parts = [after(dk_parts[0], *others)] + dk_parts[1:]
            dk, dv, keep, send, bias_grad = weight_grads(at_core, shard, h_one, dq, dk_parts, dv_parts)
            for kind, grad in zip(grads, (dq, dk, dv)):
                kind.append([grad])
            d_biases.append(bias_grad[:, :3])
            return keep, send

        counts = (tall, tall // 2, tall // 2)
        first, ready, arrived = 0, d_heads, []
        for step, each in enumerate(counts):
            part, within = first // tall, first % tall
            dq, dk_parts, dv_parts = attend_back(
                q_rot,
                k_parts[part],
                v_parts[part],
                ready,
                heads_out[part],
                lses[part],
                key_bias[None],
                cosine,
                sine,
                first,
                within,
                each,
            )
            first += each
            dk_parts = [dk_parts[0]] + [lax.ppermute(dk_parts[by], "fsdp", ring(-by)) for by in range(1, group)]
            dv_parts = [dv_parts[0]] + [lax.ppermute(dv_parts[by], "fsdp", ring(-by)) for by in range(1, group)]
            arrived.append((dq, dk_parts, dv_parts))
            if step == 1:
                early = sum_parts(*arrived[0], dq)
                ready = after(d_heads, dq, early[0])
        early_sum = sum_core(*early, dq)
        if split:
            in_parts = [
                grads[0] + [[piece[0]] for piece in arrived[1:]],
                grads[1] + [piece[1] for piece in arrived[1:]],
                grads[2] + [piece[2] for piece in arrived[1:]],
            ]
            rest = after(d_residual, early_sum)
            *away_frames, sums_away = input_grads(at_slot, 0, inputs[1], 1, rest, vectors, packed, in_parts, True)
            frames_arrived = swap_out(*away_frames)
            early_sum = sum_pairs(early_sum, sums_away).astype(BF16)
            middle = sum_parts(*arrived[1], sums_away)
            last = sum_parts(*arrived[2], middle[0], sum_rows, *mixed_arrived)
            core_sums = jnp.concatenate([sum_core(*sums, last[0]) for sums in (middle, last)], axis=-1)
            rest, core_sums, _ = lax.optimization_barrier((d_residual, core_sums, frames_arrived[0]))
            own_frames, sums_own = input_grads(at_slot, slots, inputs[0], 0, rest, vectors, packed, grads)
            sums_one = sums_own + sums_away
        else:
            early_sum = sum_pairs(early_sum).astype(BF16)
            middle, last = sum_parts(*arrived[1]), sum_parts(*arrived[2])
            core_sums = jnp.concatenate([sum_core(*sums) for sums in (middle, last)], axis=-1)
            both, sums_one = input_grads(at_slot, 0, inputs[0], 0, d_residual, vectors, packed, grads)
            own_frames, frames_arrived = placed_own(both[:local]), swap_out(both[local:])
        side_sums = sum_side(core_sums).astype(BF16)
        early_sum = sum_side(early_sum, side_sums).astype(BF16)

        vector = jnp.concatenate(
            [sums_one[:2], sums_two[: 6 + ups], jnp.concatenate(d_biases).T]
        )
        for_slot = 6
        vector = after(vector, *frames_arrived)
        total = vector
        for by in range(1, group):
            total = total + lax.ppermute(vector, "fsdp", ring(by))
        total, side_sums = lax.optimization_barrier((total, side_sums))
        all_sums = sum_far(jnp.concatenate([early_sum[:, None], side_sums], axis=1))
        sums = [all_sums[0], sum_pairs(all_sums[1:].astype(BF16))]
        sum_rows, mixed = after(sum_rows, total).astype(F32), after(mixed, total)
        g_out = sum_rows[:, :width]
        g_up = sum_rows[:, width : width + hidden_width].reshape(shard, ups, n_dp * n_fsdp, shard)
        g_up = g_up.swapaxes(1, 2).reshape(w_up.shape)
        g_down = jnp.concatenate([sum_rows[:, (1 + ups + i) * width : (2 + ups + i) * width] for i in range(ups)])
        mixed = placed_away(mixed, mixed_arrived)
        packs = gather_dp(total).reshape(n_dp, -1, width)
        pack = jnp.concatenate([packs[:, :for_slot].reshape(-1, width), jnp.sum(packs[:, for_slot:], axis=0)])
        pack, g_out, g_up, g_down, mixed = lax.optimization_barrier((pack, g_out, g_up, g_down, mixed))
        grad_frames = placed_away(own_frames, frames_arrived)
        across = shift(pack, "fsdp", n_fsdp, group)
        count = n_dp * for_slot
        d_mod = jnp.stack([jnp.where(slot == s, pack[:count], across[:count]).reshape(n_dp, -1) for s in range(slots)], axis=1)
        d_mod = d_mod.reshape(n_dp * slots, for_slot * width)
        d_vectors = pack[count:] + across[count:]

        g_w_ada = lax.dot_general(
            active_mine.astype(F32),
            d_mod,
            (((0,), (0,)), ((), ())),
            precision=lax.Precision.HIGHEST,
            preferred_element_type=F32,
        )

        def mine(vector):
            vector = vector.reshape(-1)
            size = vector.shape[0] // (n_dp * n_fsdp)
            return lax.dynamic_slice_in_dim(vector, me * size, size)

        columns = jnp.concatenate(sums, axis=1).reshape(shard, -1, 3, pick_block(tall // 2 * HDIM, 128))
        g_qkv = [columns[:, :, i].reshape(shard, width) for i in range(3)]
        return (
            mixed,
            grad_frames,
            g_w_ada,
            mine(jnp.sum(d_mod, axis=0)),
            g_qkv[0],
            mine(d_vectors[2 + ups]),
            g_qkv[1],
            mine(d_vectors[3 + ups]),
            g_qkv[2],
            mine(d_vectors[4 + ups]),
            g_out,
            mine(d_vectors[0]),
            g_up,
            jnp.concatenate([mine(d_vectors[2 + i]) for i in range(ups)]),
            g_down,
            mine(d_vectors[1]),
        )

    return body


def solution(mesh):
    rows, vector, matrix = P("dp", "fsdp", None), P(AXES), P(AXES, None)
    return jax.shard_map(
        make_body(mesh),
        mesh=mesh,
        in_specs=(rows, P("dp"), P("dp")) + (matrix, vector) * 7 + (rows,),
        out_specs=(rows, rows) + (matrix, vector) * 7,
        check_vma=False,
    )
```
